256 devices in a mesh: ctx: 32 (over y_lo, z, core), head: 8 (over x, y_hi).
Axes of the slice: x: 4, y: 4 (y_hi: 2, y_lo: 2; y = y_hi * 2 + y_lo), z: 8, core: 2. Of those that a mesh axis runs over, the one named last changes fastest.
Arguments:
- main_q_nope: bfloat16 [512, 16384], P(None, 'head'), may hold values from -130 to 130
- main_q_rope: bfloat16 [512, 8192], P(None, 'head'), may hold values from -6 to 6
- main_k_nope: bfloat16 [32768, 16384], P('ctx', 'head'), may hold values from -9 to 9
- main_k_rope: bfloat16 [32768, 64], P('ctx'), may hold values from -6 to 6
- index_q: bfloat16 [512, 8192], P('head'), may hold values from -90 to 90
- index_k: bfloat16 [32768, 128], P('ctx'), may hold values from -8 to 8
- index_w: float32 [512, 64], P('head'), may hold values from -3 to 3
- query_pos: int32 [512], replicated, may hold values from 0 to 32767
- key_blocks: int32 [32], P('ctx'), may hold values from 0 to 31, each once
Outputs:
- grad_index_q: float32 [512, 8192], P('head', 'ctx')
- grad_index_k: float32 [32768, 128], P(('ctx', 'head'))
- grad_index_w: float32 [512, 64], P('head')
The draws below stay inside these ranges and needn't reach their ends.
All inputs are finite; a program needn't handle non-finite values.
Results may differ from the reference program's by a relative error of at most 0.015.
Values sent between devices are 32-bit elements; how exact they have to be, the bound alone decides.
No kernel may reach another device: no remote copies, remote signals or barrier semaphores. Data moves between devices by JAX's collectives and lax.ppermute only.
A program may use at most 128 MiB of HBM per device.

```python
import math
import jax
import jax.numpy as jnp
from jax import lax

HEADS = 128
NOPE = 128
ROPE = 64
IDX_HEADS = 64
IDX_DIM = 128
QUERIES = 512
KEYS_DEV = 1024
CONTEXT = 32768
N_CTX = 32


def shared_direction(key, salt, width):
    return jnp.clip(jax.random.normal(jax.random.fold_in(key, salt), (width,), jnp.float32), -2.0, 2.0)


def drawn_normal(key, shape):
    return jnp.clip(jax.random.normal(key, shape, jnp.float32), -6.0, 6.0)


def strong_rows(key, count, lowest, highest):
    ranks = jax.random.permutation(key, count).astype(jnp.float32)
    chosen = max(2, count // 8)
    spread = jnp.minimum(ranks / (chosen - 1), 1.0)
    strength = lowest * jnp.exp(spread * math.log(highest / lowest))
    return jnp.where(ranks < chosen, strength, 0.0)[:, None]


def key_levels(key, rows, block_rows, spread, offset):
    single = jnp.clip(jax.random.normal(jax.random.fold_in(key, 7), (rows, 1), jnp.float32), -4.0, 4.0) * spread
    blocks = jax.random.uniform(jax.random.fold_in(key, 8), (rows // block_rows, 1), jnp.float32, -offset, offset)
    return single + jnp.repeat(blocks, block_rows, axis=0)


def draw_main_q_nope(key, part):
    direction = shared_direction(key, 101, HEADS * NOPE)
    common = shared_direction(key, 303, HEADS * NOPE)
    key = jax.random.fold_in(key, 1)
    values = drawn_normal(key, (QUERIES, HEADS * NOPE))
    values = values + common[None, :]
    values = values + strong_rows(jax.random.fold_in(key, 9), QUERIES, 8.0, 60.0) * direction[None, :]
    return values.astype(jnp.bfloat16)


def draw_main_k_nope(key, part):
    direction = shared_direction(key, 101, HEADS * NOPE)
    common = shared_direction(key, 303, HEADS * NOPE)
    key = jax.random.fold_in(key, 2)
    values = drawn_normal(key, (CONTEXT, HEADS * NOPE))
    levels = key_levels(key, CONTEXT, KEYS_DEV, 0.14, 0.13)
    values = 0.8 * values + direction[None, :]
    values = values + levels * common[None, :]
    return values.astype(jnp.bfloat16)


def draw_index_q(key, part):
    key = jax.random.fold_in(key, 3)
    values = drawn_normal(key, (QUERIES, IDX_HEADS * IDX_DIM))
    return values.astype(jnp.bfloat16)


def draw_index_k(key, part):
    direction = shared_direction(key, 202, IDX_DIM)
    key = jax.random.fold_in(key, 4)
    values = drawn_normal(key, (CONTEXT, IDX_DIM))
    values = 0.8 * values + direction[None, :]
    return values.astype(jnp.bfloat16)


def place_ends(entries, own_key, low, top_value):
    dims = entries.shape
    place = [jax.random.randint(jax.random.fold_in(own_key, axis), (), 0, dims[axis]) for axis in range(len(dims))]
    entries = entries.at[tuple(place)].set(low)
    longest = dims.index(max(dims))
    place[longest] = (place[longest] + 1) % dims[longest]
    return entries.at[tuple(place)].set(top_value)


def block_scale(own_key, shape, pieces, least, largest):
    def one(position, blocks):
        steps = jax.random.uniform(jax.random.fold_in(jax.random.fold_in(own_key, 6), position), (blocks,), jnp.float32, least / len(pieces), largest / len(pieces))
        return jnp.repeat(jnp.exp(steps), shape[position] // blocks).reshape((-1,) + (1,) * (len(shape) - position - 1))

    gain = one(*pieces[0])
    for cut in pieces[1:]:
        gain = gain * one(*cut)
    return gain


def centred(rng, extent, scale, bound, shards=(), kind=jnp.bfloat16):
    values = scale * jax.random.normal(rng, extent, jnp.float32)
    if shards:
        values = values * block_scale(rng, extent, shards, -0.22, 0.18)
    return jnp.clip(values, -bound, bound).astype(kind)


def setup_inputs(seed: int = 0) -> dict:
    splits = jax.random.split(jax.random.key(seed), 10)
    main_q_nope = draw_main_q_nope(jax.random.fold_in(splits[9], 71), 0)
    main_q_rope = centred(splits[1], (QUERIES, HEADS * ROPE), 1.0, 6.0, ((1, 8),))
    main_k_nope = draw_main_k_nope(jax.random.fold_in(splits[9], 71), 0)
    main_k_rope = centred(splits[3], (CONTEXT, ROPE), 1.0, 6.0, ((0, 32),))
    index_q = draw_index_q(jax.random.fold_in(splits[9], 71), 0)
    index_k = draw_index_k(jax.random.fold_in(splits[9], 71), 0)
    index_w = centred(splits[6], (QUERIES, IDX_HEADS), 0.6, 3.0, ((0, 8),), jnp.float32)
    query_pos = place_ends(jax.random.randint(splits[7], (QUERIES,), 0, CONTEXT), jax.random.fold_in(splits[7], 1), 0, CONTEXT - 1).astype(jnp.int32)
    key_blocks = jax.random.permutation(splits[8], N_CTX).astype(jnp.int32)
    return dict(main_q_nope=main_q_nope, main_q_rope=main_q_rope, main_k_nope=main_k_nope, main_k_rope=main_k_rope, index_q=index_q, index_k=index_k, index_w=index_w, query_pos=query_pos, key_blocks=key_blocks)


negative_fill = -1e+30
row_block = 16

def reference(main_q_nope, main_q_rope, main_k_nope, main_k_rope, index_q, index_k, index_w, query_pos, key_blocks):
    key_pos = (key_blocks[:, None] * KEYS_DEV + jnp.arange(KEYS_DEV, dtype=jnp.int32)[None, :]).reshape(-1)
    visible = key_pos[None, :] <= query_pos[:, None]
    score_scale = 1.0 / math.sqrt(NOPE + ROPE)
    query_nope = main_q_nope.reshape(QUERIES, HEADS, NOPE)
    query_rope = main_q_rope.reshape(QUERIES, HEADS, ROPE)
    key_nope = main_k_nope.reshape(CONTEXT, HEADS, NOPE)

    def add_head(head_index, running):
        q_head = lax.dynamic_index_in_dim(query_nope, head_index, 1, keepdims=False)
        r_head = lax.dynamic_index_in_dim(query_rope, head_index, 1, keepdims=False)
        k_head = lax.dynamic_index_in_dim(key_nope, head_index, 1, keepdims=False)
        scores = jnp.dot(q_head, k_head.T, preferred_element_type=jnp.float32)
        scores = scores + jnp.dot(r_head, main_k_rope.T, preferred_element_type=jnp.float32)
        scores = jnp.where(visible, scores * score_scale, negative_fill)
        row_top = lax.optimization_barrier(jnp.max(scores, axis=1, keepdims=True))
        row_total = lax.optimization_barrier(jnp.sum(jnp.where(visible, jnp.exp(scores - row_top), 0.0), axis=1, keepdims=True))
        main_lse = row_top + jnp.log(row_total)
        return running + jnp.where(visible, jnp.exp(scores - main_lse), 0.0)
    target = lax.fori_loop(0, HEADS, add_head, jnp.zeros((QUERIES, CONTEXT), jnp.float32)) / HEADS
    inv_root = 1.0 / math.sqrt(IDX_DIM)
    block_count = QUERIES // row_block
    keys_wide = index_k.astype(jnp.float32)

    def block_step(key_total, inputs):
        q_rows, w_rows, t_rows, v_rows = inputs
        q_heads = q_rows.reshape(row_block, IDX_HEADS, IDX_DIM).astype(jnp.float32)
        inner = jnp.einsum('rjd,kd->rjk', q_heads, keys_wide) * inv_root
        active = jnp.maximum(inner, 0.0)
        logits = lax.optimization_barrier(jnp.sum(w_rows[:, :, None] * active, axis=1))
        logits = jnp.where(v_rows, logits, negative_fill)
        row_top = lax.optimization_barrier(jnp.max(logits, axis=1, keepdims=True))
        row_total = lax.optimization_barrier(jnp.sum(jnp.where(v_rows, jnp.exp(logits - row_top), 0.0), axis=1, keepdims=True))
        index_lse = row_top + jnp.log(row_total)
        logit_grad = jnp.where(v_rows, jnp.exp(logits - index_lse) - t_rows, 0.0)
        weighted = jnp.where(inner > 0, logit_grad[:, None, :] * w_rows[:, :, None], 0.0).astype(jnp.bfloat16)
        weighted_wide = weighted.astype(jnp.float32)
        query_part = jnp.einsum('rjk,kd->rjd', weighted_wide, keys_wide).reshape(row_block, IDX_HEADS * IDX_DIM) * inv_root
        key_part = jnp.einsum('rjk,rjd->kd', weighted_wide, q_heads) * inv_root
        weight_part = lax.optimization_barrier(jnp.sum(logit_grad[:, None, :] * active, axis=2))
        return (key_total + key_part, (query_part, weight_part))
    inputs = (index_q.reshape(block_count, row_block, IDX_HEADS * IDX_DIM), index_w.reshape(block_count, row_block, IDX_HEADS), target.reshape(block_count, row_block, CONTEXT), visible.reshape(block_count, row_block, CONTEXT))
    grad_index_k, outputs = lax.scan(block_step, jnp.zeros((CONTEXT, IDX_DIM), jnp.float32), inputs)
    grad_index_q = outputs[0].reshape(QUERIES, IDX_HEADS * IDX_DIM)
    grad_index_w = outputs[1].reshape(QUERIES, IDX_HEADS)
    return (grad_index_q, grad_index_k, grad_index_w)
```

```python
import math

import jax
import jax.numpy as jnp
from jax import lax
from jax.experimental import pallas as pl
from jax.experimental.pallas import tpu as pltpu
from jax.sharding import PartitionSpec as P

HEADS = 128
NOPE = 128
ROPE = 64
IDX_HEADS = 64
IDX_DIM = 128
N_CTX = 32
N_HEAD = 8
N_Z = 8
LOG2E = math.log2(math.e)
SCORE_SCALE = LOG2E / math.sqrt(NOPE + ROPE)
INV_ROOT = 1.0 / math.sqrt(IDX_DIM)
NEG = -1e30
F32 = jnp.float32
BF16 = jnp.bfloat16
NT = (((1,), (1,)), ((), ()))
NN = (((1,), (0,)), ((), ()))
GROUP = 8


def dot(a, b, dims):
    return lax.dot_general(a, b, dims, preferred_element_type=F32)


def column(row, lanes=128):
    return jnp.broadcast_to(row, (lanes, row.shape[1])).T


def ctx_place():
    ctx = lax.axis_index("ctx")
    return ctx // (2 * N_Z), ctx // 2 % N_Z, ctx % 2


def fill_rope(krt_ref, krp):
    kr = krt_ref[...].T
    zero = jnp.zeros_like(kr)
    krp[0] = jnp.concatenate([kr, zero], axis=1)
    krp[1] = jnp.concatenate([zero, kr], axis=1)


def fill_weights(w_ref, wb):
    for j in range(IDX_HEADS):
        wb[j] = jnp.broadcast_to(w_ref[:, j : j + 1], wb.shape[1:])


def lanes_of(block, width):
    return jnp.concatenate([block] * (width // 128), axis=-1)


def stacked(block):
    count = block.shape[1] // 128
    return jnp.concatenate([block[:, i * 128 : (i + 1) * 128] for i in range(count)], axis=0)


def index_kernel(
    base_ref, qpos_ref, iq_first, iq_odd, iq_next, ik_ref, w_ref, logits_ref, row_ref, r_ref,
    wb, qcol, even, odd,
):
    step = pl.program_id(0)
    rows, keys = logits_ref.shape

    @pl.when(step == 0)
    def _():
        even[...] = dot(stacked(iq_first[...]), ik_ref[...], NT)
        fill_weights(w_ref, wb)
        logits_ref[...] = jnp.zeros_like(logits_ref)
        qcol[...] = column(qpos_ref[...])

    for n, (source, done, made) in enumerate(((iq_odd, even, odd), (iq_next, odd, even))):
        q = stacked(source[...])
        for half in range(2):
            wide = slice(half * 512, (half + 1) * 512)
            made[:, wide] = dot(q, ik_ref[wide, :], NT)
            for kc in range(4 * half, 4 * half + 4):
                cols = slice(kc * 128, (kc + 1) * 128)
                total = logits_ref[:, cols]
                for i in range(GROUP):
                    mine = slice(i * rows, (i + 1) * rows)
                    inner = done[mine, cols]
                    r_ref[n, mine, cols] = inner.astype(BF16)
                    total = total + jnp.maximum(inner, 0.0) * wb[(2 * step + n) * GROUP + i]
                logits_ref[:, cols] = total

    @pl.when(step == pl.num_programs(0) - 1)
    def _():
        key = lax.broadcasted_iota(jnp.int32, (rows, keys), 1) + base_ref[0] * keys
        start = pl.multiple_of(lax.axis_index("head") * rows, rows)
        limit = lanes_of(qcol[pl.ds(start, rows), :], keys)
        logits = jnp.where(key <= limit, logits_ref[...] * (INV_ROOT * LOG2E), NEG)
        logits_ref[...] = logits
        top = jnp.max(logits, axis=1, keepdims=True)
        total = jnp.sum(jnp.exp2(logits - top), axis=1, keepdims=True)
        lse = jnp.broadcast_to(top + jnp.log2(total), (rows, 128)).T
        row_ref[...] = jnp.concatenate([lse[:16, :rows], jnp.zeros((16, 128 - rows), F32)], axis=1)


def pair_operands(refs, krp, p):
    qn_ref, qr_ref, kn_ref = refs
    part = slice(p * 128, (p + 1) * 128)
    q = jnp.concatenate([qn_ref[:, part], qr_ref[...]], axis=1)
    return q, jnp.concatenate([kn_ref[:, part], krp[p]], axis=1)


def online_lse(s_ref, bias, cols, chunk=64):
    keys = bias.shape[0]
    top = jnp.full((8, 256), 2.0 * NEG, F32)
    total = jnp.zeros((8, 256), F32)
    for kc in range(keys // chunk):
        rows = slice(kc * chunk, (kc + 1) * chunk)
        s = (s_ref[rows, cols] + bias[rows, cols]).reshape(chunk // 8, 8, 256)
        new = jnp.maximum(top, jnp.max(s, axis=0))
        e = jnp.exp2((s - new[None]) * SCORE_SCALE)
        total = total * jnp.exp2((top - new) * SCORE_SCALE) + jnp.sum(e, axis=0)
        top = new
    best = jnp.max(top, axis=0, keepdims=True)
    total = jnp.sum(total * jnp.exp2((top - best) * SCORE_SCALE), axis=0, keepdims=True)
    return best * SCORE_SCALE + jnp.log2(total)


def stats_kernel(base_ref, qpos_ref, row_ref, krt_ref, *refs):
    first, odd_in, next_in = refs[:3], refs[3:6], refs[6:9]
    out_ref, bias, krp, even, odd = refs[9:]
    step = pl.program_id(0)
    keys, queries = bias.shape

    @pl.when(step == 0)
    def _():
        fill_rope(krt_ref, krp)
        for p in range(2):
            q, k = pair_operands(first, krp, p)
            even[p] = dot(k, q, NT)
        key = lax.broadcasted_iota(jnp.int32, bias.shape, 0) + base_ref[0] * keys
        bias[...] = jnp.where(key <= qpos_ref[...], 0.0, NEG)
        out_ref[:, queries:] = row_ref[...]

    for n, (source, done, made) in enumerate(((odd_in, even, odd), (next_in, odd, even))):
        for p in range(2):
            q, k = pair_operands(source, krp, p)
            made[p] = dot(k, q, NT)
            for qc in range(queries // 256):
                cols = slice(qc * 256, (qc + 1) * 256)
                out_ref[pl.ds(4 * step + 2 * n + p, 1), cols] = online_lse(done.at[p], bias, cols)


def probs_kernel(lse_ref, krt_ref, *refs):
    first, odd_in, next_in = refs[:3], refs[3:6], refs[6:9]
    out_ref, krp, even, odd = refs[9:]
    step = pl.program_id(0)
    queries, keys = out_ref.shape

    @pl.when(step == 0)
    def _():
        fill_rope(krt_ref, krp)
        for p in range(2):
            even[p] = dot(*pair_operands(first, krp, p), NT)
        out_ref[...] = jnp.zeros_like(out_ref)

    for n, (source, done, made) in enumerate(((odd_in, even, odd), (next_in, odd, even))):
        at = 4 * step + 2 * n
        lse = [column(lse_ref[pl.ds(at + p, 1), :queries]) for p in range(2)]
        for half in range(2):
            made[half] = dot(*pair_operands(source, krp, half), NT)
            for r in range(8 * half, 8 * half + 8):
                rows = slice(r * 32, (r + 1) * 32)
                total = out_ref[rows, :]
                for p in range(2):
                    s = done[p, rows, :] * SCORE_SCALE - lanes_of(lse[p][rows], keys)
                    total = total + jnp.exp2(s)
                out_ref[rows, :] = total


def lg_kernel(lse_ref, logits_ref, target_ref, lg_ref):
    rows, width = lg_ref.shape
    lse = column(lse_ref[:1, :])[:rows]
    for c in range(width // 128):
        cols = slice(c * 128, (c + 1) * 128)
        target = target_ref[0, :, cols]
        for h in range(1, N_HEAD):
            target = target + target_ref[h, :, cols]
        logits = logits_ref[:, cols]
        lg = jnp.exp2(logits - lse) - target * (1.0 / HEADS)
        lg_ref[:, cols] = jnp.where(logits > 0.5 * NEG, lg, 0.0)


def masked_lg(r, lg):
    lg = jnp.concatenate([lg] * (r.shape[0] // lg.shape[0]), axis=0)
    return jnp.where(r > 0, lg, jnp.zeros_like(lg))


def gk_kernel(lg_ref, iq_ref, w_ref, r_ref, gk_ref, gw_out, wb, lgb_ref, gkt_ref, gw_ref):
    step = pl.program_id(0)
    rows, keys = lg_ref.shape

    @pl.when(step == 0)
    def _():
        fill_weights(w_ref, wb)
        lgb_ref[...] = lg_ref[...].astype(BF16)
        gkt_ref[...] = jnp.zeros_like(gkt_ref)
        gw_ref[...] = jnp.zeros_like(gw_ref)

    q = stacked(iq_ref[...])
    w = jnp.concatenate([wb[step * GROUP + i] for i in range(GROUP)], axis=0)
    wqt = (q.astype(F32) * w).astype(BF16).T
    totals = [jnp.zeros((rows, 128), F32) for _ in range(GROUP)]
    for kc in range(keys // 256):
        cols = slice(kc * 256, (kc + 1) * 256)
        r = r_ref[0, :, cols]
        gkt_ref[:, cols] += dot(wqt, masked_lg(r, lgb_ref[:, cols]), NN)
        lg = lg_ref[:, cols]
        for i in range(GROUP):
            active = jnp.maximum(r[i * rows : (i + 1) * rows].astype(F32), 0.0) * lg
            totals[i] = totals[i] + active[:, :128] + active[:, 128:]
    lane = lax.broadcasted_iota(jnp.int32, (rows, IDX_HEADS), 1)
    new = gw_ref[...]
    for i in range(GROUP):
        value = jnp.sum(totals[i], axis=1, keepdims=True) * INV_ROOT
        new = jnp.where(lane == step * GROUP + i, value, new)
    gw_ref[...] = new

    @pl.when(step == pl.num_programs(0) - 1)
    def _():
        for c in range(keys // 128):
            gk_ref[c] = gkt_ref[:, c * 128 : (c + 1) * 128].T * INV_ROOT
        gw_out[...] = jnp.concatenate([gw_ref[i * 16 : (i + 1) * 16, :] for i in range(4)], axis=1)


def group_dests(part):
    y_lo, _, core = ctx_place()
    return [(y_lo * N_Z + part * 4 + i) * 2 + core for i in range(4)]


def inner_kernel(iq_ref, *refs):
    iks, (r_ref, ikb_ref) = refs[:4], refs[4:]
    part, source = pl.program_id(0), pl.program_id(1)

    @pl.when((part == 0) & (source == 0))
    def _():
        for i in range(4):
            ikb_ref[i] = iks[i][...].astype(BF16)

    dests = group_dests(part)
    blocks = [iq_ref[:, pl.ds(pl.multiple_of(c * 256, 256), 256)] for c in dests]
    q = jnp.concatenate([stacked(block) for block in blocks], axis=0)
    r_ref[0, 0] = dot(q, ikb_ref[source], NT).astype(BF16)


def gq_kernel(lg0, lg1, lg2, lg3, r_ref, ikb_ref, w_ref, gwy_ref, gwc_ref, gq_ref, wb, lgb_ref, g_ref):
    part, source = pl.program_id(0), pl.program_id(1)
    rows = lg0.shape[0]

    @pl.when((part == 0) & (source == 0))
    def _():
        fill_weights(w_ref, wb)
        for i, lg in enumerate((lg0, lg1, lg2, lg3)):
            lgb_ref[i] = lg[...].astype(BF16)

    grown = dot(masked_lg(r_ref[0, 0], lgb_ref[source]), ikb_ref[source], NN)

    @pl.when(source == 0)
    def _():
        g_ref[...] = grown

    @pl.when(source > 0)
    def _():
        g_ref[...] += grown

    @pl.when(source == 3)
    def _():
        gw = gwy_ref[...] + gwc_ref[...]
        dests = group_dests(part)
        for i in range(4):
            pair = []
            for n in range(2):
                at = (2 * i + n) * rows
                pair.append(g_ref[at : at + rows, :] * wb[dests[i] * 2 + n] * INV_ROOT)
            gq_ref[i, :rows, :] = jnp.concatenate(pair, axis=1)
            gq_ref[i, rows:, :] = gw


def finish_kernel(parts_ref, gks_ref, gq_ref, gk_ref, gw_ref):
    total, keys = parts_ref[0], gks_ref[0]
    for i in range(1, 8):
        total = total + parts_ref[i]
        keys = keys + gks_ref[i]
    gq_ref[...] = total[:64]
    gk_ref[...] = keys
    gw_ref[...] = jnp.concatenate([total[64:, i * 64 : (i + 1) * 64] for i in range(4)], axis=0)


def smem():
    return pl.BlockSpec(memory_space=pltpu.SMEM)


def whole(shape):
    return pl.BlockSpec(shape, lambda *_: (0,) * len(shape))


def wholes(arrays):
    return [whole(x.shape) for x in arrays]


def floats(*shapes):
    return [jax.ShapeDtypeStruct(s, F32) for s in shapes]


def in_vmem():
    return pl.BlockSpec(memory_space=pltpu.VMEM)


def call(kernel, name, grid, ins, in_specs, out_shapes, out_specs, scratch, vmem=56):
    return pl.pallas_call(
        kernel,
        grid=grid,
        in_specs=in_specs,
        out_specs=out_specs,
        out_shape=out_shapes,
        scratch_shapes=scratch,
        compiler_params=pltpu.CompilerParams(vmem_limit_bytes=vmem * 1024 * 1024),
        name=name,
    )(*ins)


def turns(count):
    return [lambda i: 0, lambda i: 2 * i + 1, lambda i: jnp.minimum(2 * i + 2, count - 1)]


def column_block(rows, width, turn):
    return pl.BlockSpec((rows, width), lambda i: (0, turn(i)))


def run_index(key_blocks, qpos, iq, ik, w):
    rows, keys = iq.shape[0], ik.shape[0]
    groups = IDX_HEADS // GROUP
    shapes = [(rows, keys), (16, 128)]
    stored = (groups, GROUP * rows, keys)
    return call(
        index_kernel,
        "index_forward",
        (groups // 2,),
        (key_blocks, qpos, iq, iq, iq, ik, w),
        [
            smem(),
            whole(qpos.shape),
            *[column_block(rows, GROUP * 128, turn) for turn in turns(groups)],
            *wholes([ik, w]),
        ],
        [*floats(*shapes), jax.ShapeDtypeStruct(stored, BF16)],
        [*[whole(s) for s in shapes], pl.BlockSpec((2, *stored[1:]), lambda i: (i, 0, 0))],
        [
            pltpu.VMEM((IDX_HEADS, rows, 128), F32),
            pltpu.VMEM((qpos.shape[1], 128), jnp.int32),
            pltpu.VMEM((GROUP * rows, keys), F32),
            pltpu.VMEM((GROUP * rows, keys), F32),
        ],
    )


def main_specs(queries, keys, pairs):
    specs = []
    for turn in turns(pairs):
        specs += [
            column_block(queries, 256, turn),
            column_block(queries, 128, turn),
            column_block(keys, 256, turn),
        ]
    return specs


def run_stats(key_blocks, qpos, index_row, qn, qr, kn, krt):
    queries, keys, pairs = qn.shape[0], kn.shape[0], qn.shape[1] // 256
    shape = (2 * pairs, queries + 128)
    return call(
        stats_kernel,
        "main_stats",
        (pairs // 2,),
        (key_blocks, qpos, index_row, krt, *[qn, qr, kn] * 3),
        [smem(), *wholes([qpos, index_row, krt]), *main_specs(queries, keys, pairs)],
        floats(shape),
        [whole(shape)],
        [
            pltpu.VMEM((keys, queries), F32),
            pltpu.VMEM((2, keys, 128), BF16),
            pltpu.VMEM((2, keys, queries), F32),
            pltpu.VMEM((2, keys, queries), F32),
        ],
    )[0]


def run_probs(lse, qn, qr, kn, krt):
    queries, keys, pairs = qn.shape[0], kn.shape[0], qn.shape[1] // 256
    return call(
        probs_kernel,
        "main_probs",
        (pairs // 2,),
        (lse, krt, *[qn, qr, kn] * 3),
        [*wholes([lse, krt]), *main_specs(queries, keys, pairs)],
        floats((queries, keys)),
        [whole((queries, keys))],
        [
            pltpu.VMEM((2, keys, 128), BF16),
            pltpu.VMEM((2, queries, keys), F32),
            pltpu.VMEM((2, queries, keys), F32),
        ],
    )[0]


def run_lg(lse, logits, target):
    return pl.pallas_call(
        lg_kernel,
        in_specs=[in_vmem()] * 3,
        out_specs=in_vmem(),
        out_shape=floats(logits.shape)[0],
        compiler_params=pltpu.CompilerParams(vmem_limit_bytes=8 * 1024 * 1024),
        name="logit_grad",
    )(lse, logits, target)


def run_gk(lg, iq, w, r):
    rows, keys = lg.shape
    shapes = [(keys // 128, 128, IDX_DIM), (16, 256)]
    return call(
        gk_kernel,
        "grad_k",
        (IDX_HEADS // GROUP,),
        (lg, iq, w, r),
        [
            whole(lg.shape),
            pl.BlockSpec((rows, GROUP * 128), lambda i: (0, i)),
            whole(w.shape),
            pl.BlockSpec((1, *r.shape[1:]), lambda i: (i, 0, 0)),
        ],
        floats(*shapes),
        [whole(s) for s in shapes],
        [
            pltpu.VMEM((IDX_HEADS, rows, 128), F32),
            pltpu.VMEM((rows, keys), BF16),
            pltpu.VMEM((IDX_DIM, keys), F32),
            pltpu.VMEM((rows, IDX_HEADS), F32),
        ],
    )


def run_inner(iq, iks):
    rows, keys = iq.shape[0], iks[0].shape[0]
    stored, kept = (2, 4, 8 * rows, keys), (4, keys, IDX_DIM)
    return call(
        inner_kernel,
        "inner_group",
        (2, 4),
        [iq, *iks],
        wholes([iq, *iks]),
        [jax.ShapeDtypeStruct(stored, BF16), jax.ShapeDtypeStruct(kept, BF16)],
        [pl.BlockSpec((1, 1, *stored[2:]), lambda i, j: (i, j, 0, 0)), whole(kept)],
        [],
    )


def run_gq(lgs, r, ikb, w, gwy, gwc):
    rows, keys = lgs[0].shape
    shape = (N_Z, rows + 16, 256)
    return call(
        gq_kernel,
        "grad_q",
        (2, 4),
        [*lgs, r, ikb, w, gwy, gwc],
        [
            *wholes(lgs),
            pl.BlockSpec((1, 1, *r.shape[2:]), lambda i, j: (i, j, 0, 0)),
            *wholes([ikb, w, gwy, gwc]),
        ],
        floats(shape),
        [pl.BlockSpec((4, *shape[1:]), lambda i, j: (i, 0, 0))],
        [
            pltpu.VMEM((IDX_HEADS, rows, 128), F32),
            pltpu.VMEM((4, rows, keys), BF16),
            pltpu.VMEM((8 * rows, IDX_DIM), F32),
        ],
    )[0]


def run_finish(parts, gks):
    shapes = [(64, 256), (128, 128), (64, 64)]
    return pl.pallas_call(
        finish_kernel,
        in_specs=[in_vmem()] * 2,
        out_specs=[in_vmem()] * 3,
        out_shape=floats(*shapes),
        name="finish",
    )(parts, gks)


def ctx_xor(value, bits):
    return lax.ppermute(value, "ctx", [(i, i ^ bits) for i in range(N_CTX)])


def z_shift(value, by):
    to = [i // 16 * 16 + (i // 2 + by) % N_Z * 2 + i % 2 for i in range(N_CTX)]
    return lax.ppermute(value, "ctx", list(enumerate(to)))


def merged(*values):
    top = values[0]
    for value in values[1:]:
        top = jnp.maximum(top, value)
    total = sum(jnp.exp2(value - top) for value in values)
    return top + jnp.log2(total)


def per_device(qn, qr, kn, kr, iq, ik, w, query_pos, key_blocks):
    qpos = query_pos[None, :]
    krt = kr.T
    ikf = ik.astype(F32)
    ikf_y = ctx_xor(ikf, 16)
    logits, index_row, r = run_index(key_blocks, qpos, iq, ik, w)
    lse = run_stats(key_blocks, qpos, index_row, qn, qr, kn, krt)
    lse, ikf_y = lax.optimization_barrier((lse, ikf_y))
    lse = merged(lse, ctx_xor(lse, 1))
    lse = merged(lse, ctx_xor(lse, 16))
    below, above = z_shift(lse, 1), z_shift(lse, -1)
    two, three = merged(lse, below), merged(lse, below, above)
    lse = merged(three, z_shift(three, 3), z_shift(two, -3))
    probs = run_probs(lse, qn, qr, kn, krt)
    probs, ikf, ikf_y = lax.optimization_barrier((probs, ikf, ikf_y))
    target = lax.all_to_all(probs.reshape(N_HEAD, -1, probs.shape[1]), "head", 0, 0)
    r_group, ikb = run_inner(iq, [ik, ctx_xor(ikf, 1), ikf_y, ctx_xor(ikf_y, 1)])

    target, r_group, ikb = lax.optimization_barrier((target, r_group, ikb))
    lg = run_lg(lse[:8, qn.shape[0] :], logits, target)
    lg_y, lg_c = ctx_xor(lg, 16), ctx_xor(lg, 1)
    gks, gw = run_gk(lg, iq, w, r)
    lg_y, gw = lax.optimization_barrier((lg_y, gw))
    lg_yc = ctx_xor(lg_y, 1)
    gw = gw + ctx_xor(gw, 16)
    parts = run_gq([lg, lg_c, lg_y, lg_yc], r_group, ikb, w, gw, ctx_xor(gw, 1))
    gks, parts = lax.optimization_barrier((gks, parts))
    groups = [[(y * N_Z + z) * 2 + c for z in range(N_Z)] for y in range(2) for c in range(2)]
    parts = lax.all_to_all(parts, "ctx", 0, 0, axis_index_groups=groups)
    gks = lax.all_to_all(gks, "head", 0, 0)
    return run_finish(parts, gks)


def solution(mesh):
    return jax.shard_map(
        per_device,
        mesh=mesh,
        in_specs=(
            P(None, "head"),
            P(None, "head"),
            P("ctx", "head"),
            P("ctx", None),
            P("head", None),
            P("ctx", None),
            P("head", None),
            P(),
            P("ctx"),
        ),
        out_specs=(P("head", "ctx"), P(("ctx", "head"), None), P("head", None)),
        check_vma=False,
    )
```

```python
import math

import jax
import jax.numpy as jnp
from jax import lax
from jax.experimental import pallas as pl
from jax.experimental.pallas import tpu as pltpu
from jax.sharding import PartitionSpec as P

HEADS = 128
NOPE = 128
ROPE = 64
IDX_HEADS = 64
IDX_DIM = 128
N_CTX = 32
N_HEAD = 8
N_Z = 8
LOG2E = math.log2(math.e)
SCORE_SCALE = LOG2E / math.sqrt(NOPE + ROPE)
INV_ROOT = 1.0 / math.sqrt(IDX_DIM)
NEG = -1e30
F32 = jnp.float32
BF16 = jnp.bfloat16
NT = (((1,), (1,)), ((), ()))
NN = (((1,), (0,)), ((), ()))
GROUP = 8


def dot(a, b, dims):
    return lax.dot_general(a, b, dims, preferred_element_type=F32)


def column(row, lanes=128):
    return jnp.broadcast_to(row, (lanes, row.shape[1])).T


def ctx_place():
    ctx = lax.axis_index("ctx")
    return ctx // (2 * N_Z), ctx // 2 % N_Z, ctx % 2


def fill_rope(krt_ref, krp):
    kr = krt_ref[...].T
    zero = jnp.zeros_like(kr)
    krp[0] = jnp.concatenate([kr, zero], axis=1)
    krp[1] = jnp.concatenate([zero, kr], axis=1)


def fill_weights(w_ref, wb):
    for j in range(IDX_HEADS):
        wb[j] = jnp.broadcast_to(w_ref[:, j : j + 1], wb.shape[1:])


def lanes_of(block, width):
    return jnp.concatenate([block] * (width // 128), axis=-1)


def stacked(block):
    count = block.shape[1] // 128
    return jnp.concatenate([block[:, i * 128 : (i + 1) * 128] for i in range(count)], axis=0)


def index_kernel(
    base_ref, qpos_ref, iq_ref, ik_ref, w_ref, logits_ref, row_ref, r_ref, wb, qcol, s_ref
):
    step = pl.program_id(0)
    rows, keys = logits_ref.shape

    @pl.when(step == 0)
    def _():
        fill_weights(w_ref, wb)
        logits_ref[...] = jnp.zeros_like(logits_ref)
        qcol[...] = column(qpos_ref[...])

    s_ref[...] = dot(stacked(iq_ref[...]), ik_ref[...], NT)
    for kc in range(keys // 128):
        cols = slice(kc * 128, (kc + 1) * 128)
        total = logits_ref[:, cols]
        for i in range(GROUP):
            mine = slice(i * rows, (i + 1) * rows)
            inner = s_ref[mine, cols]
            r_ref[0, mine, cols] = inner.astype(BF16)
            total = total + jnp.maximum(inner, 0.0) * wb[step * GROUP + i]
        logits_ref[:, cols] = total

    @pl.when(step == pl.num_programs(0) - 1)
    def _():
        key = lax.broadcasted_iota(jnp.int32, (rows, keys), 1) + base_ref[0] * keys
        start = pl.multiple_of(lax.axis_index("head") * rows, rows)
        limit = lanes_of(qcol[pl.ds(start, rows), :], keys)
        logits = jnp.where(key <= limit, logits_ref[...] * (INV_ROOT * LOG2E), NEG)
        logits_ref[...] = logits
        top = jnp.max(logits, axis=1, keepdims=True)
        total = jnp.sum(jnp.exp2(logits - top), axis=1, keepdims=True)
        lse = jnp.broadcast_to(top + jnp.log2(total), (rows, 128)).T
        row_ref[...] = jnp.concatenate([lse[:16, :rows], jnp.zeros((16, 128 - rows), F32)], axis=1)


def pair_operands(refs, krp, p):
    qn_ref, qr_ref, kn_ref = refs
    part = slice(p * 128, (p + 1) * 128)
    q = jnp.concatenate([qn_ref[:, part], qr_ref[...]], axis=1)
    return q, jnp.concatenate([kn_ref[:, part], krp[p]], axis=1)


def online_lse(s_ref, bias, cols, chunk=64):
    keys = bias.shape[0]
    top = jnp.full((8, 256), 2.0 * NEG, F32)
    total = jnp.zeros((8, 256), F32)
    for kc in range(keys // chunk):
        rows = slice(kc * chunk, (kc + 1) * chunk)
        s = (s_ref[rows, cols] + bias[rows, cols]).reshape(chunk // 8, 8, 256)
        new = jnp.maximum(top, jnp.max(s, axis=0))
        e = jnp.exp2((s - new[None]) * SCORE_SCALE)
        total = total * jnp.exp2((top - new) * SCORE_SCALE) + jnp.sum(e, axis=0)
        top = new
    best = jnp.max(top, axis=0, keepdims=True)
    total = jnp.sum(total * jnp.exp2((top - best) * SCORE_SCALE), axis=0, keepdims=True)
    return best * SCORE_SCALE + jnp.log2(total)


def stats_kernel(
    base_ref, qpos_ref, row_ref, krt_ref, qn_ref, qr_ref, kn_ref, out_ref, bias, krp, s_ref
):
    step = pl.program_id(0)
    keys, queries = bias.shape

    @pl.when(step == 0)
    def _():
        key = lax.broadcasted_iota(jnp.int32, bias.shape, 0) + base_ref[0] * keys
        bias[...] = jnp.where(key <= qpos_ref[...], 0.0, NEG)
        fill_rope(krt_ref, krp)
        out_ref[:, queries:] = row_ref[...]

    for p in range(2):
        q, k = pair_operands((qn_ref, qr_ref, kn_ref), krp, p)
        s_ref[p] = dot(k, q, NT)
    for p in range(2):
        for qc in range(queries // 256):
            cols = slice(qc * 256, (qc + 1) * 256)
            out_ref[pl.ds(2 * step + p, 1), cols] = online_lse(s_ref.at[p], bias, cols)


def probs_kernel(lse_ref, krt_ref, qn_ref, qr_ref, kn_ref, out_ref, krp, s_ref):
    step = pl.program_id(0)
    queries, keys = out_ref.shape

    @pl.when(step == 0)
    def _():
        fill_rope(krt_ref, krp)
        out_ref[...] = jnp.zeros_like(out_ref)

    lse = []
    for p in range(2):
        s_ref[p] = dot(*pair_operands((qn_ref, qr_ref, kn_ref), krp, p), NT)
        lse.append(column(lse_ref[pl.ds(2 * step + p, 1), :queries]))
    for r in range(queries // 32):
        rows = slice(r * 32, (r + 1) * 32)
        total = out_ref[rows, :]
        for p in range(2):
            s = s_ref[p, rows, :] * SCORE_SCALE - lanes_of(lse[p][rows], keys)
            total = total + jnp.exp2(s)
        out_ref[rows, :] = total


def lg_kernel(lse_ref, logits_ref, target_ref, lg_ref):
    rows, width = lg_ref.shape
    lse = column(lse_ref[:1, :])[:rows]
    for c in range(width // 128):
        cols = slice(c * 128, (c + 1) * 128)
        target = target_ref[0, :, cols]
        for h in range(1, N_HEAD):
            target = target + target_ref[h, :, cols]
        logits = logits_ref[:, cols]
        lg = jnp.exp2(logits - lse) - target * (1.0 / HEADS)
        lg_ref[:, cols] = jnp.where(logits > 0.5 * NEG, lg, 0.0)


def masked_lg(r, lg):
    lg = jnp.concatenate([lg] * (r.shape[0] // lg.shape[0]), axis=0)
    return jnp.where(r > 0, lg, jnp.zeros_like(lg))


def gk_kernel(lg_ref, iq_ref, w_ref, *refs):
    rs, (gk_ref, gw_out, wb, lgb_ref, gkt_ref, gw_ref) = refs[:PIECES], refs[PIECES:]
    step = pl.program_id(0)
    rows, keys = lg_ref.shape

    @pl.when(step == 0)
    def _():
        fill_weights(w_ref, wb)
        lgb_ref[...] = lg_ref[...].astype(BF16)
        gkt_ref[...] = jnp.zeros_like(gkt_ref)
        gw_ref[...] = jnp.zeros_like(gw_ref)

    q = stacked(iq_ref[...])
    w = jnp.concatenate([wb[step * GROUP + i] for i in range(GROUP)], axis=0)
    wqt = (q.astype(F32) * w).astype(BF16).T
    totals = [jnp.zeros((rows, 128), F32) for _ in range(GROUP)]
    for kc in range(keys // 256):
        cols = slice(kc * 256, (kc + 1) * 256)
        r = jnp.concatenate([r_ref[0, :, cols] for r_ref in rs], axis=0)
        gkt_ref[:, cols] += dot(wqt, masked_lg(r, lgb_ref[:, cols]), NN)
        lg = lg_ref[:, cols]
        for i in range(GROUP):
            active = jnp.maximum(r[i * rows : (i + 1) * rows].astype(F32), 0.0) * lg
            totals[i] = totals[i] + active[:, :128] + active[:, 128:]
    lane = lax.broadcasted_iota(jnp.int32, (rows, IDX_HEADS), 1)
    new = gw_ref[...]
    for i in range(GROUP):
        value = jnp.sum(totals[i], axis=1, keepdims=True) * INV_ROOT
        new = jnp.where(lane == step * GROUP + i, value, new)
    gw_ref[...] = new

    @pl.when(step == pl.num_programs(0) - 1)
    def _():
        for c in range(keys // 128):
            gk_ref[c] = gkt_ref[:, c * 128 : (c + 1) * 128].T * INV_ROOT
        gw_out[...] = jnp.concatenate([gw_ref[i * 16 : (i + 1) * 16, :] for i in range(4)], axis=1)


def group_dests(part):
    y_lo, _, core = ctx_place()
    return [(y_lo * N_Z + part * 4 + i) * 2 + core for i in range(4)]


def inner_kernel(iq_ref, *refs):
    iks, (r_ref, ikb_ref) = refs[:4], refs[4:]
    part, source = pl.program_id(0), pl.program_id(1)

    @pl.when((part == 0) & (source == 0))
    def _():
        for i in range(4):
            ikb_ref[i] = iks[i][...].astype(BF16)

    dests = group_dests(part)
    blocks = [iq_ref[:, pl.ds(pl.multiple_of(c * 256, 256), 256)] for c in dests]
    q = jnp.concatenate([stacked(block) for block in blocks], axis=0)
    r_ref[0, 0] = dot(q, ikb_ref[source], NT).astype(BF16)


def gq_kernel(lg0, lg1, lg2, lg3, *refs):
    rs, (ikb_ref, w_ref, *gws) = refs[:PIECES], refs[PIECES : PIECES + 6]
    gq_ref, wb, lgb_ref, g_ref = refs[PIECES + 6 :]
    part, source = pl.program_id(0), pl.program_id(1)
    rows = lg0.shape[0]

    @pl.when((part == 0) & (source == 0))
    def _():
        fill_weights(w_ref, wb)
        for i, lg in enumerate((lg0, lg1, lg2, lg3)):
            lgb_ref[i] = lg[...].astype(BF16)

    r = jnp.concatenate([r_ref[0, 0] for r_ref in rs], axis=0)
    grown = dot(masked_lg(r, lgb_ref[source]), ikb_ref[source], NN)

    @pl.when(source == 0)
    def _():
        g_ref[...] = grown

    @pl.when(source > 0)
    def _():
        g_ref[...] += grown

    @pl.when(source == 3)
    def _():
        gw = (gws[0][...] + gws[1][...]) + (gws[2][...] + gws[3][...])
        dests = group_dests(part)
        for i in range(4):
            pair = []
            for n in range(2):
                at = (2 * i + n) * rows
                pair.append(g_ref[at : at + rows, :] * wb[dests[i] * 2 + n] * INV_ROOT)
            gq_ref[i, :rows, :] = jnp.concatenate(pair, axis=1)
            gq_ref[i, rows:, :] = gw


def finish_kernel(parts_ref, gks_ref, gq_ref, gk_ref, gw_ref):
    total, keys = parts_ref[0], gks_ref[0]
    for i in range(1, 8):
        total = total + parts_ref[i]
        keys = keys + gks_ref[i]
    gq_ref[...] = total[:64]
    gk_ref[...] = keys
    gw_ref[...] = jnp.concatenate([total[64:, i * 64 : (i + 1) * 64] for i in range(4)], axis=0)


def smem():
    return pl.BlockSpec(memory_space=pltpu.SMEM)


def whole(shape):
    return pl.BlockSpec(shape, lambda *_: (0,) * len(shape))


def wholes(arrays):
    return [whole(x.shape) for x in arrays]


def floats(*shapes):
    return [jax.ShapeDtypeStruct(s, F32) for s in shapes]


PIECES = 4


def piece_specs(shape, index):
    *lead, rows, width = shape
    block = (*[1] * len(lead), rows // PIECES, width)
    return [pl.BlockSpec(block, lambda *at, n=n: (*index(*at), n, 0)) for n in range(PIECES)]


def in_vmem():
    return pl.BlockSpec(memory_space=pltpu.VMEM)


def call(kernel, name, grid, ins, in_specs, out_shapes, out_specs, scratch, vmem=56):
    return pl.pallas_call(
        kernel,
        grid=grid,
        in_specs=in_specs,
        out_specs=out_specs,
        out_shape=out_shapes,
        scratch_shapes=scratch,
        compiler_params=pltpu.CompilerParams(vmem_limit_bytes=vmem * 1024 * 1024),
        name=name,
    )(*ins)


def run_index(key_blocks, qpos, iq, ik, w):
    rows, keys = iq.shape[0], ik.shape[0]
    groups = IDX_HEADS // GROUP
    shapes = [(rows, keys), (16, 128)]
    stored = (groups, GROUP * rows, keys)
    return call(
        index_kernel,
        "index_forward",
        (groups,),
        (key_blocks, qpos, iq, ik, w),
        [
            smem(),
            whole(qpos.shape),
            pl.BlockSpec((rows, GROUP * 128), lambda i: (0, i)),
            *wholes([ik, w]),
        ],
        [*floats(*shapes), jax.ShapeDtypeStruct(stored, BF16)],
        [*[whole(s) for s in shapes], pl.BlockSpec((1, *stored[1:]), lambda i: (i, 0, 0))],
        [
            pltpu.VMEM((IDX_HEADS, rows, 128), F32),
            pltpu.VMEM((qpos.shape[1], 128), jnp.int32),
            pltpu.VMEM((GROUP * rows, keys), F32),
        ],
    )


def main_specs(queries, keys):
    return [
        pl.BlockSpec((queries, 256), lambda i: (0, i)),
        pl.BlockSpec((queries, 128), lambda i: (0, i)),
        pl.BlockSpec((keys, 256), lambda i: (0, i)),
    ]


def run_stats(key_blocks, qpos, index_row, qn, qr, kn, krt):
    queries, keys, pairs = qn.shape[0], kn.shape[0], qn.shape[1] // 256
    shape = (2 * pairs, queries + 128)
    return call(
        stats_kernel,
        "main_stats",
        (pairs,),
        (key_blocks, qpos, index_row, krt, qn, qr, kn),
        [smem(), *wholes([qpos, index_row, krt]), *main_specs(queries, keys)],
        floats(shape),
        [whole(shape)],
        [
            pltpu.VMEM((keys, queries), F32),
            pltpu.VMEM((2, keys, 128), BF16),
            pltpu.VMEM((2, keys, queries), F32),
        ],
    )[0]


def run_probs(lse, qn, qr, kn, krt):
    queries, keys, pairs = qn.shape[0], kn.shape[0], qn.shape[1] // 256
    return call(
        probs_kernel,
        "main_probs",
        (pairs,),
        (lse, krt, qn, qr, kn),
        [*wholes([lse, krt]), *main_specs(queries, keys)],
        floats((queries, keys)),
        [whole((queries, keys))],
        [pltpu.VMEM((2, keys, 128), BF16), pltpu.VMEM((2, queries, keys), F32)],
    )[0]


def run_lg(lse, logits, target):
    return pl.pallas_call(
        lg_kernel,
        in_specs=[in_vmem()] * 3,
        out_specs=in_vmem(),
        out_shape=floats(logits.shape)[0],
        compiler_params=pltpu.CompilerParams(vmem_limit_bytes=8 * 1024 * 1024),
        name="logit_grad",
    )(lse, logits, target)


def run_gk(lg, iq, w, r):
    rows, keys = lg.shape
    shapes = [(keys // 128, 128, IDX_DIM), (16, 256)]
    return call(
        gk_kernel,
        "grad_k",
        (IDX_HEADS // GROUP,),
        (lg, iq, w, *[r] * PIECES),
        [
            whole(lg.shape),
            pl.BlockSpec((rows, GROUP * 128), lambda i: (0, i)),
            whole(w.shape),
            *piece_specs(r.shape, lambda i: (i,)),
        ],
        floats(*shapes),
        [whole(s) for s in shapes],
        [
            pltpu.VMEM((IDX_HEADS, rows, 128), F32),
            pltpu.VMEM((rows, keys), BF16),
            pltpu.VMEM((IDX_DIM, keys), F32),
            pltpu.VMEM((rows, IDX_HEADS), F32),
        ],
    )


def run_inner(iq, iks):
    rows, keys = iq.shape[0], iks[0].shape[0]
    stored, kept = (2, 4, 8 * rows, keys), (4, keys, IDX_DIM)
    return call(
        inner_kernel,
        "inner_group",
        (2, 4),
        [iq, *iks],
        wholes([iq, *iks]),
        [jax.ShapeDtypeStruct(stored, BF16), jax.ShapeDtypeStruct(kept, BF16)],
        [pl.BlockSpec((1, 1, *stored[2:]), lambda i, j: (i, j, 0, 0)), whole(kept)],
        [],
    )


def run_gq(lgs, r, ikb, w, gws):
    rows, keys = lgs[0].shape
    shape = (N_Z, rows + 16, 256)
    return call(
        gq_kernel,
        "grad_q",
        (2, 4),
        [*lgs, *[r] * PIECES, ikb, w, *gws],
        [
            *wholes(lgs),
            *piece_specs(r.shape, lambda i, j: (i, j)),
            *wholes([ikb, w, *gws]),
        ],
        floats(shape),
        [pl.BlockSpec((4, *shape[1:]), lambda i, j: (i, 0, 0))],
        [
            pltpu.VMEM((IDX_HEADS, rows, 128), F32),
            pltpu.VMEM((4, rows, keys), BF16),
            pltpu.VMEM((8 * rows, IDX_DIM), F32),
        ],
    )[0]


def run_finish(parts, gks):
    shapes = [(64, 256), (128, 128), (64, 64)]
    return pl.pallas_call(
        finish_kernel,
        in_specs=[in_vmem()] * 2,
        out_specs=[in_vmem()] * 3,
        out_shape=floats(*shapes),
        name="finish",
    )(parts, gks)


def ctx_xor(value, bits):
    return lax.ppermute(value, "ctx", [(i, i ^ bits) for i in range(N_CTX)])


def z_shift(value, by):
    to = [i // 16 * 16 + (i // 2 + by) % N_Z * 2 + i % 2 for i in range(N_CTX)]
    return lax.ppermute(value, "ctx", list(enumerate(to)))


def merged(*values):
    top = values[0]
    for value in values[1:]:
        top = jnp.maximum(top, value)
    total = sum(jnp.exp2(value - top) for value in values)
    return top + jnp.log2(total)


def per_device(qn, qr, kn, kr, iq, ik, w, query_pos, key_blocks):
    qpos = query_pos[None, :]
    krt = kr.T
    ikf = ik.astype(F32)
    ikf_y = ctx_xor(ikf, 16)
    logits, index_row, r = run_index(key_blocks, qpos, iq, ik, w)
    lse = run_stats(key_blocks, qpos, index_row, qn, qr, kn, krt)
    lse, ikf_y = lax.optimization_barrier((lse, ikf_y))
    lse = merged(lse, ctx_xor(lse, 1))
    lse = merged(lse, ctx_xor(lse, 16))
    below, above = z_shift(lse, 1), z_shift(lse, -1)
    two, three = merged(lse, below), merged(lse, below, above)
    lse = merged(three, z_shift(three, 3), z_shift(two, -3))
    probs = run_probs(lse, qn, qr, kn, krt)
    probs, ikf, ikf_y = lax.optimization_barrier((probs, ikf, ikf_y))
    target = lax.all_to_all(probs.reshape(N_HEAD, -1, probs.shape[1]), "head", 0, 0)
    r_group, ikb = run_inner(iq, [ik, ctx_xor(ikf, 1), ikf_y, ctx_xor(ikf_y, 1)])

    target, r_group, ikb = lax.optimization_barrier((target, r_group, ikb))
    lg = run_lg(lse[:8, qn.shape[0] :], logits, target)
    lg_y, lg_c = ctx_xor(lg, 16), ctx_xor(lg, 1)
    gks, gw = run_gk(lg, iq, w, r)
    lg_y, gw = lax.optimization_barrier((lg_y, gw))
    lg_yc = ctx_xor(lg_y, 1)
    gws = [gw, *[ctx_xor(gw, bits) for bits in (16, 17, 1)]]
    parts = run_gq([lg, lg_c, lg_y, lg_yc], r_group, ikb, w, gws)
    groups = [[(y * N_Z + z) * 2 + c for z in range(N_Z)] for y in range(2) for c in range(2)]
    parts = lax.all_to_all(parts, "ctx", 0, 0, axis_index_groups=groups)
    gks = lax.all_to_all(gks, "head", 0, 0)
    return run_finish(parts, gks)


def solution(mesh):
    return jax.shard_map(
        per_device,
        mesh=mesh,
        in_specs=(
            P(None, "head"),
            P(None, "head"),
            P("ctx", "head"),
            P("ctx", None),
            P("head", None),
            P("ctx", None),
            P("head", None),
            P(),
            P("ctx"),
        ),
        out_specs=(P("head", "ctx"), P(("ctx", "head"), None), P("head", None)),
        check_vma=False,
    )
```

```python
import math

import jax
import jax.numpy as jnp
from jax import lax
from jax.experimental import pallas as pl
from jax.experimental.pallas import tpu as pltpu
from jax.sharding import PartitionSpec as P

HEADS = 128
NOPE = 128
ROPE = 64
IDX_HEADS = 64
IDX_DIM = 128
N_CTX = 32
N_HEAD = 8
N_Z = 8
LOG2E = math.log2(math.e)
SCORE_SCALE = LOG2E / math.sqrt(NOPE + ROPE)
INV_ROOT = 1.0 / math.sqrt(IDX_DIM)
NEG = -1e30
F32 = jnp.float32
BF16 = jnp.bfloat16
NT = (((1,), (1,)), ((), ()))
NN = (((1,), (0,)), ((), ()))
GROUP = 8


def dot(a, b, dims):
    return lax.dot_general(a, b, dims, preferred_element_type=F32)


def column(row, lanes=128):
    return jnp.broadcast_to(row, (lanes, row.shape[1])).T


def ctx_place():
    ctx = lax.axis_index("ctx")
    return ctx // (2 * N_Z), ctx // 2 % N_Z, ctx % 2


def fill_rope(krt_ref, krp):
    kr = krt_ref[...].T
    zero = jnp.zeros_like(kr)
    krp[0] = jnp.concatenate([kr, zero], axis=1)
    krp[1] = jnp.concatenate([zero, kr], axis=1)


def fill_weights(w_ref, wb):
    for j in range(IDX_HEADS):
        wb[j] = jnp.broadcast_to(w_ref[:, j : j + 1], wb.shape[1:])


def lanes_of(block, width):
    return jnp.concatenate([block] * (width // 128), axis=-1)


def stacked(block):
    count = block.shape[1] // 128
    return jnp.concatenate([block[:, i * 128 : (i + 1) * 128] for i in range(count)], axis=0)


def index_kernel(base_ref, qpos_ref, iq_ref, ik_ref, w_ref, logits_ref, row_ref, wp, qcol, s_ref, acc):
    step = pl.program_id(0)
    rows, keys = logits_ref.shape

    @pl.when(step == 0)
    def _():
        wt = w_ref[...].T
        for i in range(IDX_HEADS // 2):
            pair = [wt[2 * i : 2 * i + 1], wt[2 * i + 1 : 2 * i + 2]]
            wp[i : i + 1, :] = jnp.concatenate(pair, axis=1)
        acc[...] = jnp.zeros_like(acc)
        qcol[...] = column(qpos_ref[...])

    s_ref[...] = dot(ik_ref[...], stacked(iq_ref[...]), NT)
    weights = [wp[pl.ds(step * GROUP // 2 + i, 1), :] for i in range(GROUP // 2)]
    for r in range(keys // 64):
        at = slice(r * 64, (r + 1) * 64)
        total = acc[at, :]
        for i, weight in enumerate(weights):
            total = total + jnp.maximum(s_ref[at, i * 128 : (i + 1) * 128], 0.0) * weight
        acc[at, :] = total

    @pl.when(step == pl.num_programs(0) - 1)
    def _():
        turned = acc[...].T
        key = lax.broadcasted_iota(jnp.int32, (rows, keys), 1) + base_ref[0] * keys
        start = pl.multiple_of(lax.axis_index("head") * rows, rows)
        limit = lanes_of(qcol[pl.ds(start, rows), :], keys)
        logits = (turned[:rows] + turned[rows:]) * (INV_ROOT * LOG2E)
        logits = jnp.where(key <= limit, logits, NEG)
        logits_ref[...] = logits
        top = jnp.max(logits, axis=1, keepdims=True)
        total = jnp.sum(jnp.exp2(logits - top), axis=1, keepdims=True)
        lse = jnp.broadcast_to(top + jnp.log2(total), (rows, 128)).T
        row_ref[...] = jnp.concatenate([lse[:16, :rows], jnp.zeros((16, 128 - rows), F32)], axis=1)


def pair_operands(refs, krp, p):
    qn_ref, qr_ref, kn_ref = refs
    part = slice(p * 128, (p + 1) * 128)
    q = jnp.concatenate([qn_ref[:, part], qr_ref[...]], axis=1)
    return q, jnp.concatenate([kn_ref[:, part], krp[p]], axis=1)


def online_lse(s_ref, bias, cols, chunk=64):
    keys = bias.shape[0]
    top = jnp.full((8, 256), 2.0 * NEG, F32)
    total = jnp.zeros((8, 256), F32)
    for kc in range(keys // chunk):
        rows = slice(kc * chunk, (kc + 1) * chunk)
        s = (s_ref[rows, cols] + bias[rows, cols]).reshape(chunk // 8, 8, 256)
        new = jnp.maximum(top, jnp.max(s, axis=0))
        e = jnp.exp2((s - new[None]) * SCORE_SCALE)
        total = total * jnp.exp2((top - new) * SCORE_SCALE) + jnp.sum(e, axis=0)
        top = new
    best = jnp.max(top, axis=0, keepdims=True)
    total = jnp.sum(total * jnp.exp2((top - best) * SCORE_SCALE), axis=0, keepdims=True)
    return best * SCORE_SCALE + jnp.log2(total)


def stats_kernel(
    base_ref, qpos_ref, row_ref, krt_ref, qn_ref, qr_ref, kn_ref, out_ref, bias, krp, s_ref
):
    step = pl.program_id(0)
    keys, queries = bias.shape

    @pl.when(step == 0)
    def _():
        key = lax.broadcasted_iota(jnp.int32, bias.shape, 0) + base_ref[0] * keys
        bias[...] = jnp.where(key <= qpos_ref[...], 0.0, NEG)
        fill_rope(krt_ref, krp)
        out_ref[:, queries:] = row_ref[...]

    for p in range(2):
        q, k = pair_operands((qn_ref, qr_ref, kn_ref), krp, p)
        s_ref[p] = dot(k, q, NT)
    for p in range(2):
        for qc in range(queries // 256):
            cols = slice(qc * 256, (qc + 1) * 256)
            out_ref[pl.ds(2 * step + p, 1), cols] = online_lse(s_ref.at[p], bias, cols)


def probs_kernel(lse_ref, krt_ref, qn_ref, qr_ref, kn_ref, out_ref, krp, s_ref):
    step = pl.program_id(0)
    queries, keys = out_ref.shape

    @pl.when(step == 0)
    def _():
        fill_rope(krt_ref, krp)
        out_ref[...] = jnp.zeros_like(out_ref)

    lse = []
    for p in range(2):
        s_ref[p] = dot(*pair_operands((qn_ref, qr_ref, kn_ref), krp, p), NT)
        lse.append(column(lse_ref[pl.ds(2 * step + p, 1), :queries]))
    for r in range(queries // 32):
        rows = slice(r * 32, (r + 1) * 32)
        total = out_ref[rows, :]
        for p in range(2):
            s = s_ref[p, rows, :] * SCORE_SCALE - lanes_of(lse[p][rows], keys)
            total = total + jnp.exp2(s)
        out_ref[rows, :] = total


def lg_kernel(lse_ref, logits_ref, target_ref, lg_ref):
    rows, width = lg_ref.shape
    lse = column(lse_ref[:1, lse_ref.shape[1] - 128 :])[:rows]
    for c in range(width // 128):
        cols = slice(c * 128, (c + 1) * 128)
        target = target_ref[0, :, cols]
        for h in range(1, N_HEAD):
            target = target + target_ref[h, :, cols]
        logits = logits_ref[:, cols]
        lg = jnp.exp2(logits - lse) - target * (1.0 / HEADS)
        lg_ref[:, cols] = jnp.where(logits > 0.5 * NEG, lg, 0.0)


def gk_kernel(
    lg_ref, iq_ref, ik_ref, w_ref, keep_ref, send_ref, gw_out, wb, lgt_ref, m_ref, gk_ref, gwt_ref
):
    step = pl.program_id(0)
    rows, keys = lg_ref.shape
    width = GROUP * rows

    @pl.when(step == 0)
    def _():
        fill_weights(w_ref, wb)
        lgt_ref[...] = jnp.concatenate([lg_ref[...]] * (128 // rows), axis=0).T
        gk_ref[...] = jnp.zeros_like(gk_ref)

    q = stacked(iq_ref[...])
    w = jnp.concatenate([wb[step * GROUP + i] for i in range(GROUP)], axis=0)
    wq = (q.astype(F32) * w).astype(BF16)
    gw = jnp.zeros((8, width), F32)
    for c in range(2):
        inner = dot(ik_ref[c * 512 : (c + 1) * 512, :], q, NT)
        for r in range(16):
            at = slice(c * 512 + r * 32, c * 512 + (r + 1) * 32)
            part = inner[r * 32 : (r + 1) * 32]
            masked = jnp.where(part > 0.0, lanes_of(lgt_ref[at, :], width), 0.0)
            m_ref[at, :] = masked.astype(BF16)
            gw = gw + jnp.sum((part * masked).reshape(4, 8, width), axis=0)
        at = slice(c * 512, (c + 1) * 512)
        gk_ref[at, :] += dot(m_ref[at, :], wq, NN)
    gw = jnp.sum(gw, axis=0, keepdims=True) * INV_ROOT
    for i in range(GROUP):
        gwt_ref[pl.ds(step * GROUP + i, 1), :] = gw[:, i * rows : (i + 1) * rows]

    @pl.when(step == pl.num_programs(0) - 1)
    def _():
        me = lax.axis_index("head")
        size = keys // N_HEAD
        for out, slots in ((keep_ref, (0, 1, 6, 7)), (send_ref, (2, 3, 4, 5))):
            for n, m in enumerate(slots):
                start = pl.multiple_of((me ^ m) * size, size)
                out[n] = gk_ref[pl.ds(start, size), :] * INV_ROOT
        gw_out[...] = jnp.concatenate([gwt_ref[i * 16 : (i + 1) * 16] for i in range(4)], axis=1)


def gq_kernel(*refs):
    lgs, iks, (iq_ref, w_ref), gws = refs[:4], refs[4:8], refs[8:10], refs[10:14]
    gq_ref, wb, lg_ref, ikb_ref, q_ref, g_ref = refs[14:]
    source = pl.program_id(0)
    rows, keys = lgs[0].shape
    count = q_ref.shape[0] // rows
    y_lo, _, core = ctx_place()
    dests = [(y_lo * N_Z + i) * 2 + core for i in range(N_Z)]

    @pl.when(source == 0)
    def _():
        fill_weights(w_ref, wb)
        g_ref[...] = jnp.zeros_like(g_ref)
        for i in range(4):
            lg_ref[i] = lgs[i][...]
            ikb_ref[i] = iks[i][...].astype(BF16)
        for i in range(N_Z):
            block = iq_ref[:, pl.ds(pl.multiple_of(dests[i] * 256, 256), 256)]
            q_ref[2 * i * rows : 2 * (i + 1) * rows, :] = stacked(block)

    for c in range(4):
        cols = slice(c * 256, (c + 1) * 256)
        k = ikb_ref[source, cols, :]
        inner = dot(q_ref[...], k, NT)
        lg = jnp.concatenate([lg_ref[source, :, cols]] * count, axis=0)
        g_ref[...] += dot(jnp.where(inner > 0.0, lg, 0.0).astype(BF16), k, NN)

    @pl.when(source == 3)
    def _():
        gw = (gws[0][...] + gws[1][...]) + (gws[2][...] + gws[3][...])
        for i in range(N_Z):
            pair = []
            for n in range(2):
                at = (2 * i + n) * rows
                pair.append(g_ref[at : at + rows, :] * wb[dests[i] * 2 + n] * INV_ROOT)
            gq_ref[i, :rows, :] = jnp.concatenate(pair, axis=1)
            gq_ref[i, rows:, :] = gw


def finish_kernel(parts_ref, mine_ref, got_ref, gq_ref, gk_ref, gw_ref):
    total = parts_ref[0]
    for i in range(1, N_Z):
        total = total + parts_ref[i]
    gq_ref[...] = total[:64]
    gk_ref[...] = mine_ref[...] + got_ref[...]
    gwt = jnp.concatenate([total[64:, i * 64 : (i + 1) * 64] for i in range(4)], axis=0)
    gw_ref[...] = gwt.T


def smem():
    return pl.BlockSpec(memory_space=pltpu.SMEM)


def whole(shape):
    return pl.BlockSpec(shape, lambda *_: (0,) * len(shape))


def wholes(arrays):
    return [whole(x.shape) for x in arrays]


def floats(*shapes):
    return [jax.ShapeDtypeStruct(s, F32) for s in shapes]


def in_vmem():
    return pl.BlockSpec(memory_space=pltpu.VMEM)


def call(kernel, name, grid, ins, in_specs, out_shapes, out_specs, scratch, vmem=56):
    return pl.pallas_call(
        kernel,
        grid=grid,
        in_specs=in_specs,
        out_specs=out_specs,
        out_shape=out_shapes,
        scratch_shapes=scratch,
        compiler_params=pltpu.CompilerParams(vmem_limit_bytes=vmem * 1024 * 1024),
        name=name,
    )(*ins)


def run_index(key_blocks, qpos, iq, ik, w):
    rows, keys = iq.shape[0], ik.shape[0]
    groups = IDX_HEADS // GROUP
    shapes = [(rows, keys), (16, 128)]
    return call(
        index_kernel,
        "index_forward",
        (groups,),
        (key_blocks, qpos, iq, ik, w),
        [
            smem(),
            whole(qpos.shape),
            pl.BlockSpec((rows, GROUP * 128), lambda i: (0, i)),
            *wholes([ik, w]),
        ],
        floats(*shapes),
        [whole(s) for s in shapes],
        [
            pltpu.VMEM((IDX_HEADS // 2, 128), F32),
            pltpu.VMEM((qpos.shape[1], 128), jnp.int32),
            pltpu.VMEM((keys, GROUP * rows), F32),
            pltpu.VMEM((keys, 128), F32),
        ],
    )


def main_specs(queries, keys):
    return [
        pl.BlockSpec((queries, 256), lambda i: (0, i)),
        pl.BlockSpec((queries, 128), lambda i: (0, i)),
        pl.BlockSpec((keys, 256), lambda i: (0, i)),
    ]


def run_stats(key_blocks, qpos, index_row, qn, qr, kn, krt):
    queries, keys, pairs = qn.shape[0], kn.shape[0], qn.shape[1] // 256
    shape = (2 * pairs, queries + 128)
    return call(
        stats_kernel,
        "main_stats",
        (pairs,),
        (key_blocks, qpos, index_row, krt, qn, qr, kn),
        [smem(), *wholes([qpos, index_row, krt]), *main_specs(queries, keys)],
        floats(shape),
        [whole(shape)],
        [
            pltpu.VMEM((keys, queries), F32),
            pltpu.VMEM((2, keys, 128), BF16),
            pltpu.VMEM((2, keys, queries), F32),
        ],
    )[0]


def run_probs(lse, qn, qr, kn, krt):
    queries, keys, pairs = qn.shape[0], kn.shape[0], qn.shape[1] // 256
    return call(
        probs_kernel,
        "main_probs",
        (pairs,),
        (lse, krt, qn, qr, kn),
        [*wholes([lse, krt]), *main_specs(queries, keys)],
        floats((queries, keys)),
        [whole((queries, keys))],
        [pltpu.VMEM((2, keys, 128), BF16), pltpu.VMEM((2, queries, keys), F32)],
        24,
    )[0]


def run_lg(lse, logits, target):
    return pl.pallas_call(
        lg_kernel,
        in_specs=[in_vmem()] * 3,
        out_specs=in_vmem(),
        out_shape=floats(logits.shape)[0],
        compiler_params=pltpu.CompilerParams(vmem_limit_bytes=8 * 1024 * 1024),
        name="logit_grad",
    )(lse, logits, target)


def run_gk(lg, iq, ik, w):
    rows, keys = lg.shape
    size = keys // N_HEAD
    shapes = [(4, size, IDX_DIM), (4, size, IDX_DIM), (16, 256)]
    return call(
        gk_kernel,
        "grad_k",
        (IDX_HEADS // GROUP,),
        (lg, iq, ik, w),
        [
            whole(lg.shape),
            pl.BlockSpec((rows, GROUP * 128), lambda i: (0, i)),
            *wholes([ik, w]),
        ],
        floats(*shapes),
        [whole(s) for s in shapes],
        [
            pltpu.VMEM((IDX_HEADS, rows, 128), F32),
            pltpu.VMEM((keys, 128), F32),
            pltpu.VMEM((keys, GROUP * rows), BF16),
            pltpu.VMEM((keys, IDX_DIM), F32),
            pltpu.VMEM((IDX_HEADS, rows), F32),
        ],
        20,
    )


def run_gq(lgs, iks, iq, w, gws):
    rows, keys = lgs[0].shape
    shape = (N_Z, rows + 16, 256)
    ins = [*lgs, *iks, iq, w, *gws]
    return call(
        gq_kernel,
        "grad_q",
        (4,),
        ins,
        wholes(ins),
        floats(shape),
        [whole(shape)],
        [
            pltpu.VMEM((IDX_HEADS, rows, 128), F32),
            pltpu.VMEM((4, rows, keys), F32),
            pltpu.VMEM((4, keys, IDX_DIM), BF16),
            pltpu.VMEM((2 * N_Z * rows, IDX_DIM), BF16),
            pltpu.VMEM((2 * N_Z * rows, IDX_DIM), F32),
        ],
        28,
    )[0]


def run_finish(*ins):
    shapes = [(64, 256), (128, 128), (64, 64)]
    return pl.pallas_call(
        finish_kernel,
        in_specs=[in_vmem()] * 3,
        out_specs=[in_vmem()] * 3,
        out_shape=floats(*shapes),
        name="finish",
    )(*ins)


def head_xor(value, bits):
    return lax.ppermute(value, "head", [(i, i ^ bits) for i in range(N_HEAD)])


def ctx_xor(value, bits):
    return lax.ppermute(value, "ctx", [(i, i ^ bits) for i in range(N_CTX)])


def z_shift(value, by):
    to = [i // 16 * 16 + (i // 2 + by) % N_Z * 2 + i % 2 for i in range(N_CTX)]
    return lax.ppermute(value, "ctx", list(enumerate(to)))


def merged(*values):
    top = values[0]
    for value in values[1:]:
        top = jnp.maximum(top, value)
    total = sum(jnp.exp2(value - top) for value in values)
    return top + jnp.log2(total)


def per_device(qn, qr, kn, kr, iq, ik, w, query_pos, key_blocks):
    qpos = query_pos[None, :]
    krt = kr.T
    ikf = ik.astype(F32)
    ikf_y = ctx_xor(ikf, 16)
    logits, index_row = run_index(key_blocks, qpos, iq, ik, w)
    lse = run_stats(key_blocks, qpos, index_row, qn, qr, kn, krt)
    lse, ikf_y = lax.optimization_barrier((lse, ikf_y))
    lse = merged(lse, ctx_xor(lse, 1))
    lse = merged(lse, ctx_xor(lse, 16))
    below, above = z_shift(lse, 1), z_shift(lse, -1)
    two, three = merged(lse, below), merged(lse, below, above)
    lse = merged(three, z_shift(three, 3), z_shift(two, -3))
    probs = run_probs(lse, qn, qr, kn, krt)
    probs, ikf, ikf_y = lax.optimization_barrier((probs, ikf, ikf_y))
    target = lax.all_to_all(probs.reshape(N_HEAD, -1, probs.shape[1]), "head", 0, 0)
    ikf_c, ikf_yc = ctx_xor(ikf, 1), ctx_xor(ikf_y, 1)
    target, ikf_c, ikf_yc = lax.optimization_barrier((target, ikf_c, ikf_yc))

    lg = run_lg(lse, logits, target)
    lg_y, lg_c = ctx_xor(lg, 16), ctx_xor(lg, 1)
    keep, send, gw = run_gk(lg, iq, ik, w)
    lg_y, lg_c, send, gw = lax.optimization_barrier((lg_y, lg_c, send, gw))
    lg_yc = ctx_xor(lg_y, 1)
    gws = [gw, *[ctx_xor(gw, bits) for bits in (16, 17, 1)]]
    got = head_xor(send, 2)
    parts = run_gq([lg, lg_c, lg_y, lg_yc], [ik, ikf_c, ikf_y, ikf_yc], iq, w, gws)
    got, parts = lax.optimization_barrier((got, parts))
    got = head_xor(keep[2:] + got[2:], 6) + (keep[:2] + got[:2])
    got, mine = head_xor(got[1], 1), got[0]
    groups = [[(y * N_Z + z) * 2 + c for z in range(N_Z)] for y in range(2) for c in range(2)]
    parts = lax.all_to_all(parts, "ctx", 0, 0, axis_index_groups=groups)
    return run_finish(parts, mine, got)


def solution(mesh):
    return jax.shard_map(
        per_device,
        mesh=mesh,
        in_specs=(
            P(None, "head"),
            P(None, "head"),
            P("ctx", "head"),
            P("ctx", None),
            P("head", None),
            P("ctx", None),
            P("head", None),
            P(),
            P("ctx"),
        ),
        out_specs=(P("head", "ctx"), P(("ctx", "head"), None), P("head", None)),
        check_vma=False,
    )
```

```python
import math

import jax
import jax.numpy as jnp
from jax import lax
from jax.experimental import pallas as pl
from jax.experimental.pallas import tpu as pltpu
from jax.sharding import PartitionSpec as P

HEADS = 128
NOPE = 128
ROPE = 64
IDX_HEADS = 64
IDX_DIM = 128
N_CTX = 32
N_HEAD = 8
N_Z = 8
LOG2E = math.log2(math.e)
SCORE_SCALE = LOG2E / math.sqrt(NOPE + ROPE)
INV_ROOT = 1.0 / math.sqrt(IDX_DIM)
NEG = -1e30
F32 = jnp.float32
BF16 = jnp.bfloat16
NT = (((1,), (1,)), ((), ()))
NN = (((1,), (0,)), ((), ()))
GROUP = 8


def dot(a, b, dims):
    return lax.dot_general(a, b, dims, preferred_element_type=F32)


def column(row, lanes=128):
    return jnp.broadcast_to(row, (lanes, row.shape[1])).T


def ctx_place():
    ctx = lax.axis_index("ctx")
    return ctx // (2 * N_Z), ctx // 2 % N_Z, ctx % 2


def fill_rope(krt_ref, krp):
    kr = krt_ref[...].T
    zero = jnp.zeros_like(kr)
    krp[0] = jnp.concatenate([kr, zero], axis=1)
    krp[1] = jnp.concatenate([zero, kr], axis=1)


def fill_weights(w_ref, wb):
    for j in range(IDX_HEADS):
        wb[j] = jnp.broadcast_to(w_ref[:, j : j + 1], wb.shape[1:])


def lanes_of(block, width):
    return jnp.concatenate([block] * (width // 128), axis=-1)


def stacked(block):
    count = block.shape[1] // 128
    return jnp.concatenate([block[:, i * 128 : (i + 1) * 128] for i in range(count)], axis=0)


def pair_operands(refs, krp, p):
    qn_ref, qr_ref, kn_ref = refs
    part = slice(p * 128, (p + 1) * 128)
    q = jnp.concatenate([qn_ref[:, part], qr_ref[...]], axis=1)
    return q, jnp.concatenate([kn_ref[:, part], krp[p]], axis=1)


def online_lse(s_ref, bias, cols, chunk=64):
    keys = bias.shape[0]
    top = jnp.full((8, 256), 2.0 * NEG, F32)
    total = jnp.zeros((8, 256), F32)
    for kc in range(keys // chunk):
        rows = slice(kc * chunk, (kc + 1) * chunk)
        s = (s_ref[rows, cols] + bias[rows, cols]).reshape(chunk // 8, 8, 256)
        new = jnp.maximum(top, jnp.max(s, axis=0))
        e = jnp.exp2((s - new[None]) * SCORE_SCALE)
        total = total * jnp.exp2((top - new) * SCORE_SCALE) + jnp.sum(e, axis=0)
        top = new
    best = jnp.max(top, axis=0, keepdims=True)
    total = jnp.sum(total * jnp.exp2((top - best) * SCORE_SCALE), axis=0, keepdims=True)
    return best * SCORE_SCALE + jnp.log2(total)


def front_kernel(
    base_ref, qpos_ref, krt_ref, ik_ref, w_ref, iq_ref, qn_ref, qr_ref, kn_ref, out_ref, logits_ref,
    bias, krp, s_ref, wp, qcol, si_ref, acc,
):
    step = pl.program_id(0)
    keys, queries = bias.shape
    rows = logits_ref.shape[0]

    @pl.when(step == 0)
    def _():
        key = lax.broadcasted_iota(jnp.int32, bias.shape, 0) + base_ref[0] * keys
        bias[...] = jnp.where(key <= qpos_ref[...], 0.0, NEG)
        fill_rope(krt_ref, krp)
        wt = w_ref[...].T
        for i in range(IDX_HEADS // 2):
            pair = [wt[2 * i : 2 * i + 1], wt[2 * i + 1 : 2 * i + 2]]
            wp[i : i + 1, :] = jnp.concatenate(pair, axis=1)
        acc[...] = jnp.zeros_like(acc)
        qcol[...] = column(qpos_ref[...])

    def scores(p):
        q, k = pair_operands((qn_ref, qr_ref, kn_ref), krp, p)
        s_ref[p] = dot(k, q, NT)

    def statistics(p):
        for qc in range(queries // 256):
            cols = slice(qc * 256, (qc + 1) * 256)
            out_ref[pl.ds(2 * step + p, 1), cols] = online_lse(s_ref.at[p], bias, cols)

    scores(0)
    si_ref[...] = dot(ik_ref[...], stacked(iq_ref[...]), NT)
    statistics(0)
    scores(1)
    weights = [wp[pl.ds(step * GROUP // 2 + i, 1), :] for i in range(GROUP // 2)]
    for r in range(keys // 64):
        at = slice(r * 64, (r + 1) * 64)
        total = acc[at, :]
        for i, weight in enumerate(weights):
            total = total + jnp.maximum(si_ref[at, i * 128 : (i + 1) * 128], 0.0) * weight
        acc[at, :] = total
    statistics(1)

    @pl.when(step == pl.num_programs(0) - 1)
    def _():
        turned = acc[...].T
        key = lax.broadcasted_iota(jnp.int32, (rows, keys), 1) + base_ref[0] * keys
        start = pl.multiple_of(lax.axis_index("head") * rows, rows)
        limit = lanes_of(qcol[pl.ds(start, rows), :], keys)
        logits = (turned[:rows] + turned[rows:]) * (INV_ROOT * LOG2E)
        logits = jnp.where(key <= limit, logits, NEG)
        logits_ref[...] = logits
        top = jnp.max(logits, axis=1, keepdims=True)
        total = jnp.sum(jnp.exp2(logits - top), axis=1, keepdims=True)
        lse = jnp.broadcast_to(top + jnp.log2(total), (rows, 128)).T
        row = [lse[:16, :rows], jnp.zeros((16, 128 - rows), F32)]
        out_ref[:, queries:] = jnp.concatenate(row, axis=1)


def probs_kernel(lse_ref, krt_ref, qn_ref, qr_ref, kn_ref, out_hbm, krp, s_ref, acc, sems):
    step = pl.program_id(0)
    last = pl.num_programs(0) - 1
    queries, keys = acc.shape
    size = queries // N_HEAD

    @pl.when(step == 0)
    def _():
        fill_rope(krt_ref, krp)
        acc[...] = jnp.zeros_like(acc)

    lse = []
    for p in range(2):
        s_ref[p] = dot(*pair_operands((qn_ref, qr_ref, kn_ref), krp, p), NT)
        lse.append(column(lse_ref[pl.ds(2 * step + p, 1), :queries]))
    for r in range(queries // 32):
        rows = slice(r * 32, (r + 1) * 32)
        total = acc[rows, :]
        for p in range(2):
            s = s_ref[p, rows, :] * SCORE_SCALE - lanes_of(lse[p][rows], keys)
            total = total + jnp.exp2(s)
        acc[rows, :] = total

    @pl.when(step == last)
    def _():
        copies = []
        for h in range(N_HEAD):
            rows = pl.ds(h * size, size)
            copies.append(pltpu.make_async_copy(acc.at[rows], out_hbm.at[rows], sems.at[h]))
        for copy in copies:
            copy.start()
        for copy in copies:
            copy.wait()


def lg_kernel(lse_ref, logits_ref, target_ref, lg_ref):
    rows, width = lg_ref.shape
    lse = column(lse_ref[:1, lse_ref.shape[1] - 128 :])[:rows]
    for c in range(width // 128):
        cols = slice(c * 128, (c + 1) * 128)
        target = target_ref[0, :, cols]
        for h in range(1, N_HEAD):
            target = target + target_ref[h, :, cols]
        logits = logits_ref[:, cols]
        lg = jnp.exp2(logits - lse) - target * (1.0 / HEADS)
        lg_ref[:, cols] = jnp.where(logits > 0.5 * NEG, lg, 0.0)


def gk_kernel(
    lg_ref, iq_ref, ik_ref, w_ref, keep_ref, send_ref, gw_out, wb, lgt_ref, m_ref, gk_ref, gwt_ref
):
    step = pl.program_id(0)
    rows, keys = lg_ref.shape
    width = GROUP * rows

    @pl.when(step == 0)
    def _():
        fill_weights(w_ref, wb)
        lgt_ref[...] = jnp.concatenate([lg_ref[...]] * (128 // rows), axis=0).T
        gk_ref[...] = jnp.zeros_like(gk_ref)

    q = stacked(iq_ref[...])
    w = jnp.concatenate([wb[step * GROUP + i] for i in range(GROUP)], axis=0)
    wq = (q.astype(F32) * w).astype(BF16)
    gw = jnp.zeros((8, width), F32)
    for c in range(2):
        inner = dot(ik_ref[c * 512 : (c + 1) * 512, :], q, NT)
        for r in range(16):
            at = slice(c * 512 + r * 32, c * 512 + (r + 1) * 32)
            part = inner[r * 32 : (r + 1) * 32]
            masked = jnp.where(part > 0.0, lanes_of(lgt_ref[at, :], width), 0.0)
            m_ref[at, :] = masked.astype(BF16)
            gw = gw + jnp.sum((part * masked).reshape(4, 8, width), axis=0)
        at = slice(c * 512, (c + 1) * 512)
        gk_ref[at, :] += dot(m_ref[at, :], wq, NN)
    gw = jnp.sum(gw, axis=0, keepdims=True) * INV_ROOT
    for i in range(GROUP):
        gwt_ref[pl.ds(step * GROUP + i, 1), :] = gw[:, i * rows : (i + 1) * rows]

    @pl.when(step == pl.num_programs(0) - 1)
    def _():
        me = lax.axis_index("head")
        size = keys // N_HEAD
        for out, slots in ((keep_ref, (0, 1, 6, 7)), (send_ref, (2, 3, 4, 5))):
            for n, m in enumerate(slots):
                start = pl.multiple_of((me ^ m) * size, size)
                out[n] = gk_ref[pl.ds(start, size), :] * INV_ROOT
        gw_out[...] = jnp.concatenate([gwt_ref[i * 16 : (i + 1) * 16] for i in range(4)], axis=1)


def gq_kernel(*refs):
    lgs, iks, (iq_ref, w_ref), gws = refs[:4], refs[4:8], refs[8:10], refs[10:14]
    gq_ref, wb, lg_ref, ikb_ref, q_ref, g_ref = refs[14:]
    source = pl.program_id(0)
    rows, keys = lgs[0].shape
    count = q_ref.shape[0] // rows
    y_lo, _, core = ctx_place()
    dests = [(y_lo * N_Z + i) * 2 + core for i in range(N_Z)]

    @pl.when(source == 0)
    def _():
        fill_weights(w_ref, wb)
        g_ref[...] = jnp.zeros_like(g_ref)
        for i in range(4):
            lg_ref[i] = lgs[i][...]
            ikb_ref[i] = iks[i][...].astype(BF16)
        for i in range(N_Z):
            block = iq_ref[:, pl.ds(pl.multiple_of(dests[i] * 256, 256), 256)]
            q_ref[2 * i * rows : 2 * (i + 1) * rows, :] = stacked(block)

    for c in range(4):
        cols = slice(c * 256, (c + 1) * 256)
        k = ikb_ref[source, cols, :]
        inner = dot(q_ref[...], k, NT)
        lg = jnp.concatenate([lg_ref[source, :, cols]] * count, axis=0)
        g_ref[...] += dot(jnp.where(inner > 0.0, lg, 0.0).astype(BF16), k, NN)

    @pl.when(source == 3)
    def _():
        gw = (gws[0][...] + gws[1][...]) + (gws[2][...] + gws[3][...])
        for i in range(N_Z):
            pair = []
            for n in range(2):
                at = (2 * i + n) * rows
                pair.append(g_ref[at : at + rows, :] * wb[dests[i] * 2 + n] * INV_ROOT)
            gq_ref[i, :rows, :] = jnp.concatenate(pair, axis=1)
            gq_ref[i, rows:, :] = gw


def finish_kernel(parts_ref, mine_ref, got_ref, gq_ref, gk_ref, gw_ref):
    total = parts_ref[0]
    for i in range(1, N_Z):
        total = total + parts_ref[i]
    gq_ref[...] = total[:64]
    gk_ref[...] = mine_ref[...] + got_ref[...]
    gwt = jnp.concatenate([total[64:, i * 64 : (i + 1) * 64] for i in range(4)], axis=0)
    gw_ref[...] = gwt.T


def smem():
    return pl.BlockSpec(memory_space=pltpu.SMEM)


def whole(shape):
    return pl.BlockSpec(shape, lambda *_: (0,) * len(shape))


def wholes(arrays):
    return [whole(x.shape) for x in arrays]


def floats(*shapes):
    return [jax.ShapeDtypeStruct(s, F32) for s in shapes]


def in_vmem():
    return pl.BlockSpec(memory_space=pltpu.VMEM)


def call(kernel, name, grid, ins, in_specs, out_shapes, out_specs, scratch, vmem=56):
    return pl.pallas_call(
        kernel,
        grid=grid,
        in_specs=in_specs,
        out_specs=out_specs,
        out_shape=out_shapes,
        scratch_shapes=scratch,
        compiler_params=pltpu.CompilerParams(vmem_limit_bytes=vmem * 1024 * 1024),
        name=name,
    )(*ins)


def main_specs(queries, keys):
    return [
        pl.BlockSpec((queries, 256), lambda i: (0, i)),
        pl.BlockSpec((queries, 128), lambda i: (0, i)),
        pl.BlockSpec((keys, 256), lambda i: (0, i)),
    ]


def run_front(key_blocks, qpos, krt, ik, w, iq, qn, qr, kn):
    queries, keys, pairs = qn.shape[0], kn.shape[0], qn.shape[1] // 256
    rows = iq.shape[0]
    shapes = [(2 * pairs, queries + 128), (rows, keys)]
    return call(
        front_kernel,
        "front",
        (pairs,),
        (key_blocks, qpos, krt, ik, w, iq, qn, qr, kn),
        [
            smem(),
            *wholes([qpos, krt, ik, w]),
            pl.BlockSpec((rows, GROUP * 128), lambda i: (0, i)),
            *main_specs(queries, keys),
        ],
        floats(*shapes),
        [whole(s) for s in shapes],
        [
            pltpu.VMEM((keys, queries), F32),
            pltpu.VMEM((2, keys, 128), BF16),
            pltpu.VMEM((2, keys, queries), F32),
            pltpu.VMEM((IDX_HEADS // 2, 128), F32),
            pltpu.VMEM((queries, 128), jnp.int32),
            pltpu.VMEM((keys, GROUP * rows), F32),
            pltpu.VMEM((keys, 128), F32),
        ],
    )


def run_probs(lse, qn, qr, kn, krt):
    queries, keys, pairs = qn.shape[0], kn.shape[0], qn.shape[1] // 256
    return call(
        probs_kernel,
        "main_probs",
        (pairs,),
        (lse, krt, qn, qr, kn),
        [*wholes([lse, krt]), *main_specs(queries, keys)],
        floats((queries, keys)),
        [pl.BlockSpec(memory_space=pltpu.HBM)],
        [
            pltpu.VMEM((2, keys, 128), BF16),
            pltpu.VMEM((2, queries, keys), F32),
            pltpu.VMEM((queries, keys), F32),
            pltpu.SemaphoreType.DMA((N_HEAD,)),
        ],
        24,
    )[0]


def run_lg(lse, logits, target):
    return pl.pallas_call(
        lg_kernel,
        in_specs=[in_vmem()] * 3,
        out_specs=in_vmem(),
        out_shape=floats(logits.shape)[0],
        compiler_params=pltpu.CompilerParams(vmem_limit_bytes=8 * 1024 * 1024),
        name="logit_grad",
    )(lse, logits, target)


def run_gk(lg, iq, ik, w):
    rows, keys = lg.shape
    size = keys // N_HEAD
    shapes = [(4, size, IDX_DIM), (4, size, IDX_DIM), (16, 256)]
    return call(
        gk_kernel,
        "grad_k",
        (IDX_HEADS // GROUP,),
        (lg, iq, ik, w),
        [
            whole(lg.shape),
            pl.BlockSpec((rows, GROUP * 128), lambda i: (0, i)),
            *wholes([ik, w]),
        ],
        floats(*shapes),
        [whole(s) for s in shapes],
        [
            pltpu.VMEM((IDX_HEADS, rows, 128), F32),
            pltpu.VMEM((keys, 128), F32),
            pltpu.VMEM((keys, GROUP * rows), BF16),
            pltpu.VMEM((keys, IDX_DIM), F32),
            pltpu.VMEM((IDX_HEADS, rows), F32),
        ],
        20,
    )


def run_gq(lgs, iks, iq, w, gws):
    rows, keys = lgs[0].shape
    shape = (N_Z, rows + 16, 256)
    ins = [*lgs, *iks, iq, w, *gws]
    return call(
        gq_kernel,
        "grad_q",
        (4,),
        ins,
        wholes(ins),
        floats(shape),
        [whole(shape)],
        [
            pltpu.VMEM((IDX_HEADS, rows, 128), F32),
            pltpu.VMEM((4, rows, keys), F32),
            pltpu.VMEM((4, keys, IDX_DIM), BF16),
            pltpu.VMEM((2 * N_Z * rows, IDX_DIM), BF16),
            pltpu.VMEM((2 * N_Z * rows, IDX_DIM), F32),
        ],
        28,
    )[0]


def run_finish(*ins):
    shapes = [(64, 256), (128, 128), (64, 64)]
    return pl.pallas_call(
        finish_kernel,
        in_specs=[in_vmem()] * 3,
        out_specs=[in_vmem()] * 3,
        out_shape=floats(*shapes),
        compiler_params=pltpu.CompilerParams(vmem_limit_bytes=8 * 1024 * 1024),
        name="finish",
    )(*ins)


def head_xor(value, bits):
    return lax.ppermute(value, "head", [(i, i ^ bits) for i in range(N_HEAD)])


def ctx_xor(value, bits):
    return lax.ppermute(value, "ctx", [(i, i ^ bits) for i in range(N_CTX)])


def z_shift(value, by):
    to = [i // 16 * 16 + (i // 2 + by) % N_Z * 2 + i % 2 for i in range(N_CTX)]
    return lax.ppermute(value, "ctx", list(enumerate(to)))


def merged(*values):
    top = values[0]
    for value in values[1:]:
        top = jnp.maximum(top, value)
    total = sum(jnp.exp2(value - top) for value in values)
    return top + jnp.log2(total)


def over_z(lse):
    below, above = z_shift(lse, 1), z_shift(lse, -1)
    two, three = merged(lse, below), merged(lse, below, above)
    return merged(three, z_shift(three, 3), z_shift(two, -3))


def per_device(qn, qr, kn, kr, iq, ik, w, query_pos, key_blocks):
    qpos = query_pos[None, :]
    krt = kr.T
    lse, logits = run_front(key_blocks, qpos, krt, ik, w, iq, qn, qr, kn)
    lse = merged(lse, ctx_xor(lse, 1))
    lse = merged(lse, ctx_xor(lse, 16))
    lse, ik_later = lax.optimization_barrier((lse, ik))
    ikf = ik_later.astype(F32)
    ikf_y, ikf_c = ctx_xor(ikf, 16), ctx_xor(ikf, 1)
    lse, ikf_y, ikf_c = lax.optimization_barrier((over_z(lse), ikf_y, ikf_c))
    probs = run_probs(lse, qn, qr, kn, krt)
    probs, ikf_y = lax.optimization_barrier((probs, ikf_y))
    target = lax.all_to_all(probs.reshape(N_HEAD, -1, probs.shape[1]), "head", 0, 0)
    ikf_yc = ctx_xor(ikf_y, 1)
    target, ikf_yc = lax.optimization_barrier((target, ikf_yc))

    lg = run_lg(lse, logits, target)
    lg_y, lg_c = ctx_xor(lg, 16), ctx_xor(lg, 1)
    keep, send, gw = run_gk(lg, iq, ik, w)
    lg_y, lg_c, send, gw = lax.optimization_barrier((lg_y, lg_c, send, gw))
    lg_yc = ctx_xor(lg_y, 1)
    gws = [gw, *[ctx_xor(gw, bits) for bits in (16, 17, 1)]]
    got = head_xor(send, 2)
    parts = run_gq([lg, lg_c, lg_y, lg_yc], [ik, ikf_c, ikf_y, ikf_yc], iq, w, gws)
    got, parts = lax.optimization_barrier((got, parts))
    got = head_xor(keep[2:] + got[2:], 6) + (keep[:2] + got[:2])
    got, mine = head_xor(got[1], 1), got[0]
    groups = [[(y * N_Z + z) * 2 + c for z in range(N_Z)] for y in range(2) for c in range(2)]
    parts = lax.all_to_all(parts, "ctx", 0, 0, axis_index_groups=groups)
    return run_finish(parts, mine, got)


def solution(mesh):
    return jax.shard_map(
        per_device,
        mesh=mesh,
        in_specs=(
            P(None, "head"),
            P(None, "head"),
            P("ctx", "head"),
            P("ctx", None),
            P("head", None),
            P("ctx", None),
            P("head", None),
            P(),
            P("ctx"),
        ),
        out_specs=(P("head", "ctx"), P(("ctx", "head"), None), P("head", None)),
        check_vma=False,
    )
```

```python
import math

import jax
import jax.numpy as jnp
from jax import lax
from jax.experimental import pallas as pl
from jax.experimental.pallas import tpu as pltpu
from jax.sharding import PartitionSpec as P

HEADS = 128
NOPE = 128
ROPE = 64
IDX_HEADS = 64
IDX_DIM = 128
N_CTX = 32
N_HEAD = 8
N_Z = 8
LOG2E = math.log2(math.e)
SCORE_SCALE = LOG2E / math.sqrt(NOPE + ROPE)
INV_ROOT = 1.0 / math.sqrt(IDX_DIM)
NEG = -1e30
F32 = jnp.float32
BF16 = jnp.bfloat16
NT = (((1,), (1,)), ((), ()))
NN = (((1,), (0,)), ((), ()))
GROUP = 8


def dot(a, b, dims):
    return lax.dot_general(a, b, dims, preferred_element_type=F32)


def column(row, lanes=128):
    return jnp.broadcast_to(row, (lanes, row.shape[1])).T


def ctx_place():
    ctx = lax.axis_index("ctx")
    return ctx // (2 * N_Z), ctx // 2 % N_Z, ctx % 2


def fill_rope(krt_ref, krp):
    kr = krt_ref[...].T
    zero = jnp.zeros_like(kr)
    krp[0] = jnp.concatenate([kr, zero], axis=1)
    krp[1] = jnp.concatenate([zero, kr], axis=1)


def fill_weights(w_ref, wb):
    for j in range(IDX_HEADS):
        wb[j] = jnp.broadcast_to(w_ref[:, j : j + 1], wb.shape[1:])


def lanes_of(block, width):
    return jnp.concatenate([block] * (width // 128), axis=-1)


def stacked(block):
    count = block.shape[1] // 128
    return jnp.concatenate([block[:, i * 128 : (i + 1) * 128] for i in range(count)], axis=0)


def pair_operands(refs, krp, p):
    qn_ref, qr_ref, kn_ref = refs
    part = slice(p * 128, (p + 1) * 128)
    q = jnp.concatenate([qn_ref[:, part], qr_ref[...]], axis=1)
    return q, jnp.concatenate([kn_ref[:, part], krp[p]], axis=1)


def online_lse(s_ref, bias, cols, chunk=64):
    keys = bias.shape[0]
    top = jnp.full((8, 256), 2.0 * NEG, F32)
    total = jnp.zeros((8, 256), F32)
    for kc in range(keys // chunk):
        rows = slice(kc * chunk, (kc + 1) * chunk)
        s = (s_ref[rows, cols] + bias[rows, cols]).reshape(chunk // 8, 8, 256)
        new = jnp.maximum(top, jnp.max(s, axis=0))
        e = jnp.exp2((s - new[None]) * SCORE_SCALE)
        total = total * jnp.exp2((top - new) * SCORE_SCALE) + jnp.sum(e, axis=0)
        top = new
    best = jnp.max(top, axis=0, keepdims=True)
    total = jnp.sum(total * jnp.exp2((top - best) * SCORE_SCALE), axis=0, keepdims=True)
    return best * SCORE_SCALE + jnp.log2(total)


def front_kernel(
    base_ref, qpos_ref, krt_ref, ik_ref, w_ref, iq_ref, qn_ref, qr_ref, kn_ref, out_ref, logits_ref,
    bias, krp, s_ref, wp, qcol, si_ref, acc,
):
    step = pl.program_id(0)
    keys, queries = bias.shape
    rows = logits_ref.shape[0]

    @pl.when(step == 0)
    def _():
        key = lax.broadcasted_iota(jnp.int32, bias.shape, 0) + base_ref[0] * keys
        bias[...] = jnp.where(key <= qpos_ref[...], 0.0, NEG)
        fill_rope(krt_ref, krp)
        wt = w_ref[...].T
        for i in range(IDX_HEADS // 2):
            pair = [wt[2 * i : 2 * i + 1], wt[2 * i + 1 : 2 * i + 2]]
            wp[i : i + 1, :] = jnp.concatenate(pair, axis=1)
        acc[...] = jnp.zeros_like(acc)
        qcol[...] = column(qpos_ref[...])

    def scores(p):
        q, k = pair_operands((qn_ref, qr_ref, kn_ref), krp, p)
        s_ref[p] = dot(k, q, NT)

    def statistics(p):
        for qc in range(queries // 256):
            cols = slice(qc * 256, (qc + 1) * 256)
            out_ref[pl.ds(2 * step + p, 1), cols] = online_lse(s_ref.at[p], bias, cols)

    scores(0)
    si_ref[...] = dot(ik_ref[...], stacked(iq_ref[...]), NT)
    statistics(0)
    scores(1)
    weights = [wp[pl.ds(step * GROUP // 2 + i, 1), :] for i in range(GROUP // 2)]
    for r in range(keys // 64):
        at = slice(r * 64, (r + 1) * 64)
        total = acc[at, :]
        for i, weight in enumerate(weights):
            total = total + jnp.maximum(si_ref[at, i * 128 : (i + 1) * 128], 0.0) * weight
        acc[at, :] = total
    statistics(1)

    @pl.when(step == pl.num_programs(0) - 1)
    def _():
        turned = acc[...].T
        key = lax.broadcasted_iota(jnp.int32, (rows, keys), 1) + base_ref[0] * keys
        start = pl.multiple_of(lax.axis_index("head") * rows, rows)
        limit = lanes_of(qcol[pl.ds(start, rows), :], keys)
        logits = (turned[:rows] + turned[rows:]) * (INV_ROOT * LOG2E)
        logits = jnp.where(key <= limit, logits, NEG)
        logits_ref[...] = logits
        top = jnp.max(logits, axis=1, keepdims=True)
        total = jnp.sum(jnp.exp2(logits - top), axis=1, keepdims=True)
        lse = jnp.broadcast_to(top + jnp.log2(total), (rows, 128)).T
        row = [lse[:16, :rows], jnp.zeros((16, 128 - rows), F32)]
        out_ref[:, queries:] = jnp.concatenate(row, axis=1)


def probs_kernel(
    lse_ref, logits_hbm, krt_ref, qn_ref, qr_ref, kn_ref, out_hbm, index_ref,
    krp, s_ref, acc, logits_ref, sems,
):
    step = pl.program_id(0)
    last = pl.num_programs(0) - 1
    queries, keys = acc.shape
    size = queries // N_HEAD

    @pl.when(step == 0)
    def _():
        fill_rope(krt_ref, krp)
        acc[...] = jnp.zeros_like(acc)
        pltpu.make_async_copy(logits_hbm, logits_ref, sems.at[N_HEAD]).start()

    lse = []
    for p in range(2):
        s_ref[p] = dot(*pair_operands((qn_ref, qr_ref, kn_ref), krp, p), NT)
        lse.append(column(lse_ref[pl.ds(2 * step + p, 1), :queries]))
    for r in range(queries // 32):
        rows = slice(r * 32, (r + 1) * 32)
        total = acc[rows, :]
        for p in range(2):
            s = s_ref[p, rows, :] * SCORE_SCALE - lanes_of(lse[p][rows], keys)
            total = total + jnp.exp2(s)
        acc[rows, :] = total

    @pl.when(step == last)
    def _():
        copies = []
        for h in range(N_HEAD):
            rows = pl.ds(h * size, size)
            copies.append(pltpu.make_async_copy(acc.at[rows], out_hbm.at[rows], sems.at[h]))
        for copy in copies:
            copy.start()
        pltpu.make_async_copy(logits_hbm, logits_ref, sems.at[N_HEAD]).wait()
        logits = logits_ref[...]
        top = lanes_of(column(lse_ref[:1, queries:])[:size], keys)
        index_ref[...] = jnp.where(logits > 0.5 * NEG, jnp.exp2(logits - top), -1.0)
        for copy in copies:
            copy.wait()


def lg_kernel(index_ref, target_ref, lg_ref):
    for c in range(lg_ref.shape[1] // 128):
        cols = slice(c * 128, (c + 1) * 128)
        target = target_ref[0, :, cols]
        for h in range(1, N_HEAD):
            target = target + target_ref[h, :, cols]
        prob = index_ref[:, cols]
        lg_ref[:, cols] = jnp.where(prob >= 0.0, prob - target * (1.0 / HEADS), 0.0)


def gk_kernel(
    lg_ref, iq_ref, ik_ref, w_ref, keep_ref, send_ref, gw_out, wb, lgt_ref, m_ref, gk_ref, gwt_ref
):
    step = pl.program_id(0)
    rows, keys = lg_ref.shape
    width = GROUP * rows

    @pl.when(step == 0)
    def _():
        fill_weights(w_ref, wb)
        lgt_ref[...] = jnp.concatenate([lg_ref[...]] * (128 // rows), axis=0).T
        gk_ref[...] = jnp.zeros_like(gk_ref)

    q = stacked(iq_ref[...])
    w = jnp.concatenate([wb[step * GROUP + i] for i in range(GROUP)], axis=0)
    wq = (q.astype(F32) * w).astype(BF16)
    gw = jnp.zeros((8, width), F32)
    for c in range(2):
        inner = dot(ik_ref[c * 512 : (c + 1) * 512, :], q, NT)
        for r in range(16):
            at = slice(c * 512 + r * 32, c * 512 + (r + 1) * 32)
            part = inner[r * 32 : (r + 1) * 32]
            masked = jnp.where(part > 0.0, lanes_of(lgt_ref[at, :], width), 0.0)
            m_ref[at, :] = masked.astype(BF16)
            gw = gw + jnp.sum((part * masked).reshape(4, 8, width), axis=0)
        at = slice(c * 512, (c + 1) * 512)
        gk_ref[at, :] += dot(m_ref[at, :], wq, NN)
    gw = jnp.sum(gw, axis=0, keepdims=True) * INV_ROOT
    for i in range(GROUP):
        gwt_ref[pl.ds(step * GROUP + i, 1), :] = gw[:, i * rows : (i + 1) * rows]

    @pl.when(step == pl.num_programs(0) - 1)
    def _():
        me = lax.axis_index("head")
        size = keys // N_HEAD
        for out, slots in ((keep_ref, (0, 1, 6, 7)), (send_ref, (2, 3, 4, 5))):
            for n, m in enumerate(slots):
                start = pl.multiple_of((me ^ m) * size, size)
                out[n] = gk_ref[pl.ds(start, size), :] * INV_ROOT
        gw_out[...] = jnp.concatenate([gwt_ref[i * 16 : (i + 1) * 16] for i in range(4)], axis=1)


def gq_kernel(*refs):
    lgs, iks, (iq_ref, w_ref) = refs[:4], refs[4:8], refs[8:10]
    gq_ref, wt, lg_ref, ikb_ref, q_ref, g_ref = refs[10:]
    source = pl.program_id(0)
    rows, keys = lgs[0].shape
    count = q_ref.shape[0] // rows
    y_lo, _, core = ctx_place()
    dests = [(y_lo * N_Z + i) * 2 + core for i in range(N_Z)]

    @pl.when(source == 0)
    def _():
        wt[...] = w_ref[...].T * INV_ROOT
        g_ref[...] = jnp.zeros_like(g_ref)
        for i in range(4):
            lg_ref[i] = lgs[i][...]
            ikb_ref[i] = iks[i][...].astype(BF16)
        for i in range(N_Z):
            block = iq_ref[:, pl.ds(pl.multiple_of(dests[i] * 256, 256), 256)]
            q_ref[2 * i * rows : 2 * (i + 1) * rows, :] = stacked(block)

    for c in range(4):
        cols = slice(c * 256, (c + 1) * 256)
        k = ikb_ref[source, cols, :]
        inner = dot(q_ref[...], k, NT)
        lg = jnp.concatenate([lg_ref[source, :, cols]] * count, axis=0)
        g_ref[...] += dot(jnp.where(inner > 0.0, lg, 0.0).astype(BF16), k, NN)

    @pl.when(source == 3)
    def _():
        for i in range(N_Z):
            pair = []
            for n in range(2):
                at = (2 * i + n) * rows
                weight = column(wt[pl.ds(dests[i] * 2 + n, 1), :])
                pair.append(g_ref[at : at + rows, :] * weight)
            gq_ref[i, :rows, :] = jnp.concatenate(pair, axis=1)


def gw_rows_kernel(gw0, gw1, gw2, gw3, gq_ref, out_ref):
    gw = (gw0[...] + gw1[...]) + (gw2[...] + gw3[...])
    for i in range(N_Z):
        out_ref[i] = gw


def finish_kernel(parts_ref, mine_ref, got_ref, gq_ref, gk_ref, gw_ref):
    total = parts_ref[0]
    for i in range(1, N_Z):
        total = total + parts_ref[i]
    gq_ref[...] = total[:64]
    gk_ref[...] = mine_ref[...] + got_ref[...]
    gwt = jnp.concatenate([total[64:, i * 64 : (i + 1) * 64] for i in range(4)], axis=0)
    gw_ref[...] = gwt.T


def smem():
    return pl.BlockSpec(memory_space=pltpu.SMEM)


def whole(shape):
    return pl.BlockSpec(shape, lambda *_: (0,) * len(shape))


def wholes(arrays):
    return [whole(x.shape) for x in arrays]


def floats(*shapes):
    return [jax.ShapeDtypeStruct(s, F32) for s in shapes]


def in_vmem():
    return pl.BlockSpec(memory_space=pltpu.VMEM)


def call(kernel, name, grid, ins, in_specs, out_shapes, out_specs, scratch, vmem=56):
    return pl.pallas_call(
        kernel,
        grid=grid,
        in_specs=in_specs,
        out_specs=out_specs,
        out_shape=out_shapes,
        scratch_shapes=scratch,
        compiler_params=pltpu.CompilerParams(vmem_limit_bytes=vmem * 1024 * 1024),
        name=name,
    )(*ins)


def main_specs(queries, keys):
    return [
        pl.BlockSpec((queries, 256), lambda i: (0, i)),
        pl.BlockSpec((queries, 128), lambda i: (0, i)),
        pl.BlockSpec((keys, 256), lambda i: (0, i)),
    ]


def run_front(key_blocks, qpos, krt, ik, w, iq, qn, qr, kn):
    queries, keys, pairs = qn.shape[0], kn.shape[0], qn.shape[1] // 256
    rows = iq.shape[0]
    shapes = [(2 * pairs, queries + 128), (rows, keys)]
    return call(
        front_kernel,
        "front",
        (pairs,),
        (key_blocks, qpos, krt, ik, w, iq, qn, qr, kn),
        [
            smem(),
            *wholes([qpos, krt, ik, w]),
            pl.BlockSpec((rows, GROUP * 128), lambda i: (0, i)),
            *main_specs(queries, keys),
        ],
        floats(*shapes),
        [whole(s) for s in shapes],
        [
            pltpu.VMEM((keys, queries), F32),
            pltpu.VMEM((2, keys, 128), BF16),
            pltpu.VMEM((2, keys, queries), F32),
            pltpu.VMEM((IDX_HEADS // 2, 128), F32),
            pltpu.VMEM((queries, 128), jnp.int32),
            pltpu.VMEM((keys, GROUP * rows), F32),
            pltpu.VMEM((keys, 128), F32),
        ],
    )


def run_probs(lse, logits, qn, qr, kn, krt):
    queries, keys, pairs = qn.shape[0], kn.shape[0], qn.shape[1] // 256
    return call(
        probs_kernel,
        "main_probs",
        (pairs,),
        (lse, logits, krt, qn, qr, kn),
        [
            whole(lse.shape),
            pl.BlockSpec(memory_space=pltpu.HBM),
            whole(krt.shape),
            *main_specs(queries, keys),
        ],
        floats((queries, keys), logits.shape),
        [pl.BlockSpec(memory_space=pltpu.HBM), whole(logits.shape)],
        [
            pltpu.VMEM((2, keys, 128), BF16),
            pltpu.VMEM((2, queries, keys), F32),
            pltpu.VMEM((queries, keys), F32),
            pltpu.VMEM(logits.shape, F32),
            pltpu.SemaphoreType.DMA((N_HEAD + 1,)),
        ],
        24,
    )


def run_lg(index_probs, target):
    return pl.pallas_call(
        lg_kernel,
        in_specs=[in_vmem()] * 2,
        out_specs=in_vmem(),
        out_shape=floats(index_probs.shape)[0],
        compiler_params=pltpu.CompilerParams(vmem_limit_bytes=8 * 1024 * 1024),
        name="logit_grad",
    )(index_probs, target)


def run_gk(lg, iq, ik, w):
    rows, keys = lg.shape
    size = keys // N_HEAD
    shapes = [(4, size, IDX_DIM), (4, size, IDX_DIM), (16, 256)]
    return call(
        gk_kernel,
        "grad_k",
        (IDX_HEADS // GROUP,),
        (lg, iq, ik, w),
        [
            whole(lg.shape),
            pl.BlockSpec((rows, GROUP * 128), lambda i: (0, i)),
            *wholes([ik, w]),
        ],
        floats(*shapes),
        [whole(s) for s in shapes],
        [
            pltpu.VMEM((IDX_HEADS, rows, 128), F32),
            pltpu.VMEM((keys, 128), F32),
            pltpu.VMEM((keys, GROUP * rows), BF16),
            pltpu.VMEM((keys, IDX_DIM), F32),
            pltpu.VMEM((IDX_HEADS, rows), F32),
        ],
        20,
    )


def run_gq(lgs, iks, iq, w):
    rows, keys = lgs[0].shape
    shape = (N_Z, rows + 16, 256)
    ins = [*lgs, *iks, iq, w]
    return call(
        gq_kernel,
        "grad_q",
        (4,),
        ins,
        wholes(ins),
        floats(shape),
        [whole(shape)],
        [
            pltpu.VMEM(w.shape, F32),
            pltpu.VMEM((4, rows, keys), F32),
            pltpu.VMEM((4, keys, IDX_DIM), BF16),
            pltpu.VMEM((2 * N_Z * rows, IDX_DIM), BF16),
            pltpu.VMEM((2 * N_Z * rows, IDX_DIM), F32),
        ],
        28,
    )[0]


def run_gw_rows(parts, gws):
    rows = gws[0].shape[0]
    return pl.pallas_call(
        gw_rows_kernel,
        grid=(1,),
        in_specs=[*wholes(gws), pl.BlockSpec(memory_space=pl.ANY)],
        out_specs=pl.BlockSpec((N_Z, rows, 256), lambda i: (0, 64 // rows, 0)),
        out_shape=floats(parts.shape)[0],
        input_output_aliases={4: 0},
        compiler_params=pltpu.CompilerParams(vmem_limit_bytes=8 * 1024 * 1024),
        name="grad_w_rows",
    )(*gws, parts)


def run_finish(*ins):
    shapes = [(64, 256), (128, 128), (64, 64)]
    return pl.pallas_call(
        finish_kernel,
        in_specs=[in_vmem()] * 3,
        out_specs=[in_vmem()] * 3,
        out_shape=floats(*shapes),
        compiler_params=pltpu.CompilerParams(vmem_limit_bytes=8 * 1024 * 1024),
        name="finish",
    )(*ins)


def head_xor(value, bits):
    return lax.ppermute(value, "head", [(i, i ^ bits) for i in range(N_HEAD)])


def ctx_xor(value, bits):
    return lax.ppermute(value, "ctx", [(i, i ^ bits) for i in range(N_CTX)])


def z_shift(value, by):
    to = [i // 16 * 16 + (i // 2 + by) % N_Z * 2 + i % 2 for i in range(N_CTX)]
    return lax.ppermute(value, "ctx", list(enumerate(to)))


def merged(*values):
    top = values[0]
    for value in values[1:]:
        top = jnp.maximum(top, value)
    total = sum(jnp.exp2(value - top) for value in values)
    return top + jnp.log2(total)


def over_z(lse):
    below, above = z_shift(lse, 1), z_shift(lse, -1)
    two, three = merged(lse, below), merged(lse, below, above)
    return merged(three, z_shift(three, 3), z_shift(two, -3))


def per_device(qn, qr, kn, kr, iq, ik, w, query_pos, key_blocks):
    qpos = query_pos[None, :]
    krt = kr.T
    lse, logits = run_front(key_blocks, qpos, krt, ik, w, iq, qn, qr, kn)
    lse = merged(lse, ctx_xor(lse, 1))
    lse = merged(lse, ctx_xor(lse, 16))
    lse, ik_later = lax.optimization_barrier((lse, ik))
    ikf = ik_later.astype(F32)
    ikf_y, ikf_c = ctx_xor(ikf, 16), ctx_xor(ikf, 1)
    lse, ikf_c = lax.optimization_barrier((over_z(lse), ikf_c))
    probs, index_probs = run_probs(lse, logits, qn, qr, kn, krt)
    probs, ikf_y = lax.optimization_barrier((probs, ikf_y))
    target = lax.all_to_all(probs.reshape(N_HEAD, -1, probs.shape[1]), "head", 0, 0)
    ikf_yc = ctx_xor(ikf_y, 1)
    target, ikf_yc = lax.optimization_barrier((target, ikf_yc))

    lg = run_lg(index_probs, target)
    lg_y, lg_c = ctx_xor(lg, 16), ctx_xor(lg, 1)
    keep, send, gw = run_gk(lg, iq, ik, w)
    lg_y, lg_c, send, gw = lax.optimization_barrier((lg_y, lg_c, send, gw))
    lg_yc = ctx_xor(lg_y, 1)
    gws = [gw, *[ctx_xor(gw, bits) for bits in (16, 17, 1)]]
    got = head_xor(send, 2)
    parts = run_gq([lg, lg_c, lg_y, lg_yc], [ik, ikf_c, ikf_y, ikf_yc], iq, w)
    parts = run_gw_rows(parts, gws)
    got, parts = lax.optimization_barrier((got, parts))
    got = head_xor(keep[2:] + got[2:], 6) + (keep[:2] + got[:2])
    got, mine = head_xor(got[1], 1), got[0]
    groups = [[(y * N_Z + z) * 2 + c for z in range(N_Z)] for y in range(2) for c in range(2)]
    parts = lax.all_to_all(parts, "ctx", 0, 0, axis_index_groups=groups)
    return run_finish(parts, mine, got)


def solution(mesh):
    return jax.shard_map(
        per_device,
        mesh=mesh,
        in_specs=(
            P(None, "head"),
            P(None, "head"),
            P("ctx", "head"),
            P("ctx", None),
            P("head", None),
            P("ctx", None),
            P("head", None),
            P(),
            P("ctx"),
        ),
        out_specs=(P("head", "ctx"), P(("ctx", "head"), None), P("head", None)),
        check_vma=False,
    )
```

```python
import math

import jax
import jax.numpy as jnp
from jax import lax
from jax.experimental import pallas as pl
from jax.experimental.pallas import tpu as pltpu
from jax.sharding import PartitionSpec as P

HEADS = 128
NOPE = 128
ROPE = 64
IDX_HEADS = 64
IDX_DIM = 128
N_CTX = 32
N_HEAD = 8
N_Z = 8
LOG2E = math.log2(math.e)
SCORE_SCALE = LOG2E / math.sqrt(NOPE + ROPE)
INV_ROOT = 1.0 / math.sqrt(IDX_DIM)
NEG = -1e30
F32 = jnp.float32
BF16 = jnp.bfloat16
NT = (((1,), (1,)), ((), ()))
NN = (((1,), (0,)), ((), ()))
GROUP = 8


def dot(a, b, dims):
    return lax.dot_general(a, b, dims, preferred_element_type=F32)


def column(row, lanes=128):
    return jnp.broadcast_to(row, (lanes, row.shape[1])).T


def ctx_place():
    ctx = lax.axis_index("ctx")
    return ctx // (2 * N_Z), ctx // 2 % N_Z, ctx % 2


def fill_rope(krt_ref, krp):
    kr = krt_ref[...].T
    zero = jnp.zeros_like(kr)
    krp[0] = jnp.concatenate([kr, zero], axis=1)
    krp[1] = jnp.concatenate([zero, kr], axis=1)


def fill_weights(w_ref, wb):
    for j in range(IDX_HEADS):
        wb[j] = jnp.broadcast_to(w_ref[:, j : j + 1], wb.shape[1:])


def lanes_of(block, width):
    return jnp.concatenate([block] * (width // 128), axis=-1)


def stacked(block):
    count = block.shape[1] // 128
    return jnp.concatenate([block[:, i * 128 : (i + 1) * 128] for i in range(count)], axis=0)


def pair_operands(refs, krp, p):
    qn_ref, qr_ref, kn_ref = refs
    part = slice(p * 128, (p + 1) * 128)
    q = jnp.concatenate([qn_ref[:, part], qr_ref[...]], axis=1)
    return q, jnp.concatenate([kn_ref[:, part], krp[p]], axis=1)


def online_lse(s_ref, bias, cols, chunk=64):
    keys = bias.shape[0]
    top = jnp.full((8, 256), 2.0 * NEG, F32)
    total = jnp.zeros((8, 256), F32)
    for kc in range(keys // chunk):
        rows = slice(kc * chunk, (kc + 1) * chunk)
        s = (s_ref[rows, cols] + bias[rows, cols]).reshape(chunk // 8, 8, 256)
        new = jnp.maximum(top, jnp.max(s, axis=0))
        e = jnp.exp2((s - new[None]) * SCORE_SCALE)
        total = total * jnp.exp2((top - new) * SCORE_SCALE) + jnp.sum(e, axis=0)
        top = new
    best = jnp.max(top, axis=0, keepdims=True)
    total = jnp.sum(total * jnp.exp2((top - best) * SCORE_SCALE), axis=0, keepdims=True)
    return best * SCORE_SCALE + jnp.log2(total)


def front_kernel(
    base_ref, qpos_ref, krt_ref, ik_ref, w_ref, iq_ref, qn_ref, qr_ref, kn_ref, out_ref, logits_ref,
    bias, krp, s_ref, wp, qcol, si_ref, acc,
):
    step = pl.program_id(0)
    keys, queries = bias.shape
    rows = logits_ref.shape[0]

    @pl.when(step == 0)
    def _():
        key = lax.broadcasted_iota(jnp.int32, bias.shape, 0) + base_ref[0] * keys
        bias[...] = jnp.where(key <= qpos_ref[...], 0.0, NEG)
        fill_rope(krt_ref, krp)
        wt = w_ref[...].T
        for i in range(IDX_HEADS // 2):
            pair = [wt[2 * i : 2 * i + 1], wt[2 * i + 1 : 2 * i + 2]]
            wp[i : i + 1, :] = jnp.concatenate(pair, axis=1)
        acc[...] = jnp.zeros_like(acc)
        qcol[...] = column(qpos_ref[...])

    def scores(p):
        q, k = pair_operands((qn_ref, qr_ref, kn_ref), krp, p)
        s_ref[p] = dot(k, q, NT)

    def statistics(p):
        for qc in range(queries // 256):
            cols = slice(qc * 256, (qc + 1) * 256)
            out_ref[pl.ds(2 * step + p, 1), cols] = online_lse(s_ref.at[p], bias, cols)

    scores(0)
    si_ref[...] = dot(ik_ref[...], stacked(iq_ref[...]), NT)
    statistics(0)
    scores(1)
    weights = [wp[pl.ds(step * GROUP // 2 + i, 1), :] for i in range(GROUP // 2)]
    for r in range(keys // 64):
        at = slice(r * 64, (r + 1) * 64)
        total = acc[at, :]
        for i, weight in enumerate(weights):
            total = total + jnp.maximum(si_ref[at, i * 128 : (i + 1) * 128], 0.0) * weight
        acc[at, :] = total
    statistics(1)

    @pl.when(step == pl.num_programs(0) - 1)
    def _():
        turned = acc[...].T
        key = lax.broadcasted_iota(jnp.int32, (rows, keys), 1) + base_ref[0] * keys
        start = pl.multiple_of(lax.axis_index("head") * rows, rows)
        limit = lanes_of(qcol[pl.ds(start, rows), :], keys)
        logits = (turned[:rows] + turned[rows:]) * (INV_ROOT * LOG2E)
        logits = jnp.where(key <= limit, logits, NEG)
        logits_ref[...] = logits
        top = jnp.max(logits, axis=1, keepdims=True)
        total = jnp.sum(jnp.exp2(logits - top), axis=1, keepdims=True)
        lse = jnp.broadcast_to(top + jnp.log2(total), (rows, 128)).T
        row = [lse[:16, :rows], jnp.zeros((16, 128 - rows), F32)]
        out_ref[:, queries:] = jnp.concatenate(row, axis=1)


def probs_kernel(
    base_ref, qpos_ref, lse_ref, logits_ref, krt_ref, qn_ref, qr_ref, kn_ref, out_hbm,
    krp, s_ref, acc, sems,
):
    step = pl.program_id(0)
    last = pl.num_programs(0) - 1
    queries, keys = acc.shape
    size = queries // N_HEAD

    @pl.when(step == 0)
    def _():
        fill_rope(krt_ref, krp)
        acc[...] = jnp.zeros_like(acc)

    lse = []
    for p in range(2):
        s_ref[p] = dot(*pair_operands((qn_ref, qr_ref, kn_ref), krp, p), NT)
        lse.append(column(lse_ref[pl.ds(2 * step + p, 1), :queries]))
    for r in range(queries // 32):
        rows = slice(r * 32, (r + 1) * 32)
        total = acc[rows, :]
        for p in range(2):
            s = s_ref[p, rows, :] * SCORE_SCALE - lanes_of(lse[p][rows], keys)
            total = total + jnp.exp2(s)
        acc[rows, :] = total

    @pl.when(step == last)
    def _():
        limit = column(qpos_ref[...]) - base_ref[0] * keys
        key = lax.broadcasted_iota(jnp.int32, (size, keys), 1)
        for h in range(N_HEAD):
            rows = slice(h * size, (h + 1) * size)
            acc[rows, :] = jnp.where(key <= lanes_of(limit[rows], keys), acc[rows, :], 0.0)
        top = lanes_of(column(lse_ref[:1, queries:])[:size], keys)
        mine = pl.ds(pl.multiple_of(lax.axis_index("head") * size, size), size)
        acc[mine, :] -= jnp.exp2(logits_ref[...] - top) * HEADS
        copies = []
        for h in range(N_HEAD):
            rows = pl.ds(h * size, size)
            copies.append(pltpu.make_async_copy(acc.at[rows], out_hbm.at[rows], sems.at[h]))
        for copy in copies:
            copy.start()
        for copy in copies:
            copy.wait()


def lg_kernel(target_ref, lg_ref):
    for c in range(lg_ref.shape[1] // 128):
        cols = slice(c * 128, (c + 1) * 128)
        target = target_ref[0, :, cols]
        for h in range(1, N_HEAD):
            target = target + target_ref[h, :, cols]
        lg_ref[:, cols] = target * (-1.0 / HEADS)


def gk_kernel(
    lg_ref, iq_ref, ik_ref, w_ref, keep_ref, send_ref, gw_out, wb, lgt_ref, m_ref, gk_ref, gwt_ref
):
    step = pl.program_id(0)
    rows, keys = lg_ref.shape
    width = GROUP * rows

    @pl.when(step == 0)
    def _():
        fill_weights(w_ref, wb)
        lgt_ref[...] = jnp.concatenate([lg_ref[...]] * (128 // rows), axis=0).T
        gk_ref[...] = jnp.zeros_like(gk_ref)

    q = stacked(iq_ref[...])
    w = jnp.concatenate([wb[step * GROUP + i] for i in range(GROUP)], axis=0)
    wq = (q.astype(F32) * w).astype(BF16)
    gw = jnp.zeros((8, width), F32)
    for c in range(2):
        inner = dot(ik_ref[c * 512 : (c + 1) * 512, :], q, NT)
        for r in range(16):
            at = slice(c * 512 + r * 32, c * 512 + (r + 1) * 32)
            part = inner[r * 32 : (r + 1) * 32]
            masked = jnp.where(part > 0.0, lanes_of(lgt_ref[at, :], width), 0.0)
            m_ref[at, :] = masked.astype(BF16)
            gw = gw + jnp.sum((part * masked).reshape(4, 8, width), axis=0)
        at = slice(c * 512, (c + 1) * 512)
        gk_ref[at, :] += dot(m_ref[at, :], wq, NN)
    gw = jnp.sum(gw, axis=0, keepdims=True) * INV_ROOT
    for i in range(GROUP):
        gwt_ref[pl.ds(step * GROUP + i, 1), :] = gw[:, i * rows : (i + 1) * rows]

    @pl.when(step == pl.num_programs(0) - 1)
    def _():
        me = lax.axis_index("head")
        size = keys // N_HEAD
        for out, slots in ((keep_ref, (0, 1, 6, 7)), (send_ref, (2, 3, 4, 5))):
            for n, m in enumerate(slots):
                start = pl.multiple_of((me ^ m) * size, size)
                out[n] = gk_ref[pl.ds(start, size), :] * INV_ROOT
        gw_out[...] = jnp.concatenate([gwt_ref[i * 16 : (i + 1) * 16] for i in range(4)], axis=1)


def gq_kernel(*refs):
    lgs, iks, (iq_ref, w_ref) = refs[:4], refs[4:8], refs[8:10]
    gq_ref, wt, lg_ref, ikb_ref, q_ref, g_ref = refs[10:]
    source = pl.program_id(0)
    rows, keys = lgs[0].shape
    count = q_ref.shape[0] // rows
    y_lo, _, core = ctx_place()
    dests = [(y_lo * N_Z + i) * 2 + core for i in range(N_Z)]

    @pl.when(source == 0)
    def _():
        wt[...] = w_ref[...].T * INV_ROOT
        g_ref[...] = jnp.zeros_like(g_ref)
        for i in range(4):
            lg_ref[i] = lgs[i][...]
            ikb_ref[i] = iks[i][...].astype(BF16)
        for i in range(N_Z):
            block = iq_ref[:, pl.ds(pl.multiple_of(dests[i] * 256, 256), 256)]
            q_ref[2 * i * rows : 2 * (i + 1) * rows, :] = stacked(block)

    for c in range(4):
        cols = slice(c * 256, (c + 1) * 256)
        k = ikb_ref[source, cols, :]
        inner = dot(q_ref[...], k, NT)
        lg = jnp.concatenate([lg_ref[source, :, cols]] * count, axis=0)
        g_ref[...] += dot(jnp.where(inner > 0.0, lg, 0.0).astype(BF16), k, NN)

    @pl.when(source == 3)
    def _():
        for i in range(N_Z):
            pair = []
            for n in range(2):
                at = (2 * i + n) * rows
                weight = column(wt[pl.ds(dests[i] * 2 + n, 1), :])
                pair.append(g_ref[at : at + rows, :] * weight)
            gq_ref[i, :rows, :] = jnp.concatenate(pair, axis=1)


def gw_rows_kernel(gw0, gw1, gw2, gw3, gq_ref, out_ref):
    gw = (gw0[...] + gw1[...]) + (gw2[...] + gw3[...])
    for i in range(N_Z):
        out_ref[i] = gw


def finish_kernel(parts_ref, mine_ref, got_ref, gq_ref, gk_ref, gw_ref):
    total = parts_ref[0]
    for i in range(1, N_Z):
        total = total + parts_ref[i]
    gq_ref[...] = total[:64]
    gk_ref[...] = mine_ref[...] + got_ref[...]
    gwt = jnp.concatenate([total[64:, i * 64 : (i + 1) * 64] for i in range(4)], axis=0)
    gw_ref[...] = gwt.T


def smem():
    return pl.BlockSpec(memory_space=pltpu.SMEM)


def whole(shape):
    return pl.BlockSpec(shape, lambda *_: (0,) * len(shape))


def wholes(arrays):
    return [whole(x.shape) for x in arrays]


def floats(*shapes):
    return [jax.ShapeDtypeStruct(s, F32) for s in shapes]


def in_vmem():
    return pl.BlockSpec(memory_space=pltpu.VMEM)


def call(kernel, name, grid, ins, in_specs, out_shapes, out_specs, scratch, vmem=56):
    return pl.pallas_call(
        kernel,
        grid=grid,
        in_specs=in_specs,
        out_specs=out_specs,
        out_shape=out_shapes,
        scratch_shapes=scratch,
        compiler_params=pltpu.CompilerParams(vmem_limit_bytes=vmem * 1024 * 1024),
        name=name,
    )(*ins)


def main_specs(queries, keys):
    return [
        pl.BlockSpec((queries, 256), lambda i: (0, i)),
        pl.BlockSpec((queries, 128), lambda i: (0, i)),
        pl.BlockSpec((keys, 256), lambda i: (0, i)),
    ]


def run_front(key_blocks, qpos, krt, ik, w, iq, qn, qr, kn):
    queries, keys, pairs = qn.shape[0], kn.shape[0], qn.shape[1] // 256
    rows = iq.shape[0]
    shapes = [(2 * pairs, queries + 128), (rows, keys)]
    return call(
        front_kernel,
        "front",
        (pairs,),
        (key_blocks, qpos, krt, ik, w, iq, qn, qr, kn),
        [
            smem(),
            *wholes([qpos, krt, ik, w]),
            pl.BlockSpec((rows, GROUP * 128), lambda i: (0, i)),
            *main_specs(queries, keys),
        ],
        floats(*shapes),
        [whole(s) for s in shapes],
        [
            pltpu.VMEM((keys, queries), F32),
            pltpu.VMEM((2, keys, 128), BF16),
            pltpu.VMEM((2, keys, queries), F32),
            pltpu.VMEM((IDX_HEADS // 2, 128), F32),
            pltpu.VMEM((queries, 128), jnp.int32),
            pltpu.VMEM((keys, GROUP * rows), F32),
            pltpu.VMEM((keys, 128), F32),
        ],
    )


def run_probs(key_blocks, qpos, lse, logits, qn, qr, kn, krt):
    queries, keys, pairs = qn.shape[0], kn.shape[0], qn.shape[1] // 256
    return call(
        probs_kernel,
        "main_probs",
        (pairs,),
        (key_blocks, qpos, lse, logits, krt, qn, qr, kn),
        [smem(), *wholes([qpos, lse, logits, krt]), *main_specs(queries, keys)],
        floats((queries, keys)),
        [pl.BlockSpec(memory_space=pltpu.HBM)],
        [
            pltpu.VMEM((2, keys, 128), BF16),
            pltpu.VMEM((2, queries, keys), F32),
            pltpu.VMEM((queries, keys), F32),
            pltpu.SemaphoreType.DMA((N_HEAD,)),
        ],
        24,
    )[0]


def run_lg(target):
    return pl.pallas_call(
        lg_kernel,
        in_specs=[in_vmem()],
        out_specs=in_vmem(),
        out_shape=floats(target.shape[1:])[0],
        compiler_params=pltpu.CompilerParams(vmem_limit_bytes=8 * 1024 * 1024),
        name="logit_grad",
    )(target)


def run_gk(lg, iq, ik, w):
    rows, keys = lg.shape
    size = keys // N_HEAD
    shapes = [(4, size, IDX_DIM), (4, size, IDX_DIM), (16, 256)]
    return call(
        gk_kernel,
        "grad_k",
        (IDX_HEADS // GROUP,),
        (lg, iq, ik, w),
        [
            whole(lg.shape),
            pl.BlockSpec((rows, GROUP * 128), lambda i: (0, i)),
            *wholes([ik, w]),
        ],
        floats(*shapes),
        [whole(s) for s in shapes],
        [
            pltpu.VMEM((IDX_HEADS, rows, 128), F32),
            pltpu.VMEM((keys, 128), F32),
            pltpu.VMEM((keys, GROUP * rows), BF16),
            pltpu.VMEM((keys, IDX_DIM), F32),
            pltpu.VMEM((IDX_HEADS, rows), F32),
        ],
        20,
    )


def run_gq(lgs, iks, iq, w):
    rows, keys = lgs[0].shape
    shape = (N_Z, rows + 16, 256)
    ins = [*lgs, *iks, iq, w]
    return call(
        gq_kernel,
        "grad_q",
        (4,),
        ins,
        wholes(ins),
        floats(shape),
        [whole(shape)],
        [
            pltpu.VMEM(w.shape, F32),
            pltpu.VMEM((4, rows, keys), F32),
            pltpu.VMEM((4, keys, IDX_DIM), BF16),
            pltpu.VMEM((2 * N_Z * rows, IDX_DIM), BF16),
            pltpu.VMEM((2 * N_Z * rows, IDX_DIM), F32),
        ],
        28,
    )[0]


def run_gw_rows(parts, gws):
    rows = gws[0].shape[0]
    return pl.pallas_call(
        gw_rows_kernel,
        grid=(1,),
        in_specs=[*wholes(gws), pl.BlockSpec(memory_space=pl.ANY)],
        out_specs=pl.BlockSpec((N_Z, rows, 256), lambda i: (0, 64 // rows, 0)),
        out_shape=floats(parts.shape)[0],
        input_output_aliases={4: 0},
        compiler_params=pltpu.CompilerParams(vmem_limit_bytes=8 * 1024 * 1024),
        name="grad_w_rows",
    )(*gws, parts)


def run_finish(*ins):
    shapes = [(64, 256), (128, 128), (64, 64)]
    return pl.pallas_call(
        finish_kernel,
        in_specs=[in_vmem()] * 3,
        out_specs=[in_vmem()] * 3,
        out_shape=floats(*shapes),
        compiler_params=pltpu.CompilerParams(vmem_limit_bytes=8 * 1024 * 1024),
        name="finish",
    )(*ins)


def head_xor(value, bits):
    return lax.ppermute(value, "head", [(i, i ^ bits) for i in range(N_HEAD)])


def ctx_xor(value, bits):
    return lax.ppermute(value, "ctx", [(i, i ^ bits) for i in range(N_CTX)])


def z_shift(value, by):
    to = [i // 16 * 16 + (i // 2 + by) % N_Z * 2 + i % 2 for i in range(N_CTX)]
    return lax.ppermute(value, "ctx", list(enumerate(to)))


def merged(*values):
    top = values[0]
    for value in values[1:]:
        top = jnp.maximum(top, value)
    total = sum(jnp.exp2(value - top) for value in values)
    return top + jnp.log2(total)


def over_z(lse):
    below, above = z_shift(lse, 1), z_shift(lse, -1)
    two, three = merged(lse, below), merged(lse, below, above)
    return merged(three, z_shift(three, 3), z_shift(two, -3))


def per_device(qn, qr, kn, kr, iq, ik, w, query_pos, key_blocks):
    qpos = query_pos[None, :]
    krt = kr.T
    lse, logits = run_front(key_blocks, qpos, krt, ik, w, iq, qn, qr, kn)
    lse = merged(lse, ctx_xor(lse, 1))
    lse = merged(lse, ctx_xor(lse, 16))
    lse, ik_later = lax.optimization_barrier((lse, ik))
    ikf = ik_later.astype(F32)
    ikf_y, ikf_c = ctx_xor(ikf, 16), ctx_xor(ikf, 1)
    probs = run_probs(key_blocks, qpos, over_z(lse), logits, qn, qr, kn, krt)
    probs, ikf_y, ikf_c = lax.optimization_barrier((probs, ikf_y, ikf_c))
    target = lax.all_to_all(probs.reshape(N_HEAD, -1, probs.shape[1]), "head", 0, 0)
    ikf_yc = ctx_xor(ikf_y, 1)
    target, ikf_yc = lax.optimization_barrier((target, ikf_yc))

    lg = run_lg(target)
    lg_y, lg_c = ctx_xor(lg, 16), ctx_xor(lg, 1)
    keep, send, gw = run_gk(lg, iq, ik, w)
    lg_y, lg_c, send, gw = lax.optimization_barrier((lg_y, lg_c, send, gw))
    lg_yc = ctx_xor(lg_y, 1)
    gws = [gw, *[ctx_xor(gw, bits) for bits in (16, 17, 1)]]
    got = head_xor(send, 2)
    parts = run_gq([lg, lg_c, lg_y, lg_yc], [ik, ikf_c, ikf_y, ikf_yc], iq, w)
    parts = run_gw_rows(parts, gws)
    got, parts = lax.optimization_barrier((got, parts))
    got = head_xor(keep[2:] + got[2:], 6) + (keep[:2] + got[:2])
    got, mine = head_xor(got[1], 1), got[0]
    groups = [[(y * N_Z + z) * 2 + c for z in range(N_Z)] for y in range(2) for c in range(2)]
    parts = lax.all_to_all(parts, "ctx", 0, 0, axis_index_groups=groups)
    return run_finish(parts, mine, got)


def solution(mesh):
    return jax.shard_map(
        per_device,
        mesh=mesh,
        in_specs=(
            P(None, "head"),
            P(None, "head"),
            P("ctx", "head"),
            P("ctx", None),
            P("head", None),
            P("ctx", None),
            P("head", None),
            P(),
            P("ctx"),
        ),
        out_specs=(P("head", "ctx"), P(("ctx", "head"), None), P("head", None)),
        check_vma=False,
    )
```

```python
import math

import jax
import jax.numpy as jnp
from jax import lax
from jax.experimental import pallas as pl
from jax.experimental.pallas import tpu as pltpu
from jax.sharding import PartitionSpec as P

HEADS = 128
NOPE = 128
ROPE = 64
IDX_HEADS = 64
IDX_DIM = 128
N_CTX = 32
N_HEAD = 8
N_Z = 8
LOG2E = math.log2(math.e)
SCORE_SCALE = LOG2E / math.sqrt(NOPE + ROPE)
INV_ROOT = 1.0 / math.sqrt(IDX_DIM)
NEG = -1e30
F32 = jnp.float32
BF16 = jnp.bfloat16
NT = (((1,), (1,)), ((), ()))
NN = (((1,), (0,)), ((), ()))
GROUP = 8


def dot(a, b, dims):
    return lax.dot_general(a, b, dims, preferred_element_type=F32)


def column(row, lanes=128):
    return jnp.broadcast_to(row, (lanes, row.shape[1])).T


def ctx_place():
    ctx = lax.axis_index("ctx")
    return ctx // (2 * N_Z), ctx // 2 % N_Z, ctx % 2


def fill_rope(krt_ref, krp):
    kr = krt_ref[...].T
    zero = jnp.zeros_like(kr)
    krp[0] = jnp.concatenate([kr, zero], axis=1)
    krp[1] = jnp.concatenate([zero, kr], axis=1)


def fill_weights(w_ref, wb):
    for j in range(IDX_HEADS):
        wb[j] = jnp.broadcast_to(w_ref[:, j : j + 1], wb.shape[1:])


def lanes_of(block, width):
    return jnp.concatenate([block] * (width // 128), axis=-1)


def stacked(block):
    count = block.shape[1] // 128
    return jnp.concatenate([block[:, i * 128 : (i + 1) * 128] for i in range(count)], axis=0)


def pair_operands(refs, krp, p):
    qn_ref, qr_ref, kn_ref = refs
    part = slice(p * 128, (p + 1) * 128)
    q = jnp.concatenate([qn_ref[:, part], qr_ref[...]], axis=1)
    return q, jnp.concatenate([kn_ref[:, part], krp[p]], axis=1)


def online_lse(s_ref, bias, cols, chunk=64):
    keys = bias.shape[0]
    top = jnp.full((8, 256), 2.0 * NEG, F32)
    total = jnp.zeros((8, 256), F32)
    for kc in range(keys // chunk):
        rows = slice(kc * chunk, (kc + 1) * chunk)
        s = (s_ref[rows, cols] + bias[rows, cols]).reshape(chunk // 8, 8, 256)
        new = jnp.maximum(top, jnp.max(s, axis=0))
        e = jnp.exp2((s - new[None]) * SCORE_SCALE)
        total = total * jnp.exp2((top - new) * SCORE_SCALE) + jnp.sum(e, axis=0)
        top = new
    best = jnp.max(top, axis=0, keepdims=True)
    total = jnp.sum(total * jnp.exp2((top - best) * SCORE_SCALE), axis=0, keepdims=True)
    return best * SCORE_SCALE + jnp.log2(total)


def front_kernel(
    base_ref, qpos_ref, krt_ref, ik_ref, w_ref, iq_ref, qn_ref, qr_ref, kn_ref, out_ref, logits_ref,
    bias, krp, s_ref, wp, qcol, si_ref, acc,
):
    step = pl.program_id(0)
    keys, queries = bias.shape
    rows = logits_ref.shape[0]

    @pl.when(step == 0)
    def _():
        key = lax.broadcasted_iota(jnp.int32, bias.shape, 0) + base_ref[0] * keys
        bias[...] = jnp.where(key <= qpos_ref[...], 0.0, NEG)
        fill_rope(krt_ref, krp)
        wt = w_ref[...].T
        for i in range(IDX_HEADS // 2):
            pair = [wt[2 * i : 2 * i + 1], wt[2 * i + 1 : 2 * i + 2]]
            wp[i : i + 1, :] = jnp.concatenate(pair, axis=1)
        acc[...] = jnp.zeros_like(acc)
        qcol[...] = column(qpos_ref[...])

    def scores(p):
        q, k = pair_operands((qn_ref, qr_ref, kn_ref), krp, p)
        s_ref[p] = dot(k, q, NT)

    def statistics(p):
        for qc in range(queries // 256):
            cols = slice(qc * 256, (qc + 1) * 256)
            out_ref[pl.ds(2 * step + p, 1), cols] = online_lse(s_ref.at[p], bias, cols)

    scores(0)
    si_ref[...] = dot(ik_ref[...], stacked(iq_ref[...]), NT)
    statistics(0)
    scores(1)
    weights = [wp[pl.ds(step * GROUP // 2 + i, 1), :] for i in range(GROUP // 2)]
    for r in range(keys // 64):
        at = slice(r * 64, (r + 1) * 64)
        total = acc[at, :]
        for i, weight in enumerate(weights):
            total = total + jnp.maximum(si_ref[at, i * 128 : (i + 1) * 128], 0.0) * weight
        acc[at, :] = total
    statistics(1)

    @pl.when(step == pl.num_programs(0) - 1)
    def _():
        turned = acc[...].T
        key = lax.broadcasted_iota(jnp.int32, (rows, keys), 1) + base_ref[0] * keys
        start = pl.multiple_of(lax.axis_index("head") * rows, rows)
        limit = lanes_of(qcol[pl.ds(start, rows), :], keys)
        logits = (turned[:rows] + turned[rows:]) * (INV_ROOT * LOG2E)
        logits = jnp.where(key <= limit, logits, NEG)
        logits_ref[...] = logits
        top = jnp.max(logits, axis=1, keepdims=True)
        total = jnp.sum(jnp.exp2(logits - top), axis=1, keepdims=True)
        lse = jnp.broadcast_to(top + jnp.log2(total), (rows, 128)).T
        row = [lse[:16, :rows], jnp.zeros((16, 128 - rows), F32)]
        out_ref[:, queries:] = jnp.concatenate(row, axis=1)


def probs_kernel(
    base_ref, qpos_ref, lse_ref, logits_ref, krt_ref, qn_ref, qr_ref, kn_ref, out_hbm,
    krp, s_ref, acc, sems,
):
    step = pl.program_id(0)
    last = pl.num_programs(0) - 1
    queries, keys = acc.shape
    size = queries // N_HEAD

    @pl.when(step == 0)
    def _():
        fill_rope(krt_ref, krp)
        acc[...] = jnp.zeros_like(acc)

    lse = []
    for p in range(2):
        s_ref[p] = dot(*pair_operands((qn_ref, qr_ref, kn_ref), krp, p), NT)
        lse.append(column(lse_ref[pl.ds(2 * step + p, 1), :queries]))
    for r in range(queries // 32):
        rows = slice(r * 32, (r + 1) * 32)
        total = acc[rows, :]
        for p in range(2):
            s = s_ref[p, rows, :] * SCORE_SCALE - lanes_of(lse[p][rows], keys)
            total = total + jnp.exp2(s)
        acc[rows, :] = total

    @pl.when(step == last)
    def _():
        limit = column(qpos_ref[...]) - base_ref[0] * keys
        key = lax.broadcasted_iota(jnp.int32, (size, keys), 1)
        for h in range(N_HEAD):
            rows = slice(h * size, (h + 1) * size)
            acc[rows, :] = jnp.where(key <= lanes_of(limit[rows], keys), acc[rows, :], 0.0)
        top = lanes_of(column(lse_ref[:1, queries:])[:size], keys)
        mine = pl.ds(pl.multiple_of(lax.axis_index("head") * size, size), size)
        acc[mine, :] -= jnp.exp2(logits_ref[...] - top) * HEADS
        copies = []
        for h in range(N_HEAD):
            rows = pl.ds(h * size, size)
            copies.append(pltpu.make_async_copy(acc.at[rows], out_hbm.at[rows], sems.at[h]))
        for copy in copies:
            copy.start()
        for copy in copies:
            copy.wait()


def lg_kernel(target_ref, lg_ref):
    for c in range(lg_ref.shape[1] // 128):
        cols = slice(c * 128, (c + 1) * 128)
        target = target_ref[0, :, cols]
        for h in range(1, N_HEAD):
            target = target + target_ref[h, :, cols]
        lg_ref[:, cols] = target * (-1.0 / HEADS)


def gk_kernel(
    lg_ref, iq_ref, ik_ref, w_ref, keep_ref, send_ref, gw_out, wb, lgt_ref, m_ref, gk_ref, gwt_ref
):
    step = pl.program_id(0)
    rows, keys = lg_ref.shape
    width = GROUP * rows

    @pl.when(step == 0)
    def _():
        fill_weights(w_ref, wb)
        lgt_ref[...] = jnp.concatenate([lg_ref[...]] * (128 // rows), axis=0).T
        gk_ref[...] = jnp.zeros_like(gk_ref)

    q = stacked(iq_ref[...])
    w = jnp.concatenate([wb[step * GROUP + i] for i in range(GROUP)], axis=0)
    wq = (q.astype(F32) * w).astype(BF16)
    gw = jnp.zeros((8, width), F32)
    for c in range(2):
        inner = dot(ik_ref[c * 512 : (c + 1) * 512, :], q, NT)
        for r in range(16):
            at = slice(c * 512 + r * 32, c * 512 + (r + 1) * 32)
            part = inner[r * 32 : (r + 1) * 32]
            masked = jnp.where(part > 0.0, lanes_of(lgt_ref[at, :], width), 0.0)
            m_ref[at, :] = masked.astype(BF16)
            gw = gw + jnp.sum((part * masked).reshape(4, 8, width), axis=0)
        at = slice(c * 512, (c + 1) * 512)
        gk_ref[at, :] += dot(m_ref[at, :], wq, NN)
    gw = jnp.sum(gw, axis=0, keepdims=True) * INV_ROOT
    for i in range(GROUP):
        gwt_ref[pl.ds(step * GROUP + i, 1), :] = gw[:, i * rows : (i + 1) * rows]

    @pl.when(step == pl.num_programs(0) - 1)
    def _():
        me = lax.axis_index("head")
        size = keys // N_HEAD
        for out, slots in ((keep_ref, (0, 1, 6, 7)), (send_ref, (2, 3, 4, 5))):
            for n, m in enumerate(slots):
                start = pl.multiple_of((me ^ m) * size, size)
                out[n] = gk_ref[pl.ds(start, size), :] * INV_ROOT
        gw_out[...] = jnp.concatenate([gwt_ref[i * 16 : (i + 1) * 16] for i in range(4)], axis=1)


def gq_kernel(*refs):
    lgs, iks, (iq_ref, w_ref) = refs[:4], refs[4:8], refs[8:10]
    gq_ref, wt, lg_ref, ikb_ref, q_ref, g_ref = refs[10:]
    source = pl.program_id(0)
    rows, keys = lgs[0].shape
    count = q_ref.shape[0] // rows
    y_lo, _, core = ctx_place()
    dests = [(y_lo * N_Z + i) * 2 + core for i in range(N_Z)]

    @pl.when(source == 0)
    def _():
        wt[...] = w_ref[...].T * INV_ROOT
        g_ref[...] = jnp.zeros_like(g_ref)
        for i in range(4):
            lg_ref[i] = lgs[i][...]
            ikb_ref[i] = iks[i][...].astype(BF16)
        for i in range(N_Z):
            block = iq_ref[:, pl.ds(pl.multiple_of(dests[i] * 256, 256), 256)]
            q_ref[2 * i * rows : 2 * (i + 1) * rows, :] = stacked(block)

    for c in range(4):
        cols = slice(c * 256, (c + 1) * 256)
        k = ikb_ref[source, cols, :]
        inner = dot(q_ref[...], k, NT)
        lg = jnp.concatenate([lg_ref[source, :, cols]] * count, axis=0)
        g_ref[...] += dot(jnp.where(inner > 0.0, lg, 0.0).astype(BF16), k, NN)

    @pl.when(source == 3)
    def _():
        for i in range(N_Z):
            pair = []
            for n in range(2):
                at = (2 * i + n) * rows
                weight = column(wt[pl.ds(dests[i] * 2 + n, 1), :])
                pair.append(g_ref[at : at + rows, :] * weight)
            gq_ref[i, :rows, :] = jnp.concatenate(pair, axis=1)


def gw_rows_kernel(gw0, gw1, gw2, gw3, gq_ref, out_ref):
    gw = (gw0[...] + gw1[...]) + (gw2[...] + gw3[...])
    for i in range(N_Z):
        out_ref[i] = gw


def finish_kernel(parts_ref, mine_ref, got_ref, gq_ref, gk_ref, gw_ref):
    total = parts_ref[0]
    for i in range(1, N_Z):
        total = total + parts_ref[i]
    gq_ref[...] = total[:64]
    gk_ref[...] = mine_ref[...] + got_ref[...]
    gwt = jnp.concatenate([total[64:, i * 64 : (i + 1) * 64] for i in range(4)], axis=0)
    gw_ref[...] = gwt.T


def smem():
    return pl.BlockSpec(memory_space=pltpu.SMEM)


def whole(shape):
    return pl.BlockSpec(shape, lambda *_: (0,) * len(shape))


def wholes(arrays):
    return [whole(x.shape) for x in arrays]


def floats(*shapes):
    return [jax.ShapeDtypeStruct(s, F32) for s in shapes]


def in_vmem():
    return pl.BlockSpec(memory_space=pltpu.VMEM)


def call(kernel, name, grid, ins, in_specs, out_shapes, out_specs, scratch, vmem=56):
    return pl.pallas_call(
        kernel,
        grid=grid,
        in_specs=in_specs,
        out_specs=out_specs,
        out_shape=out_shapes,
        scratch_shapes=scratch,
        compiler_params=pltpu.CompilerParams(vmem_limit_bytes=vmem * 1024 * 1024),
        name=name,
    )(*ins)


def main_specs(queries, keys):
    return [
        pl.BlockSpec((queries, 256), lambda i: (0, i)),
        pl.BlockSpec((queries, 128), lambda i: (0, i)),
        pl.BlockSpec((keys, 256), lambda i: (0, i)),
    ]


def run_front(key_blocks, qpos, krt, ik, w, iq, qn, qr, kn):
    queries, keys, pairs = qn.shape[0], kn.shape[0], qn.shape[1] // 256
    rows = iq.shape[0]
    shapes = [(2 * pairs, queries + 128), (rows, keys)]
    return call(
        front_kernel,
        "front",
        (pairs,),
        (key_blocks, qpos, krt, ik, w, iq, qn, qr, kn),
        [
            smem(),
            *wholes([qpos, krt, ik, w]),
            pl.BlockSpec((rows, GROUP * 128), lambda i: (0, i)),
            *main_specs(queries, keys),
        ],
        floats(*shapes),
        [whole(s) for s in shapes],
        [
            pltpu.VMEM((keys, queries), F32),
            pltpu.VMEM((2, keys, 128), BF16),
            pltpu.VMEM((2, keys, queries), F32),
            pltpu.VMEM((IDX_HEADS // 2, 128), F32),
            pltpu.VMEM((queries, 128), jnp.int32),
            pltpu.VMEM((keys, GROUP * rows), F32),
            pltpu.VMEM((keys, 128), F32),
        ],
    )


def run_probs(key_blocks, qpos, lse, logits, qn, qr, kn, krt):
    queries, keys, pairs = qn.shape[0], kn.shape[0], qn.shape[1] // 256
    return call(
        probs_kernel,
        "main_probs",
        (pairs,),
        (key_blocks, qpos, lse, logits, krt, qn, qr, kn),
        [smem(), *wholes([qpos, lse, logits, krt]), *main_specs(queries, keys)],
        floats((queries, keys)),
        [pl.BlockSpec(memory_space=pltpu.HBM)],
        [
            pltpu.VMEM((2, keys, 128), BF16),
            pltpu.VMEM((2, queries, keys), F32),
            pltpu.VMEM((queries, keys), F32),
            pltpu.SemaphoreType.DMA((N_HEAD,)),
        ],
        24,
    )[0]


def run_lg(target):
    return pl.pallas_call(
        lg_kernel,
        in_specs=[in_vmem()],
        out_specs=in_vmem(),
        out_shape=floats(target.shape[1:])[0],
        compiler_params=pltpu.CompilerParams(vmem_limit_bytes=8 * 1024 * 1024),
        name="logit_grad",
    )(target)


def run_gk(lg, iq, ik, w):
    rows, keys = lg.shape
    size = keys // N_HEAD
    shapes = [(4, size, IDX_DIM), (4, size, IDX_DIM), (16, 256)]
    return call(
        gk_kernel,
        "grad_k",
        (IDX_HEADS // GROUP,),
        (lg, iq, ik, w),
        [
            whole(lg.shape),
            pl.BlockSpec((rows, GROUP * 128), lambda i: (0, i)),
            *wholes([ik, w]),
        ],
        floats(*shapes),
        [whole(s) for s in shapes],
        [
            pltpu.VMEM((IDX_HEADS, rows, 128), F32),
            pltpu.VMEM((keys, 128), F32),
            pltpu.VMEM((keys, GROUP * rows), BF16),
            pltpu.VMEM((keys, IDX_DIM), F32),
            pltpu.VMEM((IDX_HEADS, rows), F32),
        ],
        20,
    )


def run_gq(lgs, iks, iq, w):
    rows, keys = lgs[0].shape
    shape = (N_Z, rows + 16, 256)
    ins = [*lgs, *iks, iq, w]
    return call(
        gq_kernel,
        "grad_q",
        (4,),
        ins,
        wholes(ins),
        floats(shape),
        [whole(shape)],
        [
            pltpu.VMEM(w.shape, F32),
            pltpu.VMEM((4, rows, keys), F32),
            pltpu.VMEM((4, keys, IDX_DIM), BF16),
            pltpu.VMEM((2 * N_Z * rows, IDX_DIM), BF16),
            pltpu.VMEM((2 * N_Z * rows, IDX_DIM), F32),
        ],
        28,
    )[0]


def run_gw_rows(parts, gws):
    rows = gws[0].shape[0]
    return pl.pallas_call(
        gw_rows_kernel,
        grid=(1,),
        in_specs=[*wholes(gws), pl.BlockSpec(memory_space=pl.ANY)],
        out_specs=pl.BlockSpec((N_Z, rows, 256), lambda i: (0, 64 // rows, 0)),
        out_shape=floats(parts.shape)[0],
        input_output_aliases={4: 0},
        compiler_params=pltpu.CompilerParams(vmem_limit_bytes=8 * 1024 * 1024),
        name="grad_w_rows",
    )(*gws, parts)


def run_finish(*ins):
    shapes = [(64, 256), (128, 128), (64, 64)]
    return pl.pallas_call(
        finish_kernel,
        in_specs=[in_vmem()] * 3,
        out_specs=[in_vmem()] * 3,
        out_shape=floats(*shapes),
        compiler_params=pltpu.CompilerParams(vmem_limit_bytes=8 * 1024 * 1024),
        name="finish",
    )(*ins)


def head_xor(value, bits):
    return lax.ppermute(value, "head", [(i, i ^ bits) for i in range(N_HEAD)])


def ctx_xor(value, bits):
    return lax.ppermute(value, "ctx", [(i, i ^ bits) for i in range(N_CTX)])


def z_shift(value, by):
    to = [i // 16 * 16 + (i // 2 + by) % N_Z * 2 + i % 2 for i in range(N_CTX)]
    return lax.ppermute(value, "ctx", list(enumerate(to)))


def merged(*values):
    top = values[0]
    for value in values[1:]:
        top = jnp.maximum(top, value)
    total = sum(jnp.exp2(value - top) for value in values)
    return top + jnp.log2(total)


def over_z(lse):
    below, above = z_shift(lse, 1), z_shift(lse, -1)
    two, three = merged(lse, below), merged(lse, below, above)
    return merged(three, z_shift(three, 3), z_shift(two, -3))


def per_device(qn, qr, kn, kr, iq, ik, w, query_pos, key_blocks):
    qpos = query_pos[None, :]
    krt = kr.T
    lse, logits = run_front(key_blocks, qpos, krt, ik, w, iq, qn, qr, kn)
    lse = merged(lse, ctx_xor(lse, 1))
    lse = merged(lse, ctx_xor(lse, 16))
    lse, ik_later, logits = lax.optimization_barrier((lse, ik, logits))
    ikf = ik_later.astype(F32)
    ikf_y = ctx_xor(ikf, 16)
    logits = jnp.maximum(logits, NEG)
    probs = run_probs(key_blocks, qpos, over_z(lse), logits, qn, qr, kn, krt)
    probs, ikf, ikf_y = lax.optimization_barrier((probs, ikf, ikf_y))
    target = lax.all_to_all(probs.reshape(N_HEAD, -1, probs.shape[1]), "head", 0, 0)
    ikf_c, ikf_yc = ctx_xor(ikf, 1), ctx_xor(ikf_y, 1)
    target, ikf_c, ikf_yc = lax.optimization_barrier((target, ikf_c, ikf_yc))

    lg = run_lg(target)
    lg_y, lg_c = ctx_xor(lg, 16), ctx_xor(lg, 1)
    keep, send, gw = run_gk(lg, iq, ik, w)
    lg_y, lg_c, send, gw = lax.optimization_barrier((lg_y, lg_c, send, gw))
    lg_yc = ctx_xor(lg_y, 1)
    gws = [gw, *[ctx_xor(gw, bits) for bits in (16, 17, 1)]]
    got = head_xor(send, 2)
    parts = run_gq([lg, lg_c, lg_y, lg_yc], [ik, ikf_c, ikf_y, ikf_yc], iq, w)
    parts = run_gw_rows(parts, gws)
    got, parts = lax.optimization_barrier((got, parts))
    got = head_xor(keep[2:] + got[2:], 6) + (keep[:2] + got[:2])
    got, mine = head_xor(got[1], 1), got[0]
    groups = [[(y * N_Z + z) * 2 + c for z in range(N_Z)] for y in range(2) for c in range(2)]
    parts = lax.all_to_all(parts, "ctx", 0, 0, axis_index_groups=groups)
    return run_finish(parts, mine, got)


def solution(mesh):
    return jax.shard_map(
        per_device,
        mesh=mesh,
        in_specs=(
            P(None, "head"),
            P(None, "head"),
            P("ctx", "head"),
            P("ctx", None),
            P("head", None),
            P("ctx", None),
            P("head", None),
            P(),
            P("ctx"),
        ),
        out_specs=(P("head", "ctx"), P(("ctx", "head"), None), P("head", None)),
        check_vma=False,
    )
```

```python
import math

import jax
import jax.numpy as jnp
from jax import lax
from jax.experimental import pallas as pl
from jax.experimental.pallas import tpu as pltpu
from jax.sharding import PartitionSpec as P

HEADS = 128
NOPE = 128
ROPE = 64
IDX_HEADS = 64
IDX_DIM = 128
N_CTX = 32
N_HEAD = 8
N_Z = 8
LOG2E = math.log2(math.e)
SCORE_SCALE = LOG2E / math.sqrt(NOPE + ROPE)
INV_ROOT = 1.0 / math.sqrt(IDX_DIM)
NEG = -1e30
F32 = jnp.float32
BF16 = jnp.bfloat16
NT = (((1,), (1,)), ((), ()))
NN = (((1,), (0,)), ((), ()))
GROUP = 8


def dot(a, b, dims):
    return lax.dot_general(a, b, dims, preferred_element_type=F32)


def column(row, lanes=128):
    return jnp.broadcast_to(row, (lanes, row.shape[1])).T


def ctx_place():
    ctx = lax.axis_index("ctx")
    return ctx // (2 * N_Z), ctx // 2 % N_Z, ctx % 2


def fill_rope(krt_ref, krp):
    kr = krt_ref[...].T
    zero = jnp.zeros_like(kr)
    krp[0] = jnp.concatenate([kr, zero], axis=1)
    krp[1] = jnp.concatenate([zero, kr], axis=1)


def fill_weights(w_ref, wb):
    for j in range(IDX_HEADS):
        wb[j] = jnp.broadcast_to(w_ref[:, j : j + 1], wb.shape[1:])


def lanes_of(block, width):
    return jnp.concatenate([block] * (width // 128), axis=-1)


def stacked(block):
    count = block.shape[1] // 128
    return jnp.concatenate([block[:, i * 128 : (i + 1) * 128] for i in range(count)], axis=0)


def pair_operands(refs, krp, p):
    qn_ref, qr_ref, kn_ref = refs
    part = slice(p * 128, (p + 1) * 128)
    q = jnp.concatenate([qn_ref[:, part], qr_ref[...]], axis=1)
    return q, jnp.concatenate([kn_ref[:, part], krp[p]], axis=1)


def online_lse(s_ref, bias, cols, chunk=64):
    keys = bias.shape[0]
    top = jnp.full((8, 256), 2.0 * NEG, F32)
    total = jnp.zeros((8, 256), F32)
    for kc in range(keys // chunk):
        rows = slice(kc * chunk, (kc + 1) * chunk)
        s = (s_ref[rows, cols] + bias[rows, cols]).reshape(chunk // 8, 8, 256)
        new = jnp.maximum(top, jnp.max(s, axis=0))
        e = jnp.exp2((s - new[None]) * SCORE_SCALE)
        total = total * jnp.exp2((top - new) * SCORE_SCALE) + jnp.sum(e, axis=0)
        top = new
    best = jnp.max(top, axis=0, keepdims=True)
    total = jnp.sum(total * jnp.exp2((top - best) * SCORE_SCALE), axis=0, keepdims=True)
    return best * SCORE_SCALE + jnp.log2(total)


def front_kernel(
    base_ref, qpos_ref, krt_ref, ik_ref, w_ref, iq_ref, qn_ref, qr_ref, kn_ref, out_ref, logits_ref,
    bias, krp, s_ref, wp, qcol, si_ref, acc,
):
    step = pl.program_id(0)
    keys, queries = bias.shape
    rows = logits_ref.shape[0]

    @pl.when(step == 0)
    def _():
        key = lax.broadcasted_iota(jnp.int32, bias.shape, 0) + base_ref[0] * keys
        bias[...] = jnp.where(key <= qpos_ref[...], 0.0, NEG)
        fill_rope(krt_ref, krp)
        wt = w_ref[...].T
        for i in range(IDX_HEADS // 2):
            pair = [wt[2 * i : 2 * i + 1], wt[2 * i + 1 : 2 * i + 2]]
            wp[i : i + 1, :] = jnp.concatenate(pair, axis=1)
        acc[...] = jnp.zeros_like(acc)
        si_ref[...] = jnp.zeros_like(si_ref)
        qcol[...] = column(qpos_ref[...])

    def scores(p):
        q, k = pair_operands((qn_ref, qr_ref, kn_ref), krp, p)
        s_ref[p] = dot(k, q, NT)

    def statistics(p):
        for qc in range(queries // 256):
            cols = slice(qc * 256, (qc + 1) * 256)
            out_ref[pl.ds(2 * step + p, 1), cols] = online_lse(s_ref.at[p], bias, cols)

    def add_logits(group):
        weights = [wp[pl.ds(group * GROUP // 2 + i, 1), :] for i in range(GROUP // 2)]
        for r in range(keys // 64):
            at = slice(r * 64, (r + 1) * 64)
            total = acc[at, :]
            for i, weight in enumerate(weights):
                active = jnp.maximum(si_ref[at, i * 128 : (i + 1) * 128], 0.0)
                total = total + active * weight
            acc[at, :] = total

    scores(0)
    add_logits(jnp.maximum(step - 1, 0))
    scores(1)
    statistics(0)
    si_ref[...] = dot(ik_ref[...], stacked(iq_ref[...]), NT)
    statistics(1)

    @pl.when(step == pl.num_programs(0) - 1)
    def _():
        add_logits(step)
        turned = acc[...].T
        key = lax.broadcasted_iota(jnp.int32, (rows, keys), 1) + base_ref[0] * keys
        start = pl.multiple_of(lax.axis_index("head") * rows, rows)
        limit = lanes_of(qcol[pl.ds(start, rows), :], keys)
        logits = (turned[:rows] + turned[rows:]) * (INV_ROOT * LOG2E)
        logits = jnp.where(key <= limit, logits, NEG)
        logits_ref[...] = logits
        top = jnp.max(logits, axis=1, keepdims=True)
        total = jnp.sum(jnp.exp2(logits - top), axis=1, keepdims=True)
        lse = jnp.broadcast_to(top + jnp.log2(total), (rows, 128)).T
        row = [lse[:16, :rows], jnp.zeros((16, 128 - rows), F32)]
        out_ref[:, queries:] = jnp.concatenate(row, axis=1)


def probs_kernel(
    base_ref, qpos_ref, lse_ref, logits_ref, krt_ref, qn_ref, qr_ref, kn_ref, out_hbm,
    krp, s_ref, acc, sems,
):
    step = pl.program_id(0)
    last = pl.num_programs(0) - 1
    queries, keys = acc.shape
    size = queries // N_HEAD

    @pl.when(step == 0)
    def _():
        fill_rope(krt_ref, krp)
        acc[...] = jnp.zeros_like(acc)

    lse = []
    for p in range(2):
        s_ref[p] = dot(*pair_operands((qn_ref, qr_ref, kn_ref), krp, p), NT)
        lse.append(column(lse_ref[pl.ds(2 * step + p, 1), :queries]))
    for r in range(queries // 32):
        rows = slice(r * 32, (r + 1) * 32)
        total = acc[rows, :]
        for p in range(2):
            s = s_ref[p, rows, :] * SCORE_SCALE - lanes_of(lse[p][rows], keys)
            total = total + jnp.exp2(s)
        acc[rows, :] = total

    @pl.when(step == last)
    def _():
        limit = column(qpos_ref[...]) - base_ref[0] * keys
        key = lax.broadcasted_iota(jnp.int32, (size, keys), 1)
        for h in range(N_HEAD):
            rows = slice(h * size, (h + 1) * size)
            acc[rows, :] = jnp.where(key <= lanes_of(limit[rows], keys), acc[rows, :], 0.0)
        top = lanes_of(column(lse_ref[:1, queries:])[:size], keys)
        mine = pl.ds(pl.multiple_of(lax.axis_index("head") * size, size), size)
        acc[mine, :] -= jnp.exp2(logits_ref[...] - top) * HEADS
        copies = []
        for h in range(N_HEAD):
            rows = pl.ds(h * size, size)
            copies.append(pltpu.make_async_copy(acc.at[rows], out_hbm.at[rows], sems.at[h]))
        for copy in copies:
            copy.start()
        for copy in copies:
            copy.wait()


def lg_kernel(target_ref, lg_ref):
    for c in range(lg_ref.shape[1] // 128):
        cols = slice(c * 128, (c + 1) * 128)
        target = target_ref[0, :, cols]
        for h in range(1, N_HEAD):
            target = target + target_ref[h, :, cols]
        lg_ref[:, cols] = target * (-1.0 / HEADS)


def gk_kernel(
    lg_ref, iq_ref, ik_ref, w_ref, keep_ref, send_ref, gw_out, wb, lgt_ref, m_ref, gk_ref, gwt_ref
):
    step = pl.program_id(0)
    rows, keys = lg_ref.shape
    width = GROUP * rows

    @pl.when(step == 0)
    def _():
        fill_weights(w_ref, wb)
        lgt_ref[...] = jnp.concatenate([lg_ref[...]] * (128 // rows), axis=0).T
        gk_ref[...] = jnp.zeros_like(gk_ref)

    q = stacked(iq_ref[...])
    w = jnp.concatenate([wb[step * GROUP + i] for i in range(GROUP)], axis=0)
    wq = (q.astype(F32) * w).astype(BF16)
    gw = jnp.zeros((8, width), F32)
    for c in range(2):
        inner = dot(ik_ref[c * 512 : (c + 1) * 512, :], q, NT)
        for r in range(16):
            at = slice(c * 512 + r * 32, c * 512 + (r + 1) * 32)
            part = inner[r * 32 : (r + 1) * 32]
            masked = jnp.where(part > 0.0, lanes_of(lgt_ref[at, :], width), 0.0)
            m_ref[at, :] = masked.astype(BF16)
            gw = gw + jnp.sum((part * masked).reshape(4, 8, width), axis=0)
        at = slice(c * 512, (c + 1) * 512)
        gk_ref[at, :] += dot(m_ref[at, :], wq, NN)
    gw = jnp.sum(gw, axis=0, keepdims=True) * INV_ROOT
    for i in range(GROUP):
        gwt_ref[pl.ds(step * GROUP + i, 1), :] = gw[:, i * rows : (i + 1) * rows]

    @pl.when(step == pl.num_programs(0) - 1)
    def _():
        me = lax.axis_index("head")
        size = keys // N_HEAD
        for out, slots in ((keep_ref, (0, 1, 6, 7)), (send_ref, (2, 3, 4, 5))):
            for n, m in enumerate(slots):
                start = pl.multiple_of((me ^ m) * size, size)
                out[n] = gk_ref[pl.ds(start, size), :] * INV_ROOT
        gw_out[...] = jnp.concatenate([gwt_ref[i * 16 : (i + 1) * 16] for i in range(4)], axis=1)


def gq_kernel(*refs):
    lgs, iks, (iq_ref, w_ref) = refs[:4], refs[4:8], refs[8:10]
    gq_ref, wt, lg_ref, ikb_ref, q_ref, g_ref = refs[10:]
    source = pl.program_id(0)
    rows, keys = lgs[0].shape
    count = q_ref.shape[0] // rows
    y_lo, _, core = ctx_place()
    dests = [(y_lo * N_Z + i) * 2 + core for i in range(N_Z)]

    @pl.when(source == 0)
    def _():
        wt[...] = w_ref[...].T * INV_ROOT
        g_ref[...] = jnp.zeros_like(g_ref)
        for i in range(4):
            lg_ref[i] = lgs[i][...]
            ikb_ref[i] = iks[i][...].astype(BF16)
        for i in range(N_Z):
            block = iq_ref[:, pl.ds(pl.multiple_of(dests[i] * 256, 256), 256)]
            q_ref[2 * i * rows : 2 * (i + 1) * rows, :] = stacked(block)

    for c in range(4):
        cols = slice(c * 256, (c + 1) * 256)
        k = ikb_ref[source, cols, :]
        inner = dot(q_ref[...], k, NT)
        lg = jnp.concatenate([lg_ref[source, :, cols]] * count, axis=0)
        g_ref[...] += dot(jnp.where(inner > 0.0, lg, 0.0).astype(BF16), k, NN)

    @pl.when(source == 3)
    def _():
        for i in range(N_Z):
            pair = []
            for n in range(2):
                at = (2 * i + n) * rows
                weight = column(wt[pl.ds(dests[i] * 2 + n, 1), :])
                pair.append(g_ref[at : at + rows, :] * weight)
            gq_ref[i, :rows, :] = jnp.concatenate(pair, axis=1)


def gw_rows_kernel(gw0, gw1, gw2, gw3, gq_ref, out_ref):
    gw = (gw0[...] + gw1[...]) + (gw2[...] + gw3[...])
    for i in range(N_Z):
        out_ref[i] = gw


def finish_kernel(parts_ref, mine_ref, got_ref, gq_ref, gk_ref, gw_ref):
    total = parts_ref[0]
    for i in range(1, N_Z):
        total = total + parts_ref[i]
    gq_ref[...] = total[:64]
    gk_ref[...] = mine_ref[...] + got_ref[...]
    gwt = jnp.concatenate([total[64:, i * 64 : (i + 1) * 64] for i in range(4)], axis=0)
    gw_ref[...] = gwt.T


def smem():
    return pl.BlockSpec(memory_space=pltpu.SMEM)


def whole(shape):
    return pl.BlockSpec(shape, lambda *_: (0,) * len(shape))


def wholes(arrays):
    return [whole(x.shape) for x in arrays]


def floats(*shapes):
    return [jax.ShapeDtypeStruct(s, F32) for s in shapes]


def in_vmem():
    return pl.BlockSpec(memory_space=pltpu.VMEM)


def call(kernel, name, grid, ins, in_specs, out_shapes, out_specs, scratch, vmem=56):
    return pl.pallas_call(
        kernel,
        grid=grid,
        in_specs=in_specs,
        out_specs=out_specs,
        out_shape=out_shapes,
        scratch_shapes=scratch,
        compiler_params=pltpu.CompilerParams(vmem_limit_bytes=vmem * 1024 * 1024),
        name=name,
    )(*ins)


def main_specs(queries, keys):
    return [
        pl.BlockSpec((queries, 256), lambda i: (0, i)),
        pl.BlockSpec((queries, 128), lambda i: (0, i)),
        pl.BlockSpec((keys, 256), lambda i: (0, i)),
    ]


def run_front(key_blocks, qpos, krt, ik, w, iq, qn, qr, kn):
    queries, keys, pairs = qn.shape[0], kn.shape[0], qn.shape[1] // 256
    rows = iq.shape[0]
    shapes = [(2 * pairs, queries + 128), (rows, keys)]
    return call(
        front_kernel,
        "front",
        (pairs,),
        (key_blocks, qpos, krt, ik, w, iq, qn, qr, kn),
        [
            smem(),
            *wholes([qpos, krt, ik, w]),
            pl.BlockSpec((rows, GROUP * 128), lambda i: (0, i)),
            *main_specs(queries, keys),
        ],
        floats(*shapes),
        [whole(s) for s in shapes],
        [
            pltpu.VMEM((keys, queries), F32),
            pltpu.VMEM((2, keys, 128), BF16),
            pltpu.VMEM((2, keys, queries), F32),
            pltpu.VMEM((IDX_HEADS // 2, 128), F32),
            pltpu.VMEM((queries, 128), jnp.int32),
            pltpu.VMEM((keys, GROUP * rows), F32),
            pltpu.VMEM((keys, 128), F32),
        ],
    )


def run_probs(key_blocks, qpos, lse, logits, qn, qr, kn, krt):
    queries, keys, pairs = qn.shape[0], kn.shape[0], qn.shape[1] // 256
    return call(
        probs_kernel,
        "main_probs",
        (pairs,),
        (key_blocks, qpos, lse, logits, krt, qn, qr, kn),
        [smem(), *wholes([qpos, lse, logits, krt]), *main_specs(queries, keys)],
        floats((queries, keys)),
        [pl.BlockSpec(memory_space=pltpu.HBM)],
        [
            pltpu.VMEM((2, keys, 128), BF16),
            pltpu.VMEM((2, queries, keys), F32),
            pltpu.VMEM((queries, keys), F32),
            pltpu.SemaphoreType.DMA((N_HEAD,)),
        ],
        24,
    )[0]


def run_lg(target):
    return pl.pallas_call(
        lg_kernel,
        in_specs=[in_vmem()],
        out_specs=in_vmem(),
        out_shape=floats(target.shape[1:])[0],
        compiler_params=pltpu.CompilerParams(vmem_limit_bytes=8 * 1024 * 1024),
        name="logit_grad",
    )(target)


def run_gk(lg, iq, ik, w):
    rows, keys = lg.shape
    size = keys // N_HEAD
    shapes = [(4, size, IDX_DIM), (4, size, IDX_DIM), (16, 256)]
    return call(
        gk_kernel,
        "grad_k",
        (IDX_HEADS // GROUP,),
        (lg, iq, ik, w),
        [
            whole(lg.shape),
            pl.BlockSpec((rows, GROUP * 128), lambda i: (0, i)),
            *wholes([ik, w]),
        ],
        floats(*shapes),
        [whole(s) for s in shapes],
        [
            pltpu.VMEM((IDX_HEADS, rows, 128), F32),
            pltpu.VMEM((keys, 128), F32),
            pltpu.VMEM((keys, GROUP * rows), BF16),
            pltpu.VMEM((keys, IDX_DIM), F32),
            pltpu.VMEM((IDX_HEADS, rows), F32),
        ],
        20,
    )


def run_gq(lgs, iks, iq, w):
    rows, keys = lgs[0].shape
    shape = (N_Z, rows + 16, 256)
    ins = [*lgs, *iks, iq, w]
    return call(
        gq_kernel,
        "grad_q",
        (4,),
        ins,
        wholes(ins),
        floats(shape),
        [whole(shape)],
        [
            pltpu.VMEM(w.shape, F32),
            pltpu.VMEM((4, rows, keys), F32),
            pltpu.VMEM((4, keys, IDX_DIM), BF16),
            pltpu.VMEM((2 * N_Z * rows, IDX_DIM), BF16),
            pltpu.VMEM((2 * N_Z * rows, IDX_DIM), F32),
        ],
        28,
    )[0]


def run_gw_rows(parts, gws):
    rows = gws[0].shape[0]
    return pl.pallas_call(
        gw_rows_kernel,
        grid=(1,),
        in_specs=[*wholes(gws), pl.BlockSpec(memory_space=pl.ANY)],
        out_specs=pl.BlockSpec((N_Z, rows, 256), lambda i: (0, 64 // rows, 0)),
        out_shape=floats(parts.shape)[0],
        input_output_aliases={4: 0},
        compiler_params=pltpu.CompilerParams(vmem_limit_bytes=8 * 1024 * 1024),
        name="grad_w_rows",
    )(*gws, parts)


def run_finish(*ins):
    shapes = [(64, 256), (128, 128), (64, 64)]
    return pl.pallas_call(
        finish_kernel,
        in_specs=[in_vmem()] * 3,
        out_specs=[in_vmem()] * 3,
        out_shape=floats(*shapes),
        compiler_params=pltpu.CompilerParams(vmem_limit_bytes=8 * 1024 * 1024),
        name="finish",
    )(*ins)


def head_xor(value, bits):
    return lax.ppermute(value, "head", [(i, i ^ bits) for i in range(N_HEAD)])


def ctx_xor(value, bits):
    return lax.ppermute(value, "ctx", [(i, i ^ bits) for i in range(N_CTX)])


def z_shift(value, by):
    to = [i // 16 * 16 + (i // 2 + by) % N_Z * 2 + i % 2 for i in range(N_CTX)]
    return lax.ppermute(value, "ctx", list(enumerate(to)))


def merged(*values):
    top = values[0]
    for value in values[1:]:
        top = jnp.maximum(top, value)
    total = sum(jnp.exp2(value - top) for value in values)
    return top + jnp.log2(total)


def over_z(lse):
    below, above = z_shift(lse, 1), z_shift(lse, -1)
    two, three = merged(lse, below), merged(lse, below, above)
    return merged(three, z_shift(three, 3), z_shift(two, -3))


def per_device(qn, qr, kn, kr, iq, ik, w, query_pos, key_blocks):
    qpos = query_pos[None, :]
    krt = kr.T
    lse, logits = run_front(key_blocks, qpos, krt, ik, w, iq, qn, qr, kn)
    lse = merged(lse, ctx_xor(lse, 1))
    lse = merged(lse, ctx_xor(lse, 16))
    lse, ik_later, logits = lax.optimization_barrier((lse, ik, logits))
    ikf = ik_later.astype(F32)
    ikf_y = ctx_xor(ikf, 16)
    logits = jnp.maximum(logits, NEG)
    probs = run_probs(key_blocks, qpos, over_z(lse), logits, qn, qr, kn, krt)
    probs, ikf, ikf_y = lax.optimization_barrier((probs, ikf, ikf_y))
    target = lax.all_to_all(probs.reshape(N_HEAD, -1, probs.shape[1]), "head", 0, 0)
    ikf_c, ikf_yc = ctx_xor(ikf, 1), ctx_xor(ikf_y, 1)
    target, ikf_c, ikf_yc = lax.optimization_barrier((target, ikf_c, ikf_yc))

    lg = run_lg(target)
    lg_y, lg_c = ctx_xor(lg, 16), ctx_xor(lg, 1)
    keep, send, gw = run_gk(lg, iq, ik, w)
    lg_y, lg_c, send, gw = lax.optimization_barrier((lg_y, lg_c, send, gw))
    lg_yc = ctx_xor(lg_y, 1)
    gws = [gw, *[ctx_xor(gw, bits) for bits in (16, 17, 1)]]
    got = head_xor(send, 2)
    parts = run_gq([lg, lg_c, lg_y, lg_yc], [ik, ikf_c, ikf_y, ikf_yc], iq, w)
    parts = run_gw_rows(parts, gws)
    got, parts = lax.optimization_barrier((got, parts))
    got = head_xor(keep[2:] + got[2:], 6) + (keep[:2] + got[:2])
    got, mine = head_xor(got[1], 1), got[0]
    groups = [[(y * N_Z + z) * 2 + c for z in range(N_Z)] for y in range(2) for c in range(2)]
    parts = lax.all_to_all(parts, "ctx", 0, 0, axis_index_groups=groups)
    return run_finish(parts, mine, got)


def solution(mesh):
    return jax.shard_map(
        per_device,
        mesh=mesh,
        in_specs=(
            P(None, "head"),
            P(None, "head"),
            P("ctx", "head"),
            P("ctx", None),
            P("head", None),
            P("ctx", None),
            P("head", None),
            P(),
            P("ctx"),
        ),
        out_specs=(P("head", "ctx"), P(("ctx", "head"), None), P("head", None)),
        check_vma=False,
    )
```

```python
import math

import jax
import jax.numpy as jnp
from jax import lax
from jax.experimental import pallas as pl
from jax.experimental.pallas import tpu as pltpu
from jax.sharding import PartitionSpec as P

HEADS = 128
NOPE = 128
ROPE = 64
IDX_HEADS = 64
IDX_DIM = 128
N_CTX = 32
N_HEAD = 8
N_Z = 8
LOG2E = math.log2(math.e)
SCORE_SCALE = LOG2E / math.sqrt(NOPE + ROPE)
INV_ROOT = 1.0 / math.sqrt(IDX_DIM)
NEG = -1e30
F32 = jnp.float32
BF16 = jnp.bfloat16
NT = (((1,), (1,)), ((), ()))
NN = (((1,), (0,)), ((), ()))
GROUP = 8


def dot(a, b, dims):
    return lax.dot_general(a, b, dims, preferred_element_type=F32)


def column(row, lanes=128):
    return jnp.broadcast_to(row, (lanes, row.shape[1])).T


def ctx_place():
    ctx = lax.axis_index("ctx")
    return ctx // (2 * N_Z), ctx // 2 % N_Z, ctx % 2


def fill_rope(krt_ref, krp):
    kr = krt_ref[...].T
    zero = jnp.zeros_like(kr)
    krp[0] = jnp.concatenate([kr, zero], axis=1)
    krp[1] = jnp.concatenate([zero, kr], axis=1)


def fill_weights(w_ref, wb):
    for j in range(IDX_HEADS):
        wb[j] = jnp.broadcast_to(w_ref[:, j : j + 1], wb.shape[1:])


def lanes_of(block, width):
    return jnp.concatenate([block] * (width // 128), axis=-1)


def stacked(block):
    count = block.shape[1] // 128
    return jnp.concatenate([block[:, i * 128 : (i + 1) * 128] for i in range(count)], axis=0)


def pair_operands(refs, krp, p):
    qn_ref, qr_ref, kn_ref = refs
    part = slice(p * 128, (p + 1) * 128)
    q = jnp.concatenate([qn_ref[:, part], qr_ref[...]], axis=1)
    return q, jnp.concatenate([kn_ref[:, part], krp[p]], axis=1)


def online_lse(s_ref, bias, cols, chunk=128):
    keys = bias.shape[0]
    top = jnp.full((8, 256), 2.0 * NEG, F32)
    total = jnp.zeros((8, 256), F32)
    for kc in range(keys // chunk):
        rows = slice(kc * chunk, (kc + 1) * chunk)
        s = (s_ref[rows, cols] + bias[rows, cols]).reshape(chunk // 8, 8, 256)
        new = jnp.maximum(top, jnp.max(s, axis=0))
        e = jnp.exp2((s - new[None]) * SCORE_SCALE)
        total = total * jnp.exp2((top - new) * SCORE_SCALE) + jnp.sum(e, axis=0)
        top = new
    best = jnp.max(top, axis=0, keepdims=True)
    total = jnp.sum(total * jnp.exp2((top - best) * SCORE_SCALE), axis=0, keepdims=True)
    return best * SCORE_SCALE + jnp.log2(total)


def front_kernel(
    base_ref, qpos_ref, krt_ref, ik_ref, w_ref, iq_ref, qn_ref, qr_ref, kn_ref, out_ref, logits_ref,
    bias, krp, s_ref, wp, qcol, si_ref, acc,
):
    step = pl.program_id(0)
    keys, queries = bias.shape
    rows = logits_ref.shape[0]

    @pl.when(step == 0)
    def _():
        key = lax.broadcasted_iota(jnp.int32, bias.shape, 0) + base_ref[0] * keys
        bias[...] = jnp.where(key <= qpos_ref[...], 0.0, NEG)
        fill_rope(krt_ref, krp)
        wt = w_ref[...].T
        for i in range(IDX_HEADS // 2):
            pair = [wt[2 * i : 2 * i + 1], wt[2 * i + 1 : 2 * i + 2]]
            wp[i : i + 1, :] = jnp.concatenate(pair, axis=1)
        acc[...] = jnp.zeros_like(acc)
        qcol[...] = column(qpos_ref[...])

    def scores(p):
        q, k = pair_operands((qn_ref, qr_ref, kn_ref), krp, p)
        s_ref[p] = dot(k, q, NT)

    def statistics(p):
        for qc in range(queries // 256):
            cols = slice(qc * 256, (qc + 1) * 256)
            out_ref[pl.ds(2 * step + p, 1), cols] = online_lse(s_ref.at[p], bias, cols)

    scores(0)
    scores(1)
    statistics(0)
    si_ref[...] = dot(ik_ref[...], stacked(iq_ref[...]), NT)
    statistics(1)
    weights = [wp[pl.ds(step * GROUP // 2 + i, 1), :] for i in range(GROUP // 2)]
    for r in range(keys // 64):
        at = slice(r * 64, (r + 1) * 64)
        total = acc[at, :]
        for i, weight in enumerate(weights):
            total = total + jnp.maximum(si_ref[at, i * 128 : (i + 1) * 128], 0.0) * weight
        acc[at, :] = total

    @pl.when(step == pl.num_programs(0) - 1)
    def _():
        turned = acc[...].T
        key = lax.broadcasted_iota(jnp.int32, (rows, keys), 1) + base_ref[0] * keys
        start = pl.multiple_of(lax.axis_index("head") * rows, rows)
        limit = lanes_of(qcol[pl.ds(start, rows), :], keys)
        logits = (turned[:rows] + turned[rows:]) * (INV_ROOT * LOG2E)
        logits = jnp.where(key <= limit, logits, NEG)
        logits_ref[...] = logits
        top = jnp.max(logits, axis=1, keepdims=True)
        total = jnp.sum(jnp.exp2(logits - top), axis=1, keepdims=True)
        lse = jnp.broadcast_to(top + jnp.log2(total), (rows, 128)).T
        row = [lse[:16, :rows], jnp.zeros((16, 128 - rows), F32)]
        out_ref[:, queries:] = jnp.concatenate(row, axis=1)


def probs_kernel(
    base_ref, qpos_ref, lse_ref, logits_ref, krt_ref, qn_ref, qr_ref, kn_ref, out_hbm,
    krp, s_ref, acc, sems,
):
    step = pl.program_id(0)
    last = pl.num_programs(0) - 1
    queries, keys = acc.shape
    size = queries // N_HEAD

    @pl.when(step == 0)
    def _():
        fill_rope(krt_ref, krp)
        acc[...] = jnp.zeros_like(acc)

    lse = []
    for p in range(2):
        s_ref[p] = dot(*pair_operands((qn_ref, qr_ref, kn_ref), krp, p), NT)
        lse.append(column(lse_ref[pl.ds(2 * step + p, 1), :queries]))
    for r in range(queries // 32):
        rows = slice(r * 32, (r + 1) * 32)
        total = acc[rows, :]
        for p in range(2):
            s = s_ref[p, rows, :] * SCORE_SCALE - lanes_of(lse[p][rows], keys)
            total = total + jnp.exp2(s)
        acc[rows, :] = total

    @pl.when(step == last)
    def _():
        limit = column(qpos_ref[...]) - base_ref[0] * keys
        key = lax.broadcasted_iota(jnp.int32, (size, keys), 1)
        for h in range(N_HEAD):
            rows = slice(h * size, (h + 1) * size)
            acc[rows, :] = jnp.where(key <= lanes_of(limit[rows], keys), acc[rows, :], 0.0)
        top = lanes_of(column(lse_ref[:1, queries:])[:size], keys)
        mine = pl.ds(pl.multiple_of(lax.axis_index("head") * size, size), size)
        acc[mine, :] -= jnp.exp2(logits_ref[...] - top) * HEADS
        copies = []
        for h in range(N_HEAD):
            rows = pl.ds(h * size, size)
            copies.append(pltpu.make_async_copy(acc.at[rows], out_hbm.at[rows], sems.at[h]))
        for copy in copies:
            copy.start()
        for copy in copies:
            copy.wait()


def lg_kernel(target_ref, lg_ref):
    for c in range(lg_ref.shape[1] // 128):
        cols = slice(c * 128, (c + 1) * 128)
        target = target_ref[0, :, cols]
        for h in range(1, N_HEAD):
            target = target + target_ref[h, :, cols]
        lg_ref[:, cols] = target * (-1.0 / HEADS)


def gk_kernel(
    lg_ref, iq_ref, ik_ref, w_ref, keep_ref, send_ref, gw_out, wb, lgt_ref, m_ref, gk_ref, gwt_ref
):
    step = pl.program_id(0)
    rows, keys = lg_ref.shape
    width = GROUP * rows

    @pl.when(step == 0)
    def _():
        fill_weights(w_ref, wb)
        lgt_ref[...] = jnp.concatenate([lg_ref[...]] * (128 // rows), axis=0).T
        gk_ref[...] = jnp.zeros_like(gk_ref)

    q = stacked(iq_ref[...])
    w = jnp.concatenate([wb[step * GROUP + i] for i in range(GROUP)], axis=0)
    wq = (q.astype(F32) * w).astype(BF16)
    gw = jnp.zeros((8, width), F32)
    for c in range(2):
        inner = dot(ik_ref[c * 512 : (c + 1) * 512, :], q, NT)
        for r in range(16):
            at = slice(c * 512 + r * 32, c * 512 + (r + 1) * 32)
            part = inner[r * 32 : (r + 1) * 32]
            masked = jnp.where(part > 0.0, lanes_of(lgt_ref[at, :], width), 0.0)
            m_ref[at, :] = masked.astype(BF16)
            gw = gw + jnp.sum((part * masked).reshape(4, 8, width), axis=0)
        at = slice(c * 512, (c + 1) * 512)
        gk_ref[at, :] += dot(m_ref[at, :], wq, NN)
    gw = jnp.sum(gw, axis=0, keepdims=True) * INV_ROOT
    for i in range(GROUP):
        gwt_ref[pl.ds(step * GROUP + i, 1), :] = gw[:, i * rows : (i + 1) * rows]

    @pl.when(step == pl.num_programs(0) - 1)
    def _():
        me = lax.axis_index("head")
        size = keys // N_HEAD
        for out, slots in ((keep_ref, (0, 1, 6, 7)), (send_ref, (2, 3, 4, 5))):
            for n, m in enumerate(slots):
                start = pl.multiple_of((me ^ m) * size, size)
                out[n] = gk_ref[pl.ds(start, size), :] * INV_ROOT
        gw_out[...] = jnp.concatenate([gwt_ref[i * 16 : (i + 1) * 16] for i in range(4)], axis=1)


def gq_kernel(*refs):
    lgs, iks, (iq_ref, w_ref) = refs[:4], refs[4:8], refs[8:10]
    gq_ref, wt, lg_ref, ikb_ref, q_ref, g_ref = refs[10:]
    source = pl.program_id(0)
    rows, keys = lgs[0].shape
    count = q_ref.shape[0] // rows
    y_lo, _, core = ctx_place()
    dests = [(y_lo * N_Z + i) * 2 + core for i in range(N_Z)]

    @pl.when(source == 0)
    def _():
        wt[...] = w_ref[...].T * INV_ROOT
        g_ref[...] = jnp.zeros_like(g_ref)
        for i in range(4):
            lg_ref[i] = lgs[i][...]
            ikb_ref[i] = iks[i][...].astype(BF16)
        for i in range(N_Z):
            block = iq_ref[:, pl.ds(pl.multiple_of(dests[i] * 256, 256), 256)]
            q_ref[2 * i * rows : 2 * (i + 1) * rows, :] = stacked(block)

    for c in range(4):
        cols = slice(c * 256, (c + 1) * 256)
        k = ikb_ref[source, cols, :]
        inner = dot(q_ref[...], k, NT)
        lg = jnp.concatenate([lg_ref[source, :, cols]] * count, axis=0)
        g_ref[...] += dot(jnp.where(inner > 0.0, lg, 0.0).astype(BF16), k, NN)

    @pl.when(source == 3)
    def _():
        for i in range(N_Z):
            pair = []
            for n in range(2):
                at = (2 * i + n) * rows
                weight = column(wt[pl.ds(dests[i] * 2 + n, 1), :])
                pair.append(g_ref[at : at + rows, :] * weight)
            gq_ref[i, :rows, :] = jnp.concatenate(pair, axis=1)


def gw_rows_kernel(gw0, gw1, gw2, gw3, gq_ref, out_ref):
    gw = (gw0[...] + gw1[...]) + (gw2[...] + gw3[...])
    for i in range(N_Z):
        out_ref[i] = gw


def finish_kernel(parts_ref, mine_ref, got_ref, gq_ref, gk_ref, gw_ref):
    total = parts_ref[0]
    for i in range(1, N_Z):
        total = total + parts_ref[i]
    gq_ref[...] = total[:64]
    gk_ref[...] = mine_ref[...] + got_ref[...]
    gwt = jnp.concatenate([total[64:, i * 64 : (i + 1) * 64] for i in range(4)], axis=0)
    gw_ref[...] = gwt.T


def smem():
    return pl.BlockSpec(memory_space=pltpu.SMEM)


def whole(shape):
    return pl.BlockSpec(shape, lambda *_: (0,) * len(shape))


def wholes(arrays):
    return [whole(x.shape) for x in arrays]


def floats(*shapes):
    return [jax.ShapeDtypeStruct(s, F32) for s in shapes]


def in_vmem():
    return pl.BlockSpec(memory_space=pltpu.VMEM)


def call(kernel, name, grid, ins, in_specs, out_shapes, out_specs, scratch, vmem=56):
    return pl.pallas_call(
        kernel,
        grid=grid,
        in_specs=in_specs,
        out_specs=out_specs,
        out_shape=out_shapes,
        scratch_shapes=scratch,
        compiler_params=pltpu.CompilerParams(vmem_limit_bytes=vmem * 1024 * 1024),
        name=name,
    )(*ins)


def main_specs(queries, keys):
    return [
        pl.BlockSpec((queries, 256), lambda i: (0, i)),
        pl.BlockSpec((queries, 128), lambda i: (0, i)),
        pl.BlockSpec((keys, 256), lambda i: (0, i)),
    ]


def run_front(key_blocks, qpos, krt, ik, w, iq, qn, qr, kn):
    queries, keys, pairs = qn.shape[0], kn.shape[0], qn.shape[1] // 256
    rows = iq.shape[0]
    shapes = [(2 * pairs, queries + 128), (rows, keys)]
    return call(
        front_kernel,
        "front",
        (pairs,),
        (key_blocks, qpos, krt, ik, w, iq, qn, qr, kn),
        [
            smem(),
            *wholes([qpos, krt, ik, w]),
            pl.BlockSpec((rows, GROUP * 128), lambda i: (0, i)),
            *main_specs(queries, keys),
        ],
        floats(*shapes),
        [whole(s) for s in shapes],
        [
            pltpu.VMEM((keys, queries), F32),
            pltpu.VMEM((2, keys, 128), BF16),
            pltpu.VMEM((2, keys, queries), F32),
            pltpu.VMEM((IDX_HEADS // 2, 128), F32),
            pltpu.VMEM((queries, 128), jnp.int32),
            pltpu.VMEM((keys, GROUP * rows), F32),
            pltpu.VMEM((keys, 128), F32),
        ],
    )


def run_probs(key_blocks, qpos, lse, logits, qn, qr, kn, krt):
    queries, keys, pairs = qn.shape[0], kn.shape[0], qn.shape[1] // 256
    return call(
        probs_kernel,
        "main_probs",
        (pairs,),
        (key_blocks, qpos, lse, logits, krt, qn, qr, kn),
        [smem(), *wholes([qpos, lse, logits, krt]), *main_specs(queries, keys)],
        floats((queries, keys)),
        [pl.BlockSpec(memory_space=pltpu.HBM)],
        [
            pltpu.VMEM((2, keys, 128), BF16),
            pltpu.VMEM((2, queries, keys), F32),
            pltpu.VMEM((queries, keys), F32),
            pltpu.SemaphoreType.DMA((N_HEAD,)),
        ],
        24,
    )[0]


def run_lg(target):
    return pl.pallas_call(
        lg_kernel,
        in_specs=[in_vmem()],
        out_specs=in_vmem(),
        out_shape=floats(target.shape[1:])[0],
        compiler_params=pltpu.CompilerParams(vmem_limit_bytes=8 * 1024 * 1024),
        name="logit_grad",
    )(target)


def run_gk(lg, iq, ik, w):
    rows, keys = lg.shape
    size = keys // N_HEAD
    shapes = [(4, size, IDX_DIM), (4, size, IDX_DIM), (16, 256)]
    return call(
        gk_kernel,
        "grad_k",
        (IDX_HEADS // GROUP,),
        (lg, iq, ik, w),
        [
            whole(lg.shape),
            pl.BlockSpec((rows, GROUP * 128), lambda i: (0, i)),
            *wholes([ik, w]),
        ],
        floats(*shapes),
        [whole(s) for s in shapes],
        [
            pltpu.VMEM((IDX_HEADS, rows, 128), F32),
            pltpu.VMEM((keys, 128), F32),
            pltpu.VMEM((keys, GROUP * rows), BF16),
            pltpu.VMEM((keys, IDX_DIM), F32),
            pltpu.VMEM((IDX_HEADS, rows), F32),
        ],
        20,
    )


def run_gq(lgs, iks, iq, w):
    rows, keys = lgs[0].shape
    shape = (N_Z, rows + 16, 256)
    ins = [*lgs, *iks, iq, w]
    return call(
        gq_kernel,
        "grad_q",
        (4,),
        ins,
        wholes(ins),
        floats(shape),
        [whole(shape)],
        [
            pltpu.VMEM(w.shape, F32),
            pltpu.VMEM((4, rows, keys), F32),
            pltpu.VMEM((4, keys, IDX_DIM), BF16),
            pltpu.VMEM((2 * N_Z * rows, IDX_DIM), BF16),
            pltpu.VMEM((2 * N_Z * rows, IDX_DIM), F32),
        ],
        28,
    )[0]


def run_gw_rows(parts, gws):
    rows = gws[0].shape[0]
    return pl.pallas_call(
        gw_rows_kernel,
        grid=(1,),
        in_specs=[*wholes(gws), pl.BlockSpec(memory_space=pl.ANY)],
        out_specs=pl.BlockSpec((N_Z, rows, 256), lambda i: (0, 64 // rows, 0)),
        out_shape=floats(parts.shape)[0],
        input_output_aliases={4: 0},
        compiler_params=pltpu.CompilerParams(vmem_limit_bytes=8 * 1024 * 1024),
        name="grad_w_rows",
    )(*gws, parts)


def run_finish(*ins):
    shapes = [(64, 256), (128, 128), (64, 64)]
    return pl.pallas_call(
        finish_kernel,
        in_specs=[in_vmem()] * 3,
        out_specs=[in_vmem()] * 3,
        out_shape=floats(*shapes),
        compiler_params=pltpu.CompilerParams(vmem_limit_bytes=8 * 1024 * 1024),
        name="finish",
    )(*ins)


def head_xor(value, bits):
    return lax.ppermute(value, "head", [(i, i ^ bits) for i in range(N_HEAD)])


def ctx_xor(value, bits):
    return lax.ppermute(value, "ctx", [(i, i ^ bits) for i in range(N_CTX)])


def z_shift(value, by):
    to = [i // 16 * 16 + (i // 2 + by) % N_Z * 2 + i % 2 for i in range(N_CTX)]
    return lax.ppermute(value, "ctx", list(enumerate(to)))


def merged(*values):
    top = values[0]
    for value in values[1:]:
        top = jnp.maximum(top, value)
    total = sum(jnp.exp2(value - top) for value in values)
    return top + jnp.log2(total)


def over_z(lse):
    below, above = z_shift(lse, 1), z_shift(lse, -1)
    two, three = merged(lse, below), merged(lse, below, above)
    return merged(three, z_shift(three, 3), z_shift(two, -3))


def per_device(qn, qr, kn, kr, iq, ik, w, query_pos, key_blocks):
    qpos = query_pos[None, :]
    krt = kr.T
    lse, logits = run_front(key_blocks, qpos, krt, ik, w, iq, qn, qr, kn)
    lse = merged(lse, ctx_xor(lse, 1))
    lse = merged(lse, ctx_xor(lse, 16))
    lse, ik_later, logits = lax.optimization_barrier((lse, ik, logits))
    ikf = ik_later.astype(F32)
    ikf_y = ctx_xor(ikf, 16)
    logits = jnp.maximum(logits, NEG)
    probs = run_probs(key_blocks, qpos, over_z(lse), logits, qn, qr, kn, krt)
    probs, ikf, ikf_y = lax.optimization_barrier((probs, ikf, ikf_y))
    target = lax.all_to_all(probs.reshape(N_HEAD, -1, probs.shape[1]), "head", 0, 0)
    ikf_c, ikf_yc = ctx_xor(ikf, 1), ctx_xor(ikf_y, 1)
    target, ikf_c, ikf_yc = lax.optimization_barrier((target, ikf_c, ikf_yc))

    lg = run_lg(target)
    lg_y, lg_c = ctx_xor(lg, 16), ctx_xor(lg, 1)
    keep, send, gw = run_gk(lg, iq, ik, w)
    lg_y, lg_c, send, gw = lax.optimization_barrier((lg_y, lg_c, send, gw))
    lg_yc = ctx_xor(lg_y, 1)
    gws = [gw, *[ctx_xor(gw, bits) for bits in (16, 17, 1)]]
    got = head_xor(send, 2)
    parts = run_gq([lg, lg_c, lg_y, lg_yc], [ik, ikf_c, ikf_y, ikf_yc], iq, w)
    parts = run_gw_rows(parts, gws)
    got, parts = lax.optimization_barrier((got, parts))
    got = head_xor(keep[2:] + got[2:], 6) + (keep[:2] + got[:2])
    got, mine = head_xor(got[1], 1), got[0]
    groups = [[(y * N_Z + z) * 2 + c for z in range(N_Z)] for y in range(2) for c in range(2)]
    parts = lax.all_to_all(parts, "ctx", 0, 0, axis_index_groups=groups)
    return run_finish(parts, mine, got)


def solution(mesh):
    return jax.shard_map(
        per_device,
        mesh=mesh,
        in_specs=(
            P(None, "head"),
            P(None, "head"),
            P("ctx", "head"),
            P("ctx", None),
            P("head", None),
            P("ctx", None),
            P("head", None),
            P(),
            P("ctx"),
        ),
        out_specs=(P("head", "ctx"), P(("ctx", "head"), None), P("head", None)),
        check_vma=False,
    )
```
